128 devices in a mesh: gx: 8 (over z, x_hi), gy: 16 (over x_lo, y, core).
Axes of the slice: x: 4 (x_hi: 2, x_lo: 2; x = x_hi * 2 + x_lo), y: 4, z: 4, core: 2. Of those that a mesh axis runs over, the one named last changes fastest.
Arguments:
- efield: float32 [3, 256, 512, 128], P(None, 'gx', 'gy'), may hold values from -6 to 6
- hfield: float32 [3, 256, 512, 128], P(None, 'gx', 'gy'), may hold values from -6 to 6
- e_coef: float32 [256, 512, 128], P('gx', 'gy'), may hold values from 0.2 to 0.6
- omega: float32 [4], replicated, may hold values from 0.1 to 0.8
- patch_owner: int32 [128], replicated, may hold values from 0 to 127, as said below
- patch_corner: int32 [128, 2], replicated, may hold values from 1 to 23
- surface_points: int32 [8, 16, 256], P('gx', 'gy'), may hold values from -1 to 131071, as said below
- surface_faces: int32 [8, 16, 256], P('gx', 'gy'), may hold values from 0 to 5, as said below
- angle_index: int32 [4096, 2], replicated, may hold values from 0 to 127
Outputs:
- efield_out: float32 [3, 256, 512, 128], P(None, 'gx', 'gy')
- hfield_out: float32 [3, 256, 512, 128], P(None, 'gx', 'gy')
- far_field: float32 [4096, 48], P(('gx', 'gy'))
The draws below stay inside these ranges and needn't reach their ends.
Inputs may be any that keep to these rules, and one draw needn't show every extreme that they name: `patch_owner`: every device index appears at most 4 times, and some device exactly 4 times. `surface_points`: the points lie on the faces of the box of cells 32 // 2 to 239, 16 to 495 and 16 to 111, each on the face named by surface_faces. A block's live slots come first and the rest hold -1; the number live in a block is proportional to the box-face area inside it, and the fullest block has all 256 live. `surface_faces`: empty slots hold 0. `angle_index`: the azimuthal index is below 128.
All inputs are finite; a program needn't handle non-finite values.
Results may differ from the reference program's by a relative error of at most 0.0003.
Values sent between devices are 32-bit elements; how exact they have to be, the bound alone decides.
A program may use at most 320 MiB of HBM per device.

```python
import math
import jax
import jax.numpy as jnp
from jax import lax

CB = 32
CZ = 128
PB = 8
STEPS = 2
FREQ = 4
NTH = 128
NPH = 256
SPB = 256
ANG = 4096
NPATCH = 128
NPTS = 32768
NX = 256
NY = 512
N_GX = 8
N_GY = 16
DEVICES = 128


def draw_patch_owner(key, part):
    key = jax.random.fold_in(key, 11)
    key_perm, key_kind = jax.random.split(key)
    order = jax.random.permutation(key_perm, DEVICES).astype(jnp.int32)
    kinds = jax.random.randint(key_kind, (DEVICES // 4,), 0, 2).astype(jnp.int32)
    kinds = kinds.at[0].set(1)
    numbers = jnp.arange(DEVICES, dtype=jnp.int32)
    group = numbers // 4
    lane = numbers % 4
    pick = 4 * group + jnp.where(kinds[group] == 1, 0, lane)
    return order[pick].astype(jnp.int32)


def intersection_of(start, low, high):
    return jnp.clip(jnp.minimum(start + CB - 1, high) - jnp.maximum(start, low) + 1, 0, CB).astype(jnp.int32)


def surface_layout(key):
    key = jax.random.fold_in(key, 29)
    margin = CB // 2
    z_low = CZ // 8
    z_span = CZ - 2 * z_low
    x_high = CB * N_GX - 1 - margin
    y_high = CB * N_GY - 1 - margin
    x_first = (jnp.arange(N_GX, dtype=jnp.int32) * CB)[:, None] + jnp.zeros((1, N_GY), jnp.int32)
    y_first = (jnp.arange(N_GY, dtype=jnp.int32) * CB)[None, :] + jnp.zeros((N_GX, 1), jnp.int32)
    span_x = intersection_of(x_first, margin, x_high)
    span_y = intersection_of(y_first, margin, y_high)
    x_begin = jnp.maximum(x_first, margin) - x_first
    y_begin = jnp.maximum(y_first, margin) - y_first
    has_xlow = ((x_first <= margin) & (margin < x_first + CB)).astype(jnp.int32)
    has_xhigh = ((x_first <= x_high) & (x_high < x_first + CB)).astype(jnp.int32)
    has_ylow = ((y_first <= margin) & (margin < y_first + CB)).astype(jnp.int32)
    has_yhigh = ((y_first <= y_high) & (y_high < y_first + CB)).astype(jnp.int32)
    areas = jnp.stack([has_xlow * span_y * z_span, has_xhigh * span_y * z_span, has_ylow * span_x * z_span, has_yhigh * span_x * z_span, span_x * span_y, span_x * span_y]).astype(jnp.int32)
    total = jnp.sum(areas, axis=0)
    count = SPB * total // jnp.max(total)
    draws = jax.random.randint(key, (N_GX, N_GY, SPB), 0, 1 << 30).astype(jnp.int32)
    pick = draws % jnp.maximum(total, 1)[:, :, None]
    ends = jnp.cumsum(areas, axis=0)
    face = jnp.sum((pick[None] >= ends[:, :, :, None]).astype(jnp.int32), axis=0)
    face = jnp.minimum(face, 5)
    chooser = (face[None] == jnp.arange(6, dtype=jnp.int32)[:, None, None, None]).astype(jnp.int32)
    starts = ends - areas
    offset = pick - jnp.sum(chooser * starts[:, :, :, None], axis=0)
    width_y = jnp.maximum(span_y, 1)[:, :, None]
    xb = x_begin[:, :, None]
    yb = y_begin[:, :, None]
    x_fixed = jnp.where(face == 0, margin - x_first[:, :, None], x_high - x_first[:, :, None])
    y_fixed = jnp.where(face == 2, margin - y_first[:, :, None], y_high - y_first[:, :, None])
    z_fixed = jnp.where(face == 4, z_low, CZ - 1 - z_low)
    on_x = face < 2
    on_y = (face >= 2) & (face < 4)
    local_x = jnp.where(on_x, x_fixed, jnp.where(on_y, xb + offset // z_span, xb + offset // width_y))
    local_y = jnp.where(on_x, yb + offset // z_span, jnp.where(on_y, y_fixed, yb + offset % width_y))
    local_z = jnp.where(face < 4, z_low + offset % z_span, z_fixed)
    index = (local_x * CB + local_y) * CZ + local_z
    live = jnp.arange(SPB, dtype=jnp.int32)[None, None, :] < count[:, :, None]
    points = jnp.where(live, index, -1).astype(jnp.int32)
    faces = jnp.where(live, face, 0).astype(jnp.int32)
    return (points, faces)


def draw_surface_points(key, part):
    return surface_layout(key)[0]


def draw_surface_faces(key, part):
    return surface_layout(key)[1]


def touch_ends(result, key, low, high):
    dims = result.shape
    index_at = [jax.random.randint(jax.random.fold_in(key, axis), (), 0, dims[axis]) for axis in range(len(dims))]
    result = result.at[tuple(index_at)].set(low)
    longest = dims.index(max(dims))
    index_at[longest] = (index_at[longest] + 1) % dims[longest]
    return result.at[tuple(index_at)].set(high)


def levels(stream_key, dims, cuts, least, high):
    factor_of, own = 1.0, jax.random.fold_in(stream_key, 6)
    for axis_at, shards_of in cuts:
        steps = jnp.exp(jax.random.uniform(jax.random.fold_in(own, axis_at), (shards_of,), jnp.float32, least / len(cuts), high / len(cuts)))
        factor_of = factor_of * jnp.repeat(steps, dims[axis_at] // shards_of).reshape([-1 if axis == axis_at else 1 for axis in range(len(dims))])
    return factor_of


def centred(own_key, shape, scale, bound, cuts=(), kind=jnp.bfloat16):
    result = scale * jax.random.normal(own_key, shape, jnp.float32)
    if cuts:
        result = result * levels(own_key, shape, cuts, -0.22, 0.18)
    return jnp.clip(result, -bound, bound).astype(kind)


def setup_inputs(seed: int = 0) -> dict:
    key_list = jax.random.split(jax.random.key(seed), 10)
    return {
        "efield": centred(key_list[0], (3, NX, NY, CZ), 1.0, 6.0, ((1, 8), (2, 16)), jnp.float32),
        "hfield": centred(key_list[1], (3, NX, NY, CZ), 1.0, 6.0, ((1, 8), (2, 16)), jnp.float32),
        "e_coef": jnp.clip(jnp.exp(math.log(0.6) - 1.0986123 * jax.random.uniform(key_list[2], (NX, NY, CZ), jnp.float32) ** levels(key_list[2], (NX, NY, CZ), ((0, 8), (1, 16)), -0.2, 0.2)), 0.2, 0.6),
        "omega": jnp.clip(jnp.exp(jax.random.uniform(key_list[3], (FREQ,), jnp.float32, math.log(0.1), math.log(0.8))), 0.1, 0.8),
        "patch_owner": draw_patch_owner(jax.random.fold_in(key_list[9], 71), 0),
        "patch_corner": touch_ends(jax.random.randint(key_list[5], (NPATCH, 2), 1, CB - PB), jax.random.fold_in(key_list[5], 1), 1, (CB - PB) - 1).astype(jnp.int32),
        "surface_points": draw_surface_points(jax.random.fold_in(key_list[9], 71), 0),
        "surface_faces": draw_surface_faces(jax.random.fold_in(key_list[9], 71), 0),
        "angle_index": touch_ends(jax.random.randint(key_list[8], (ANG, 2), 0, NTH), jax.random.fold_in(key_list[8], 1), 0, NTH - 1).astype(jnp.int32),
    }


H_COEF = 0.5

def forward(field, axis, edge):
    after = jnp.concatenate([lax.slice_in_dim(field, 1, field.shape[axis], axis=axis), edge], axis=axis)
    return after - field

def backward(field, axis, edge):
    before = jnp.concatenate([edge, lax.slice_in_dim(field, 0, field.shape[axis] - 1, axis=axis)], axis=axis)
    return field - before

def zero_edges(field):
    first = field[0]
    x_edge = jnp.zeros((2, 1) + first.shape[1:], first.dtype)
    y_edge = jnp.zeros((2, first.shape[0], 1, first.shape[2]), first.dtype)
    return (x_edge, y_edge)

def curl_forward(efield, x_edge, y_edge):
    if x_edge is None:
        x_edge, y_edge = zero_edges(efield)
    comp_x, comp_y, comp_z = (efield[0], efield[1], efield[2])
    z_edge = jnp.zeros(comp_x.shape[:2] + (1,), comp_x.dtype)
    curl_x = forward(comp_z, 1, y_edge[1]) - forward(comp_y, 2, z_edge)
    curl_y = forward(comp_x, 2, z_edge) - forward(comp_z, 0, x_edge[1])
    curl_z = forward(comp_y, 0, x_edge[0]) - forward(comp_x, 1, y_edge[0])
    return jnp.stack([curl_x, curl_y, curl_z])

def curl_backward(hfield, x_edge, y_edge):
    if x_edge is None:
        x_edge, y_edge = zero_edges(hfield)
    comp_x, comp_y, comp_z = (hfield[0], hfield[1], hfield[2])
    z_edge = jnp.zeros(comp_x.shape[:2] + (1,), comp_x.dtype)
    curl_x = backward(comp_z, 1, y_edge[1]) - backward(comp_y, 2, z_edge)
    curl_y = backward(comp_x, 2, z_edge) - backward(comp_z, 0, x_edge[1])
    curl_z = backward(comp_y, 0, x_edge[0]) - backward(comp_x, 1, y_edge[0])
    return jnp.stack([curl_x, curl_y, curl_z])

def refine(efield, hfield, e_coef, x_start, y_start):
    span = PB + 2
    depth = efield.shape[3]
    anchor = jnp.zeros((), jnp.int32)
    x_start = x_start.astype(jnp.int32)
    y_start = y_start.astype(jnp.int32)
    hp = lax.Precision.HIGHEST
    fine_lanes = jnp.arange(2 * depth, dtype=jnp.int32) // 2
    spread = (jnp.arange(depth, dtype=jnp.int32)[:, None] == fine_lanes[None, :]).astype(jnp.float32)
    halving = spread.T * 0.5

    def cutout(field):
        return lax.dynamic_slice(field, (anchor, x_start, y_start, anchor), (3, span, span, depth))

    def finer(field):
        wider = jnp.repeat(jnp.repeat(field, 2, axis=-3), 2, axis=-2)
        return jnp.dot(wider, spread, precision=hp)
    e_start = finer(cutout(efield))
    h_start = finer(cutout(hfield))
    coef_fine = finer(lax.dynamic_slice(e_coef, (x_start, y_start, anchor), (span, span, depth)))
    lanes = jnp.arange(2 * span)
    inner_line = (lanes >= 2) & (lanes < 2 * span - 2)
    inner = (inner_line[:, None] & inner_line[None, :])[None, :, :, None]
    e_fine, h_fine = (e_start, h_start)
    for substep in range(2):
        h_fine = h_fine - H_COEF * curl_forward(e_fine, None, None)
        e_fine = e_fine + coef_fine * curl_backward(h_fine, None, None)
        e_fine = jnp.where(inner, e_fine, e_start)
        h_fine = jnp.where(inner, h_fine, h_start)

    def coarsen(field):
        core = jnp.dot(field[:, 2:-2, 2:-2, :], halving, precision=hp)
        core = core.reshape(3, PB, 2, PB, 2, depth)
        return lax.optimization_barrier(jnp.sum(core, axis=(2, 4))) * 0.25
    start = (anchor, x_start + 1, y_start + 1, anchor)
    efield = lax.dynamic_update_slice(efield, coarsen(e_fine), start)
    hfield = lax.dynamic_update_slice(hfield, coarsen(h_fine), start)
    return (efield, hfield)

def face_normals(points, faces):
    live = (points >= 0).astype(jnp.float32)
    axis_num = faces // 2
    sign = (2 * (faces % 2) - 1).astype(jnp.float32)
    return jnp.stack([(axis_num == k).astype(jnp.float32) * sign * live for k in range(3)])

def cross_normal(normals, field):
    return jnp.stack([normals[1] * field[2] - normals[2] * field[1], normals[2] * field[0] - normals[0] * field[2], normals[0] * field[1] - normals[1] * field[0]])

def accumulate(currents, efield, hfield, points, normals, omega, moment):
    e_taken = jnp.take(efield.reshape(3, -1), points, axis=1)
    h_taken = jnp.take(hfield.reshape(3, -1), points, axis=1)
    sampled = jnp.concatenate([cross_normal(normals, h_taken), -cross_normal(normals, e_taken)], axis=0)
    cosine = jnp.cos(omega * moment)
    sine = jnp.sin(omega * moment)
    term = jnp.stack([sampled[None] * cosine[:, None, None], -sampled[None] * sine[:, None, None]], axis=1)
    return currents + term

def project(angle_rows, omega, currents, positions, scale):
    theta = math.pi * (angle_rows[:, 0].astype(jnp.float32) + 0.5) / NTH
    phi = 2.0 * math.pi * (angle_rows[:, 1].astype(jnp.float32) + 0.5) / NPH
    direction = jnp.stack([jnp.sin(theta) * jnp.cos(phi), jnp.sin(theta) * jnp.sin(phi), jnp.cos(theta)], axis=1)
    along = jnp.dot(direction, positions, precision=lax.Precision.HIGHEST, preferred_element_type=jnp.float32)
    pieces = []
    for freq_num in range(currents.shape[0]):
        phase = omega[freq_num] * along
        cosine = jnp.cos(phase)
        sine = jnp.sin(phase)
        real_cur = currents[freq_num, 0].T
        imag_cur = currents[freq_num, 1].T
        hp = lax.Precision.HIGHEST
        real_part = jnp.dot(cosine, real_cur, precision=hp) - jnp.dot(sine, imag_cur, precision=hp)
        imag_part = jnp.dot(sine, real_cur, precision=hp) + jnp.dot(cosine, imag_cur, precision=hp)
        pieces.append(real_part)
        pieces.append(imag_part)
    return jnp.concatenate(pieces, axis=1) * scale

def reference(efield, hfield, e_coef, omega, patch_owner, patch_corner, surface_points, surface_faces, angle_index):
    grid_x = CB * N_GX
    grid_y = CB * N_GY
    safe = jnp.maximum(surface_points, 0).astype(jnp.int32)
    block_x = jnp.arange(N_GX, dtype=jnp.int32)[:, None, None]
    block_y = jnp.arange(N_GY, dtype=jnp.int32)[None, :, None]
    cell_x = block_x * CB + safe // (CB * CZ)
    cell_y = block_y * CB + safe // CZ % CB
    cell_z = safe % CZ + 0 * block_x + 0 * block_y
    points = ((cell_x * grid_y + cell_y) * CZ + cell_z).reshape(-1).astype(jnp.int32)
    normals = face_normals(surface_points.reshape(-1), surface_faces.reshape(-1))
    currents = jnp.zeros((FREQ, 2, 6, points.shape[0]), jnp.float32)

    def apply(number, fields):
        owner = patch_owner[number]
        x_start = owner // N_GY * CB + patch_corner[number, 0] - 1
        y_start = owner % N_GY * CB + patch_corner[number, 1] - 1
        return refine(fields[0], fields[1], e_coef, x_start, y_start)
    for moment in range(STEPS):
        hfield = hfield - H_COEF * curl_forward(efield, None, None)
        efield = efield + e_coef * curl_backward(hfield, None, None)
        efield, hfield = lax.fori_loop(0, NPATCH, apply, (efield, hfield))
        currents = accumulate(currents, efield, hfield, points, normals, omega, float(moment + 1))
    cell_x = cell_x + 0 * cell_y
    cell_y = cell_y + 0 * cell_x
    positions = jnp.stack([(cell_x.astype(jnp.float32) + 0.5 - grid_x / 2.0).reshape(-1), (cell_y.astype(jnp.float32) + 0.5 - grid_y / 2.0).reshape(-1), (cell_z.astype(jnp.float32) + 0.5 - CZ / 2.0).reshape(-1)])
    scale = 1.0 / math.sqrt(NPTS)
    blocks = angle_index.reshape(ANG // 64, 64, 2)
    far = lax.map(lambda rows: project(rows, omega, currents, positions, scale), blocks)
    return (efield, hfield, far.reshape(ANG, 48))
```

```python
import math

import jax
import jax.numpy as jnp
import numpy as np
from jax import lax
from jax.experimental import pallas as pl
from jax.experimental.pallas import tpu as pltpu
from jax.sharding import PartitionSpec as P

PB = 8
SLOTS = 4
NTH = 128
NPH = 256
CB = 32
CZ = 128
ROWS = CB * CB
SPB = 256
FREQ = 4
GX = 8
GY = 16
ANG = 4096
QN = ANG // GX
QF = QN * FREQ
OWN = ANG // (GX * GY)
MESH = pl.DeviceIdType.MESH
F32 = jnp.float32
BF16 = jnp.bfloat16


def lanes_of(shape):
    return lax.broadcasted_iota(jnp.int32, shape, 1)


def rows_of(shape):
    return lax.broadcasted_iota(jnp.int32, shape, 0)


def z_next(v):
    return jnp.where(lanes_of(v.shape) == CZ - 1, 0.0, pltpu.roll(v, CZ - 1, 1))


def z_prev(v):
    return jnp.where(lanes_of(v.shape) == 0, 0.0, pltpu.roll(v, 1, 1))


def y_next(v, edge):
    n = v.shape[0]
    return jnp.where(rows_of(v.shape) == n - 1, edge, pltpu.roll(v, n - 1, 0))


def y_prev(v, edge):
    return jnp.where(rows_of(v.shape) == 0, edge, pltpu.roll(v, 1, 0))


def prepare(es, hs, out):
    out[0] = es[1, 0:CB]
    out[1] = es[2, 0:CB]
    last = (CB - 1) * CB
    ex, ey, ez = [es[k, last : last + CB] for k in range(3)]
    hy, hz = [hs[k, last + CB : last + 2 * CB] for k in (1, 2)]
    out[2] = hy - 0.5 * (z_next(ex) - ex + ez)
    out[3] = hz + 0.5 * (ey + y_next(ex, 0.0) - ex)
    out[8, 8:16] = ey[CB - 8 : CB] * 0.0 + es[1, CB - 1 : CB]
    out[8, 0:8] = ex[0:1] + jnp.zeros((8, CZ), F32)
    out[8, 16:32] = jnp.zeros((16, CZ), F32)
    out[4] = es[0, pl.ds(0, CB, stride=CB)]
    out[5] = es[2, pl.ds(0, CB, stride=CB)]
    ex, ey, ez = [es[k, pl.ds(CB - 1, CB, stride=CB)] for k in range(3)]
    hx, hz = [hs[k, pl.ds(2 * CB - 1, CB, stride=CB)] for k in (0, 2)]
    out[6] = hx + 0.5 * (ez + z_next(ey) - ey)
    out[7] = hz - 0.5 * (y_next(ey, 0.0) - ey + ex)


def place_halo(es, hs, halo, ye, yh):
    gx = lax.axis_index("gx")
    gy = lax.axis_index("gy")
    x_low = (gx > 0).astype(F32)
    x_high = (gx < GX - 1).astype(F32)
    y_low = (gy > 0).astype(F32)
    y_high = (gy < GY - 1).astype(F32)
    last_row = rows_of((CB, CZ)) == CB - 1
    es[1, ROWS : ROWS + CB] = halo[0] * x_high
    es[2, ROWS : ROWS + CB] = halo[1] * x_high
    ye[0] = halo[4] * y_high
    ye[1] = halo[5] * y_high
    corner = jnp.where(last_row, halo[8, 0:1] * (0.5 * y_high), 0.0)
    hs[1, 0:CB] = x_low * (halo[2] + 0.5 * es[2, 0:CB])
    hs[2, 0:CB] = x_low * (halo[3] - 0.5 * es[1, 0:CB] + corner)
    corner = jnp.where(last_row, halo[8, 8:9] * (0.5 * x_high), 0.0)
    yh[0] = y_low * (halo[6] - 0.5 * es[2, pl.ds(0, CB, stride=CB)])
    yh[1] = y_low * (halo[7] + 0.5 * es[0, pl.ds(0, CB, stride=CB)] - corner)


def advance(es, hs, cs, ye, yh):
    def slab(x, carry):
        r = pl.multiple_of(x * CB, CB)
        here = pl.ds(r, CB)
        after = pl.ds(pl.multiple_of(r + CB, CB), CB)
        ex, ey, ez = [es[k, here] for k in range(3)]
        ey1, ez1 = es[1, after], es[2, after]
        hx, hy, hz = [hs[k, after] for k in range(3)]
        hy0, hz0 = hs[1, here], hs[2, here]
        row = pl.ds(x, 1)
        hx = hx - 0.5 * (y_next(ez, ye[1, row]) - ez - z_next(ey) + ey)
        hy = hy - 0.5 * (z_next(ex) - ex - ez1 + ez)
        hz = hz - 0.5 * (ey1 - ey - y_next(ex, ye[0, row]) + ex)
        c = cs[here]
        ex = ex + c * (hz - y_prev(hz, yh[1, row]) - hy + z_prev(hy))
        ey = ey + c * (hx - z_prev(hx) - hz + hz0)
        ez = ez + c * (hy - hy0 - hx + y_prev(hx, yh[0, row]))
        for k, v in enumerate((hx, hy, hz)):
            hs[k, after] = v
        for k, v in enumerate((ex, ey, ez)):
            es[k, here] = v
        return carry

    lax.fori_loop(0, CB, slab, 0)


def neighbours():
    gx = lax.axis_index("gx")
    gy = lax.axis_index("gy")
    xn, xp = lax.rem(gx + 1, GX), lax.rem(gx + GX - 1, GX)
    yn, yp = lax.rem(gy + 1, GY), lax.rem(gy + GY - 1, GY)
    return [(xp, gy), (xn, gy), (gx, yp), (gx, yn), (xn, yp), (xp, yn)]


def pieces(ref, n):
    if n < 4:
        return ref.at[pl.ds(2 * n, 2)]
    return ref.at[8, pl.ds(8 * (n - 4), 8)]


def first_kernel(e_in, h_in, c_in, e_out, h_out, halo2, es, hs, cs, ye, yh, sent, halo1, local_sem, send_sem, recv_sem):
    loads = [
        pltpu.make_async_copy(e_in, es.at[:, pl.ds(0, ROWS)], local_sem.at[0]),
        pltpu.make_async_copy(h_in, hs.at[:, pl.ds(CB, ROWS)], local_sem.at[1]),
        pltpu.make_async_copy(c_in, cs, local_sem.at[2]),
    ]
    for copy in loads:
        copy.start()
    barrier = pltpu.get_barrier_semaphore()
    for device in neighbours():
        pl.semaphore_signal(barrier, inc=1, device_id=device, device_id_type=MESH)
    loads[0].wait()
    loads[1].wait()

    def exchange(number, halo):
        copies = []
        for n, device in enumerate(neighbours()):
            copy = pltpu.make_async_remote_copy(
                src_ref=pieces(sent.at[number], n),
                dst_ref=pieces(halo, n),
                send_sem=send_sem.at[number, n],
                recv_sem=recv_sem.at[number, n],
                device_id=device,
                device_id_type=MESH,
            )
            copy.start()
            copies.append(copy)
        return copies

    prepare(es, hs, sent.at[0])
    pl.semaphore_wait(barrier, 6)
    copies = exchange(0, halo1)
    loads[2].wait()
    for copy in copies:
        copy.wait()
    place_halo(es, hs, halo1, ye, yh)
    advance(es, hs, cs, ye, yh)
    prepare(es, hs, sent.at[1])
    copies = exchange(1, halo2)
    stores = [
        pltpu.make_async_copy(es.at[:, pl.ds(0, ROWS)], e_out, local_sem.at[0]),
        pltpu.make_async_copy(hs.at[:, pl.ds(CB, ROWS)], h_out, local_sem.at[1]),
    ]
    for copy in stores:
        copy.start()
    for copy in copies + stores:
        copy.wait()


def patch(es, hs, cs, x0, y0):
    first = rows_of((PB, CZ)) == 0
    final = rows_of((PB, CZ)) == PB - 1

    def e_at(k, i, j):
        return es[k, pl.ds((x0 + i) * CB + y0 + j, PB)]

    def h_at(k, i, j):
        return hs[k, pl.ds((x0 + i + 1) * CB + y0 + j, PB)]

    def up(v, edge):
        return jnp.where(final, edge, pltpu.roll(v, PB - 1, 0))

    def down(v, edge):
        return jnp.where(first, edge, pltpu.roll(v, 1, 0))

    class Cell:
        pass

    def averages(name, o, e, c, u1, u0, wu, v1, v0, wv, pa, pb):
        vm = 0.5 * (v0 + v1)
        um = 0.5 * (u0 + u1)
        qu = 0.25 * wu
        qv = 0.25 * wv
        base_a = e - c * (vm + qv)
        base_b = e + c * (um - qu)
        setattr(o, name + pa + "1", base_a + c * u1)
        setattr(o, name + pa + "0", base_a + c * (u0 - 0.5 * wu))
        setattr(o, name + pb + "1", base_b - c * v1)
        setattr(o, name + pb + "0", base_b - c * (v0 + 0.5 * wv))
        setattr(o, name + "s" + pa + "0", e + c * (u0 - wu - vm - 0.5 * wv))
        setattr(o, name + "s" + pb + "0", e + c * (um - 0.5 * wu - v0 - wv))

    def stage_one(i):
        o = Cell()
        ex, ey, ez = [e_at(k, i, 0) for k in range(3)]
        exu, ezu = e_at(0, i, 1), e_at(2, i, 1)
        exd, eyd, ezd = [e_at(k, i, -1) for k in range(3)]
        exf, eyf, ezf = [e_at(k, i + 1, 0) for k in range(3)]
        eyb, ezb = e_at(1, i - 1, 0), e_at(2, i - 1, 0)
        exbu, exb = e_at(0, i - 1, 1), e_at(0, i - 1, 0)
        eyfd = e_at(1, i + 1, -1)
        hx, hy, hz = [h_at(k, i, 0) for k in range(3)]
        hxd, hzd = h_at(0, i, -1), h_at(2, i, -1)
        hyb, hzb = h_at(1, i - 1, 0), h_at(2, i - 1, 0)
        c = cs[pl.ds((x0 + i) * CB + y0, PB)]
        dyex, dyez = exu - ex, ezu - ez
        dxey, dxez = eyf - ey, ezf - ez
        dzex, dzey = z_next(ex) - ex, z_next(ey) - ey
        dyexb = exbu - exb
        dxeyd = eyfd - eyd
        szex, szey = z_prev(dzex), z_prev(dzey)
        averages(
            "x", o, ex, c,
            0.5 * dyex, hz - hzd - 0.5 * (ex - exd), 0.5 * (dxey - dxeyd),
            -0.5 * dzex, hy - z_prev(hy) + 0.5 * szex, 0.5 * (dxez - z_prev(dxez)),
            "y", "z",
        )
        averages(
            "y", o, ey, c,
            0.5 * dzey, hx - z_prev(hx) - 0.5 * szey, 0.5 * (dyez - z_prev(dyez)),
            -0.5 * dxey, hz - hzb + 0.5 * (ey - eyb), 0.5 * (dyex - dyexb),
            "z", "x",
        )
        dzexb = z_next(exb) - exb
        dzeyd = z_next(eyd) - eyd
        averages(
            "z", o, ez, c,
            0.5 * dxez, hy - hyb - 0.5 * (ez - ezb), 0.5 * (dzex - dzexb),
            -0.5 * dyez, hx - hxd + 0.5 * (ez - ezd), 0.5 * (dzey - dzeyd),
            "x", "y",
        )
        o.c = c
        o.h = (hx, hy, hz)
        o.d = (dyez, dzey, dzex, dxez, dxey, dyex)
        o.down = (exd, eyd, ezd, eyfd, hxd, hzd, dzeyd)
        o.up = (exu, ezu, e_at(1, i, 1))
        return o

    def ring_ahead(i):
        o = Cell()
        ey, ez = e_at(1, i, 0), e_at(2, i, 0)
        o.yx0 = o.ysx0 = ey
        o.zx0 = o.zsx0 = ez
        return o

    def ring_behind(o):
        ex, ey, ez = [e_at(k, -1, 0) for k in range(3)]
        h2zx = h_at(2, -1, 0) - 0.5 * (o.yx0 - ey) + 0.25 * (e_at(0, -1, 1) - ex)
        h2yx = h_at(1, -1, 0) - 0.25 * (z_next(ex) - ex) + 0.5 * (o.zx0 - ez)
        return h2zx, h2yx

    def stage_two(o, n, behind):
        hx, hy, hz = o.h
        dyez, dzey, dzex, dxez, dxey, dyex = o.d
        exd, eyd, ezd, eyfd, hxd, hzd, dzeyd = o.down
        exu, ezu, eyu = o.up
        h2zx_b, h2yx_b = behind
        xy0u = up(o.xy0, exu)
        zy0u = up(o.zy0, ezu)
        h2zy = hz - 0.25 * dxey + 0.5 * dyex - 0.25 * (n.ysx0 - o.ysx0) + 0.5 * (xy0u - o.xy1)
        h2zx = hz - 0.5 * dxey + 0.25 * dyex - 0.5 * (n.yx0 - o.yx1) + 0.25 * (up(o.xsy0, exu) - o.xsy0)
        h2xz = hx - 0.25 * dyez + 0.5 * dzey - 0.25 * (up(o.zsy0, ezu) - o.zsy0) + 0.5 * (z_next(o.yz0) - o.yz1)
        h2xy = hx - 0.5 * dyez + 0.25 * dzey - 0.5 * (zy0u - o.zy1) + 0.25 * (z_next(o.ysz0) - o.ysz0)
        h2yx = hy - 0.25 * dzex + 0.5 * dxez - 0.25 * (z_next(o.xsz0) - o.xsz0) + 0.5 * (n.zx0 - o.zx1)
        h2yz = hy - 0.5 * dzex + 0.25 * dxez - 0.5 * (z_next(o.xz0) - o.xz1) + 0.25 * (n.zsx0 - o.zsx0)
        h2zy_d = down(h2zy, hzd - 0.25 * (eyfd - eyd) + 0.5 * (o.xy0 - exd))
        h2xy_d = down(h2xy, hxd - 0.5 * (o.zy0 - ezd) + 0.25 * dzeyd)
        half = 0.5 * o.c
        ex = 0.5 * (o.xy0 + o.xy1) + half * (h2zy - h2zy_d - h2yz + z_prev(h2yz))
        ey = 0.5 * (o.yz0 + o.yz1) + half * (h2xz - z_prev(h2xz) - h2zx + h2zx_b)
        ez = 0.5 * (o.zx0 + o.zx1) + half * (h2yx - h2yx_b - h2xy + h2xy_d)
        hx = hx - 0.25 * (dyez - dzey + zy0u - o.zy0 - z_next(o.yz0) + o.yz0)
        hy = hy - 0.25 * (dzex - dxez + z_next(o.xz0) - o.xz0 - n.zx0 + o.zx0)
        hz = hz - 0.25 * (dxey - dyex + n.yx0 - o.yx0 - xy0u + o.xy0)
        return (ex, ey, ez), (hx, hy, hz), (h2zx, h2yx)

    now = stage_one(0)
    behind = ring_behind(now)
    for i in range(PB):
        later = stage_one(i + 1) if i < PB - 1 else ring_ahead(i + 1)
        e_new, h_new, behind = stage_two(now, later, behind)
        pending = (i, e_new, h_new)
        if i > 0:
            write(es, hs, x0, y0, previous)
        previous = pending
        now = later
    write(es, hs, x0, y0, previous)


def write(es, hs, x0, y0, item):
    i, e_new, h_new = item
    for k in range(3):
        es[k, pl.ds((x0 + i) * CB + y0, PB)] = e_new[k]
        hs[k, pl.ds((x0 + i + 1) * CB + y0, PB)] = h_new[k]


def second_kernel(owner, corner, points, faces, place, halo, e_in, h_in, c_in, e_out, h_out, sampled, es, hs, cs, ye, yh, taken, slot_x, slot_y, count, sem):
    loads = [
        pltpu.make_async_copy(e_in, es.at[:, pl.ds(0, ROWS)], sem.at[0]),
        pltpu.make_async_copy(h_in, hs.at[:, pl.ds(CB, ROWS)], sem.at[1]),
        pltpu.make_async_copy(c_in, cs, sem.at[2]),
    ]
    for copy in loads:
        copy.start()
    me = lax.axis_index("gx") * GY + lax.axis_index("gy")

    def look(n, found):
        slot_x[found] = corner[2 * n]
        slot_y[found] = corner[2 * n + 1]
        return jnp.minimum(found + (owner[n] == me).astype(jnp.int32), SLOTS)

    count[0] = lax.fori_loop(0, GX * GY, look, 0, unroll=8)
    for copy in loads:
        copy.wait()
    lane = lanes_of((1, CZ))

    def patches():
        def one(n, carry):
            patch(es, hs, cs, slot_x[n], slot_y[n])
            return carry

        lax.fori_loop(0, count[0], one, 0)

    def sample():
        def one(n, carry):
            cell = jnp.maximum(points[n], 0)
            row = cell // CZ
            mask = lane == cell % CZ
            k = faces[n] // 2
            k1 = jnp.where(k == 2, 0, k + 1)
            k2 = jnp.where(k == 0, 2, k - 1)
            taken[pl.ds(n + 0 * SPB, 1)] = jnp.where(mask, hs[k1, pl.ds(row + CB, 1)], 0.0)
            taken[pl.ds(n + 1 * SPB, 1)] = jnp.where(mask, hs[k2, pl.ds(row + CB, 1)], 0.0)
            taken[pl.ds(n + 2 * SPB, 1)] = jnp.where(mask, es[k1, pl.ds(row, 1)], 0.0)
            taken[pl.ds(n + 3 * SPB, 1)] = jnp.where(mask, es[k2, pl.ds(row, 1)], 0.0)
            return carry

        lax.fori_loop(0, SPB, one, 0, unroll=8)
        return lax.dot_general(
            jnp.ones((8, CZ), F32), taken[...], (((1,), (1,)), ((), ())),
            precision=lax.Precision.HIGHEST, preferred_element_type=F32,
        )

    slots = place[0:1]
    face = place[1:2]
    sign = jnp.where(slots >= 0, (2 * (face % 2) - 1).astype(F32), 0.0)
    for moment in range(2):
        if moment:
            place_halo(es, hs, halo, ye, yh)
            advance(es, hs, cs, ye, yh)
        patches()
        if moment:
            stores = [
                pltpu.make_async_copy(es.at[:, pl.ds(0, ROWS)], e_out, sem.at[0]),
                pltpu.make_async_copy(hs.at[:, pl.ds(CB, ROWS)], h_out, sem.at[1]),
            ]
            for copy in stores:
                copy.start()
        got = sample()
        got = [got[0:1, j * SPB : (j + 1) * SPB] for j in range(4)]
        sampled[4 * moment : 4 * moment + 1] = -sign * got[1]
        sampled[4 * moment + 1 : 4 * moment + 2] = sign * got[0]
        sampled[4 * moment + 2 : 4 * moment + 3] = sign * got[3]
        sampled[4 * moment + 3 : 4 * moment + 4] = -sign * got[2]
    cell = jnp.maximum(slots, 0)
    sampled[8:9] = (cell // (CB * CZ)).astype(F32)
    sampled[9:10] = (cell // CZ % CB).astype(F32)
    sampled[10:11] = (cell % CZ).astype(F32)
    sampled[11:12] = jnp.where(slots >= 0, face, 6).astype(F32)
    sampled[12:16] = jnp.zeros((4, SPB), F32)
    for copy in stores:
        copy.wait()


def fitted(function, degrees, points=4001):
    r = np.cos(np.linspace(0.0, np.pi, points)) * 0.5
    basis = np.stack([r**d for d in degrees], axis=1)
    return [float(v) for v in np.linalg.lstsq(basis, function(np.pi * r) * math.sqrt(2.0), rcond=None)[0]]


SIN = fitted(np.sin, (1, 3, 5, 7, 9))
COS = fitted(np.cos, (0, 2, 4, 6, 8))


def turn(t):
    r = t - jnp.round(t)
    r2 = r * r
    s = r * (SIN[0] + r2 * (SIN[1] + r2 * (SIN[2] + r2 * (SIN[3] + r2 * SIN[4]))))
    c = COS[0] + r2 * (COS[1] + r2 * (COS[2] + r2 * (COS[3] + r2 * COS[4])))
    return 1.0 - s * s, s * c


def split(v):
    high = v.astype(BF16)
    return high, (v - high.astype(F32)).astype(BF16)


def dot(a, b):
    return jnp.dot(a, b, preferred_element_type=F32)


def dot_t(a, b):
    return lax.dot_general(a, b, (((1,), (1,)), ((), ())), preferred_element_type=F32)


XF = 128
ZF = 64
YF_ROWS = 96
CHUNK = 256
X_FACE = 111
Z_FACE = 47


def third_kernel(omega, sampled, angles, far, got, gathered, kdir, ta, tc, tb, tcf, hot, spread_hi, spread_lo, lhs1, lhs2, lhsz, big, acc, rows48, send_buf, recv_buf, send1, recv1, send2, recv2):
    gx = lax.axis_index("gx")
    gy = lax.axis_index("gy")
    barrier = pltpu.get_barrier_semaphore()
    for d in range(1, GX):
        pl.semaphore_signal(barrier, inc=1, device_id=(lax.rem(gx + d, GX), gy), device_id_type=MESH)
    for d in range(1, GY):
        pl.semaphore_signal(barrier, inc=1, device_id=(gx, lax.rem(gy + d, GY)), device_id_type=MESH)
    pl.semaphore_wait(barrier, GX + GY - 2)
    first = []
    for d in range(1, GX):
        copy = pltpu.make_async_remote_copy(
            src_ref=sampled,
            dst_ref=gathered.at[GX - d],
            send_sem=send1.at[d],
            recv_sem=recv1.at[GX - d],
            device_id=(lax.rem(gx + d, GX), gy),
            device_id_type=MESH,
        )
        copy.start()
        first.append(copy)

    index = angles[...].astype(F32)
    theta = math.pi * (index[0:1] + 0.5) / NTH
    phi = 2.0 * math.pi * (index[1:2] + 0.5) / NPH
    st, ct = jnp.sin(theta), jnp.cos(theta)
    sp, cp = jnp.sin(phi), jnp.cos(phi)
    for f in range(FREQ):
        w = omega[f] * (1.0 / (2.0 * math.pi))
        kdir[0:1, f * QN : (f + 1) * QN] = st * cp * w
        kdir[1:2, f * QN : (f + 1) * QN] = st * sp * w
        kdir[2:3, f * QN : (f + 1) * QN] = ct * w

    y_start = (gy * CB).astype(F32) + (0.5 - CB * GY / 2.0)

    def tables(n, carry):
        lanes = pl.ds(pl.multiple_of(n * CHUNK, CHUNK), CHUNK)
        kx, ky, kz = kdir[0:1, lanes], kdir[1:2, lanes], kdir[2:3, lanes]
        for j in range(0, XF, 16):
            at = rows_of((16, CHUNK)).astype(F32) + (j + 0.5)
            for k, v in enumerate(turn(at * kx)):
                high, low = split(v)
                ta[k, j : j + 16, lanes] = high
                ta[k, XF + j : XF + j + 16, lanes] = low
        for j in range(0, ZF, 16):
            at = rows_of((16, CHUNK)).astype(F32) + (j + 0.5)
            for k, v in enumerate(turn(at * kz)):
                high, low = split(v)
                tc[k, j : j + 16, lanes] = high
                tc[k, ZF + j : ZF + j + 16, lanes] = low
                tc[k, 2 * ZF + j : 2 * ZF + j + 16, lanes] = high
                tc[k, 3 * ZF + j : 3 * ZF + j + 16, lanes] = jnp.zeros((16, CHUNK), BF16)
                tcf[k, j : j + 16, lanes] = v
        for j in range(0, CB, 16):
            at = rows_of((16, CHUNK)).astype(F32) + (y_start + j)
            for k, v in enumerate(turn(at * ky)):
                tb[k, j : j + 16, lanes] = v
        at = jnp.full((8, CHUNK), X_FACE + 0.5, F32)
        for k, v in enumerate(turn(at * kx)):
            tb[k, CB : CB + 8, lanes] = v
        return carry

    lax.fori_loop(0, QF // CHUNK, tables, 0)
    gathered[0] = sampled[...]
    for copy in first:
        copy.wait()

    for b in range(GX):
        lanes = slice(b * SPB, (b + 1) * SPB)
        got[0:16, lanes] = gathered[b]
        block = lax.rem(gx + b, GX)
        x = gathered[b, 8:9] + (block * CB).astype(F32)
        z = gathered[b, 10:11]
        got[12:13, lanes] = jnp.where(x < 128.0, 127.0 - x, x - 128.0)
        got[13:14, lanes] = jnp.where(x < 128.0, -1.0, 1.0)
        got[14:15, lanes] = jnp.where(z < 64.0, 63.0 - z, z - 64.0)
        got[15:16, lanes] = jnp.where(z < 64.0, -1.0, 1.0)

    slots = GX * SPB

    def one_hot(place_row, sign_row, count):
        for b in range(GX):
            lanes = slice(b * SPB, (b + 1) * SPB)
            where_at = got[place_row : place_row + 1, lanes]
            sign = got[sign_row : sign_row + 1, lanes]
            for j in range(0, count, 16):
                at = rows_of((16, SPB)).astype(F32) + float(j)
                same = at == where_at
                hot[j : j + 16, lanes] = jnp.where(same, 1.0, 0.0).astype(BF16)
                hot[count + j : count + j + 16, lanes] = jnp.where(same, sign, 0.0).astype(BF16)

    def spread(low_face, high_face):
        for b in range(GX):
            lanes = slice(b * SPB, (b + 1) * SPB)
            cols = got[0:8, lanes]
            face = got[11:12, lanes]
            v = jnp.concatenate([jnp.where(face == low_face, cols, 0.0), jnp.where(face == high_face, cols, 0.0)], axis=0)
            high = v.astype(BF16).astype(F32)
            low = v - high
            ys = got[9:10, lanes]

            def one(y, carry):
                same = ys == y.astype(F32)
                at = pl.ds(pl.multiple_of(y * 16, 16), 16)
                spread_hi[at, lanes] = jnp.where(same, high, 0.0).astype(BF16)
                spread_lo[at, lanes] = jnp.where(same, low, 0.0).astype(BF16)
                return carry

            lax.fori_loop(0, CB, one, 0, unroll=4)

    def spread_y():
        for b in range(GX):
            lanes = slice(b * SPB, (b + 1) * SPB)
            face = got[11:12, lanes]
            v = jnp.where((face == 2.0) | (face == 3.0), got[0:8, lanes], 0.0)
            v = jnp.concatenate([v, v], axis=0)
            high = v.astype(BF16).astype(F32)
            low = v - high
            zs = got[10:11, lanes]
            second = (rows_of((16, SPB)) // 8).astype(F32)

            def one(o, carry):
                same = zs == second + (2 * o + 16).astype(F32)
                at = pl.ds(pl.multiple_of(o * 16, 16), 16)
                spread_hi[at, lanes] = jnp.where(same, high, 0.0).astype(BF16)
                spread_lo[at, lanes] = jnp.where(same, low, 0.0).astype(BF16)
                return carry

            lax.fori_loop(0, YF_ROWS // 2, one, 0, unroll=4)

    def dense(count):
        for m in range(0, count, CHUNK):
            d = dot_t(spread_hi[m : m + CHUNK], hot[...]) + dot_t(spread_lo[m : m + CHUNK], hot[...])
            for k in range(2):
                high, low = split(d[:, k * XF : (k + 1) * XF])
                lhs1[k, m : m + CHUNK, 0:XF] = high
                lhs1[k, m : m + CHUNK, XF : 2 * XF] = high
                lhs2[k, m : m + CHUNK] = low

    one_hot(12, 13, XF)
    spread(4.0, 5.0)
    dense(CB * 16)

    def outer_y(n, base):
        lanes = pl.ds(pl.multiple_of(n * CHUNK, CHUNK), CHUNK)

        def one(y, total):
            re, im = total
            at = pl.ds(pl.multiple_of(y * 16, 16), 16)
            g_re, g_im = big[0, at], big[1, at]
            bc, bs = tb[0, pl.ds(y, 1), lanes], tb[1, pl.ds(y, 1), lanes]
            return re + (bc * g_re - bs * g_im), im + (bc * g_im + bs * g_re)

        zero = jnp.zeros((16, CHUNK), F32)
        re, im = lax.fori_loop(0, CB, one, (zero, zero), unroll=4)
        acc[base, 0, :, lanes] = re
        acc[base, 1, :, lanes] = im

    def across_z(n, carry):
        lanes = pl.ds(pl.multiple_of(n * CHUNK, CHUNK), CHUNK)
        for k in range(2):
            table = ta[k, :, lanes]
            big[k, 0 : CB * 16] = dot(lhs1[k, 0 : CB * 16], table) + dot(lhs2[k, 0 : CB * 16], table[0:XF])
        outer_y(n, 0)
        return carry

    lax.fori_loop(0, QF // CHUNK, across_z, 0)
    edge = (gy == 0) | (gy == GY - 1)

    @pl.when(jnp.logical_not(edge))
    def _():
        acc[2] = jnp.zeros((2, 16, QF), F32)

    @pl.when(edge)
    def _():
        spread_y()
        dense(YF_ROWS * 8)

        def across_y(n, carry):
            lanes = pl.ds(pl.multiple_of(n * CHUNK, CHUNK), CHUNK)
            for k in range(2):
                table = ta[k, :, lanes]
                big[k] = dot(lhs1[k], table) + dot(lhs2[k], table[0:XF])

            def one(o, total):
                re, im = total
                below = pl.ds(pl.multiple_of((Z_FACE - o) * 8, 8), 8)
                above = pl.ds(pl.multiple_of((Z_FACE + 1 + o) * 8, 8), 8)
                cc, cs = tcf[0, pl.ds(o, 1), lanes], tcf[1, pl.ds(o, 1), lanes]
                a_re, a_im, b_re, b_im = big[0, above], big[1, above], big[0, below], big[1, below]
                re = re + (cc * (a_re + b_re) - cs * (a_im - b_im))
                im = im + (cc * (a_im + b_im) + cs * (a_re - b_re))
                return re, im

            zero = jnp.zeros((8, CHUNK), F32)
            re, im = lax.fori_loop(0, YF_ROWS // 2, one, (zero, zero), unroll=4)
            acc[2, 0, 0:8, lanes] = re
            acc[2, 1, 0:8, lanes] = im
            return carry

        lax.fori_loop(0, QF // CHUNK, across_y, 0)

    one_hot(14, 15, ZF)
    spread(0.0, 1.0)
    for m in range(0, CB * 16, CHUNK):
        d = dot_t(spread_hi[m : m + CHUNK], hot[0 : 2 * ZF]) + dot_t(spread_lo[m : m + CHUNK], hot[0 : 2 * ZF])
        for k in range(2):
            high, low = split(d[:, k * ZF : (k + 1) * ZF])
            lhsz[k, m : m + CHUNK] = jnp.concatenate([high, high, low, jnp.zeros_like(low)], axis=1)

    def across_x(n, carry):
        lanes = pl.ds(pl.multiple_of(n * CHUNK, CHUNK), CHUNK)
        for k in range(2):
            big[k, 0 : CB * 16] = dot(lhsz[k], tc[k, :, lanes])
        outer_y(n, 1)
        return carry

    lax.fori_loop(0, QF // CHUNK, across_x, 0)

    scale = 1.0 / math.sqrt(GX * GY * SPB)
    y_face = jnp.where(gy == 0, 16, 15)
    moment = 1.0 + (rows_of((8, 1)) // 4).astype(F32)
    for f in range(FREQ):
        lanes = slice(f * QN, (f + 1) * QN)
        mc, ms = turn(omega[f] * (1.0 / (2.0 * math.pi)) * moment)
        mc, ms = mc * scale, ms * scale

        def both(base, c, s):
            low_re, high_re = acc[base, 0, 0:8, lanes], acc[base, 0, 8:16, lanes]
            low_im, high_im = acc[base, 1, 0:8, lanes], acc[base, 1, 8:16, lanes]
            re = c * (low_re + high_re) + s * (low_im - high_im)
            im = c * (low_im + high_im) + s * (high_re - low_re)
            return re, im

        def late(re, im):
            a, b = mc * re + ms * im, mc * im - ms * re
            return a[0:4] + a[4:8], b[0:4] + b[4:8]

        zf = late(*both(0, tcf[0, Z_FACE : Z_FACE + 1, lanes], tcf[1, Z_FACE : Z_FACE + 1, lanes]))
        xf = late(*both(1, tb[0, CB : CB + 1, lanes], tb[1, CB : CB + 1, lanes]))
        c, s = tb[0, pl.ds(y_face, 1), lanes], tb[1, pl.ds(y_face, 1), lanes]
        re, im = acc[2, 0, 0:8, lanes], acc[2, 1, 0:8, lanes]
        yf = late(c * re - s * im, c * im + s * re)
        for k in range(2):
            z4, x4, y4 = zf[k], xf[k], yf[k]
            six = [
                z4[0:1] + y4[1:2], z4[1:2] + x4[0:1], x4[1:2] + y4[0:1],
                z4[2:3] + y4[3:4], z4[3:4] + x4[2:3], x4[3:4] + y4[2:3],
            ]
            for j, v in enumerate(six):
                rows48[12 * f + 6 * k + j : 12 * f + 6 * k + j + 1] = v
    rows48[48:128] = jnp.zeros((80, QN), F32)
    for t in range(0, QN, 128):
        send_buf[t : t + 128] = jnp.transpose(rows48[:, t : t + 128])

    second = []
    for d in range(1, GY):
        to = lax.rem(gy + d, GY)
        copy = pltpu.make_async_remote_copy(
            src_ref=send_buf.at[pl.ds(pl.multiple_of(to * OWN, OWN), OWN)],
            dst_ref=recv_buf.at[GY - d],
            send_sem=send2.at[d],
            recv_sem=recv2.at[GY - d],
            device_id=(gx, to),
            device_id_type=MESH,
        )
        copy.start()
        second.append(copy)
    total = send_buf[pl.ds(pl.multiple_of(gy * OWN, OWN), OWN)]
    for copy in second:
        copy.wait()
    for d in range(1, GY):
        total = total + recv_buf[d]
    far[...] = total[:, 0:48]


VMEM = pl.BlockSpec(memory_space=pltpu.VMEM)
SMEM = pl.BlockSpec(memory_space=pltpu.SMEM)
ANY = pl.BlockSpec(memory_space=pl.ANY)


def local(efield, hfield, e_coef, omega, patch_owner, patch_corner, surface_points, surface_faces, angle_index):
    field = jax.ShapeDtypeStruct((3, ROWS, CZ), F32)
    fields = [
        pltpu.VMEM((3, ROWS + CB, CZ), F32),
        pltpu.VMEM((3, ROWS + CB, CZ), F32),
        pltpu.VMEM((ROWS, CZ), F32),
        pltpu.VMEM((2, CB, CZ), F32),
        pltpu.VMEM((2, CB, CZ), F32),
    ]
    coef = e_coef.reshape(ROWS, CZ)
    efield, hfield, halo = pl.pallas_call(
        first_kernel,
        out_shape=(field, field, jax.ShapeDtypeStruct((9, CB, CZ), F32)),
        in_specs=[ANY, ANY, ANY],
        out_specs=(ANY, ANY, VMEM),
        scratch_shapes=fields
        + [
            pltpu.VMEM((2, 9, CB, CZ), F32),
            pltpu.VMEM((9, CB, CZ), F32),
            pltpu.SemaphoreType.DMA((3,)),
            pltpu.SemaphoreType.DMA((2, 6)),
            pltpu.SemaphoreType.DMA((2, 6)),
        ],
        compiler_params=pltpu.CompilerParams(collective_id=0, has_side_effects=True, vmem_limit_bytes=32 * 2**20),
        name="first_step",
    )(efield.reshape(3, ROWS, CZ), hfield.reshape(3, ROWS, CZ), coef)
    points = surface_points.reshape(SPB)
    faces = surface_faces.reshape(SPB)
    place = jnp.stack([points, faces])
    efield, hfield, sampled = pl.pallas_call(
        second_kernel,
        out_shape=(field, field, jax.ShapeDtypeStruct((16, SPB), F32)),
        in_specs=[SMEM, SMEM, SMEM, SMEM, VMEM, VMEM, ANY, ANY, ANY],
        out_specs=(ANY, ANY, VMEM),
        scratch_shapes=fields
        + [
            pltpu.VMEM((4 * SPB, CZ), F32),
            pltpu.SMEM((SLOTS + 1,), jnp.int32),
            pltpu.SMEM((SLOTS + 1,), jnp.int32),
            pltpu.SMEM((1,), jnp.int32),
            pltpu.SemaphoreType.DMA((3,)),
        ],
        compiler_params=pltpu.CompilerParams(vmem_limit_bytes=32 * 2**20),
        name="patches",
    )(patch_owner, patch_corner.reshape(-1), points, faces, place, halo, efield, hfield, coef)
    mine = lax.dynamic_slice(angle_index, (lax.axis_index("gx") * QN, 0), (QN, 2)).T
    far = pl.pallas_call(
        third_kernel,
        out_shape=jax.ShapeDtypeStruct((OWN, 48), F32),
        in_specs=[SMEM, VMEM, VMEM],
        out_specs=VMEM,
        scratch_shapes=[
            pltpu.VMEM((16, GX * SPB), F32),
            pltpu.VMEM((GX, 16, SPB), F32),
            pltpu.VMEM((8, QF), F32),
            pltpu.VMEM((2, 2 * XF, QF), BF16),
            pltpu.VMEM((2, 4 * ZF, QF), BF16),
            pltpu.VMEM((2, CB + 8, QF), F32),
            pltpu.VMEM((2, ZF, QF), F32),
            pltpu.VMEM((2 * XF, GX * SPB), BF16),
            pltpu.VMEM((YF_ROWS * 8, GX * SPB), BF16),
            pltpu.VMEM((YF_ROWS * 8, GX * SPB), BF16),
            pltpu.VMEM((2, YF_ROWS * 8, 2 * XF), BF16),
            pltpu.VMEM((2, YF_ROWS * 8, XF), BF16),
            pltpu.VMEM((2, CB * 16, 4 * ZF), BF16),
            pltpu.VMEM((2, YF_ROWS * 8, CHUNK), F32),
            pltpu.VMEM((3, 2, 16, QF), F32),
            pltpu.VMEM((128, QN), F32),
            pltpu.VMEM((QN, 128), F32),
            pltpu.VMEM((GY, OWN, 128), F32),
            pltpu.SemaphoreType.DMA((GX,)),
            pltpu.SemaphoreType.DMA((GX,)),
            pltpu.SemaphoreType.DMA((GY,)),
            pltpu.SemaphoreType.DMA((GY,)),
        ],
        compiler_params=pltpu.CompilerParams(collective_id=1, has_side_effects=True, vmem_limit_bytes=48 * 2**20),
        name="projection",
    )(omega, sampled, mine)
    shape = (3, CB, CB, CZ)
    return efield.reshape(shape), hfield.reshape(shape), far


def solution(mesh):
    placed = (
        P(None, "gx", "gy", None),
        P(None, "gx", "gy", None),
        P("gx", "gy", None),
        P(),
        P(),
        P(),
        P("gx", "gy", None),
        P("gx", "gy", None),
        P(),
    )
    return jax.shard_map(
        local,
        mesh=mesh,
        in_specs=placed,
        out_specs=(P(None, "gx", "gy", None), P(None, "gx", "gy", None), P(("gx", "gy"), None)),
        check_vma=False,
    )
```

```python
import math

import jax
import jax.numpy as jnp
import numpy as np
from jax import lax
from jax.experimental import pallas as pl
from jax.experimental.pallas import tpu as pltpu
from jax.sharding import PartitionSpec as P

PB = 8
SLOTS = 4
NTH = 128
NPH = 256
CB = 32
CZ = 128
ROWS = CB * CB
SPB = 256
FREQ = 4
GX = 8
GY = 16
ANG = 4096
QN = ANG // GX
QF = QN * FREQ
OWN = ANG // (GX * GY)
MESH = pl.DeviceIdType.MESH
F32 = jnp.float32
BF16 = jnp.bfloat16


def lanes_of(shape):
    return lax.broadcasted_iota(jnp.int32, shape, 1)


def rows_of(shape):
    return lax.broadcasted_iota(jnp.int32, shape, 0)


def z_next(v):
    return jnp.where(lanes_of(v.shape) == CZ - 1, 0.0, pltpu.roll(v, CZ - 1, 1))


def z_prev(v):
    return jnp.where(lanes_of(v.shape) == 0, 0.0, pltpu.roll(v, 1, 1))


def y_next(v, edge):
    n = v.shape[0]
    return jnp.where(rows_of(v.shape) == n - 1, edge, pltpu.roll(v, n - 1, 0))


def y_prev(v, edge):
    return jnp.where(rows_of(v.shape) == 0, edge, pltpu.roll(v, 1, 0))


def prepare(es, hs, out):
    out[0] = es[1, 0:CB]
    out[1] = es[2, 0:CB]
    last = (CB - 1) * CB
    ex, ey, ez = [es[k, last : last + CB] for k in range(3)]
    hy, hz = [hs[k, last + CB : last + 2 * CB] for k in (1, 2)]
    out[2] = hy - 0.5 * (z_next(ex) - ex + ez)
    out[3] = hz + 0.5 * (ey + y_next(ex, 0.0) - ex)
    out[8, 8:16] = ey[CB - 8 : CB] * 0.0 + es[1, CB - 1 : CB]
    out[8, 0:8] = ex[0:1] + jnp.zeros((8, CZ), F32)
    out[8, 16:32] = jnp.zeros((16, CZ), F32)
    out[4] = es[0, pl.ds(0, CB, stride=CB)]
    out[5] = es[2, pl.ds(0, CB, stride=CB)]
    ex, ey, ez = [es[k, pl.ds(CB - 1, CB, stride=CB)] for k in range(3)]
    hx, hz = [hs[k, pl.ds(2 * CB - 1, CB, stride=CB)] for k in (0, 2)]
    out[6] = hx + 0.5 * (ez + z_next(ey) - ey)
    out[7] = hz - 0.5 * (y_next(ey, 0.0) - ey + ex)


def place_halo(es, hs, halo, ye, yh):
    gx = lax.axis_index("gx")
    gy = lax.axis_index("gy")
    x_low = (gx > 0).astype(F32)
    x_high = (gx < GX - 1).astype(F32)
    y_low = (gy > 0).astype(F32)
    y_high = (gy < GY - 1).astype(F32)
    last_row = rows_of((CB, CZ)) == CB - 1
    es[1, ROWS : ROWS + CB] = halo[0] * x_high
    es[2, ROWS : ROWS + CB] = halo[1] * x_high
    ye[0] = halo[4] * y_high
    ye[1] = halo[5] * y_high
    corner = jnp.where(last_row, halo[8, 0:1] * (0.5 * y_high), 0.0)
    hs[1, 0:CB] = x_low * (halo[2] + 0.5 * es[2, 0:CB])
    hs[2, 0:CB] = x_low * (halo[3] - 0.5 * es[1, 0:CB] + corner)
    corner = jnp.where(last_row, halo[8, 8:9] * (0.5 * x_high), 0.0)
    yh[0] = y_low * (halo[6] - 0.5 * es[2, pl.ds(0, CB, stride=CB)])
    yh[1] = y_low * (halo[7] + 0.5 * es[0, pl.ds(0, CB, stride=CB)] - corner)


def advance(es, hs, cs, ye, yh):
    last = rows_of((CB, CZ)) == CB - 1
    for x in range(CB):
        r = x * CB
        here, after = slice(r, r + CB), slice(r + CB, r + 2 * CB)
        ex, ey, ez = [es[k, here] for k in range(3)]
        ey1, ez1 = es[1, after], es[2, after]
        hx, hy, hz = [hs[k, after] for k in range(3)]
        if x == 0:
            hy0, hz0 = hs[1, here], hs[2, here]
        exu = jnp.where(last, ye[0, x : x + 1], es[0, r + 1 : r + CB + 1])
        ezu = jnp.where(last, ye[1, x : x + 1], es[2, r + 1 : r + CB + 1])
        hx = hx - 0.5 * (ezu - ez - z_next(ey) + ey)
        hy = hy - 0.5 * (z_next(ex) - ex - ez1 + ez)
        hz = hz - 0.5 * (ey1 - ey - exu + ex)
        for k, v in enumerate((hx, hy, hz)):
            hs[k, after] = v
        c = cs[here]
        ex = ex + c * (hz - y_prev(hz, yh[1, x : x + 1]) - hy + z_prev(hy))
        ey = ey + c * (hx - z_prev(hx) - hz + hz0)
        ez = ez + c * (hy - hy0 - hx + y_prev(hx, yh[0, x : x + 1]))
        for k, v in enumerate((ex, ey, ez)):
            es[k, here] = v
        hy0, hz0 = hy, hz


def neighbours():
    gx = lax.axis_index("gx")
    gy = lax.axis_index("gy")
    xn, xp = lax.rem(gx + 1, GX), lax.rem(gx + GX - 1, GX)
    yn, yp = lax.rem(gy + 1, GY), lax.rem(gy + GY - 1, GY)
    return [(xp, gy), (xn, gy), (gx, yp), (gx, yn), (xn, yp), (xp, yn)]


def pieces(ref, n):
    if n < 4:
        return ref.at[pl.ds(2 * n, 2)]
    return ref.at[8, pl.ds(8 * (n - 4), 8)]


def fitted(function, degrees, points=4001):
    r = np.cos(np.linspace(0.0, np.pi, points)) * 0.5
    basis = np.stack([r**d for d in degrees], axis=1)
    return [float(v) for v in np.linalg.lstsq(basis, function(np.pi * r) * math.sqrt(2.0), rcond=None)[0]]


SIN = fitted(np.sin, (1, 3, 5, 7, 9))
COS = fitted(np.cos, (0, 2, 4, 6, 8))


def turn(t):
    r = t - jnp.round(t)
    r2 = r * r
    s = r * (SIN[0] + r2 * (SIN[1] + r2 * (SIN[2] + r2 * (SIN[3] + r2 * SIN[4]))))
    c = COS[0] + r2 * (COS[1] + r2 * (COS[2] + r2 * (COS[3] + r2 * COS[4])))
    return 1.0 - s * s, s * c


def split(v):
    high = v.astype(BF16)
    return high, (v - high.astype(F32)).astype(BF16)


def dot(a, b):
    return jnp.dot(a, b, preferred_element_type=F32)


def dot_t(a, b):
    return lax.dot_general(a, b, (((1,), (1,)), ((), ())), preferred_element_type=F32)


CUT1 = 2
CUT2 = 5
XF = 128
ZF = 64
YF_ROWS = 96
CHUNK = 256
X_FACE = 111
Z_FACE = 47


def directions(omega, angles, kdir):
    index = angles[...].astype(F32)
    theta = math.pi * (index[0:1] + 0.5) / NTH
    phi = 2.0 * math.pi * (index[1:2] + 0.5) / NPH
    st, ct = jnp.sin(theta), jnp.cos(theta)
    sp, cp = jnp.sin(phi), jnp.cos(phi)
    for f in range(FREQ):
        w = omega[f] * (1.0 / (2.0 * math.pi))
        lanes = slice(f * QN, (f + 1) * QN)
        kdir[0:1, lanes] = st * cp * w
        kdir[1:2, lanes] = st * sp * w
        kdir[2:3, lanes] = ct * w


def tables(kdir, ta, tc, tb, tcf, n):
    y_start = (lax.axis_index("gy") * CB).astype(F32) + (0.5 - CB * GY / 2.0)
    lanes = pl.ds(pl.multiple_of(n * CHUNK, CHUNK), CHUNK)
    kx, ky, kz = kdir[0:1, lanes], kdir[1:2, lanes], kdir[2:3, lanes]
    count = rows_of((16, CHUNK)).astype(F32)
    for j in range(0, XF, 16):
        for k, v in enumerate(turn((count + (j + 0.5)) * kx)):
            high, low = split(v)
            ta[k, j : j + 16, lanes] = high
            ta[k, XF + j : XF + j + 16, lanes] = low
    for j in range(0, ZF, 16):
        for k, v in enumerate(turn((count + (j + 0.5)) * kz)):
            high, low = split(v)
            tc[k, j : j + 16, lanes] = high
            tc[k, ZF + j : ZF + j + 16, lanes] = low
            tcf[k, j : j + 16, lanes] = v
    for j in range(0, CB, 16):
        for k, v in enumerate(turn((count + (y_start + j)) * ky)):
            tb[k, j : j + 16, lanes] = v
    for k, v in enumerate(turn(jnp.full((8, CHUNK), X_FACE + 0.5, F32) * kx)):
        tb[k, CB : CB + 8, lanes] = v


def first_kernel(omega, angles, e_in, h_in, c_in, e_out, h_out, halo2, ta_out, tc_out, tb_out, tcf_out, kdir, ta, tc, tb, tcf, es, hs, cs, ye, yh, sent, halo1, local_sem, send_sem, recv_sem):
    loads = [
        pltpu.make_async_copy(e_in, es.at[:, pl.ds(0, ROWS)], local_sem.at[0]),
        pltpu.make_async_copy(h_in, hs.at[:, pl.ds(CB, ROWS)], local_sem.at[1]),
        pltpu.make_async_copy(c_in, cs, local_sem.at[2]),
    ]
    for copy in loads:
        copy.start()
    barrier = pltpu.get_barrier_semaphore()
    for device in neighbours():
        pl.semaphore_signal(barrier, inc=1, device_id=device, device_id_type=MESH)
    directions(omega, angles, kdir)

    def some_tables(low, high):
        def one(n, carry):
            tables(kdir, ta, tc, tb, tcf, n)
            return carry

        lax.fori_loop(low, high, one, 0)

    some_tables(0, CUT1)
    loads[0].wait()
    loads[1].wait()

    def exchange(number, halo):
        copies = []
        for n, device in enumerate(neighbours()):
            copy = pltpu.make_async_remote_copy(
                src_ref=pieces(sent.at[number], n),
                dst_ref=pieces(halo, n),
                send_sem=send_sem.at[number, n],
                recv_sem=recv_sem.at[number, n],
                device_id=device,
                device_id_type=MESH,
            )
            copy.start()
            copies.append(copy)
        return copies

    prepare(es, hs, sent.at[0])
    pl.semaphore_wait(barrier, 6)
    copies = exchange(0, halo1)
    some_tables(CUT1, CUT2)
    loads[2].wait()
    for copy in copies:
        copy.wait()
    place_halo(es, hs, halo1, ye, yh)
    advance(es, hs, cs, ye, yh)
    prepare(es, hs, sent.at[1])
    copies = exchange(1, halo2)
    stores = [
        pltpu.make_async_copy(es.at[:, pl.ds(0, ROWS)], e_out, local_sem.at[0]),
        pltpu.make_async_copy(hs.at[:, pl.ds(CB, ROWS)], h_out, local_sem.at[1]),
    ]
    for copy in stores:
        copy.start()
    some_tables(CUT2, QF // CHUNK)
    for n, (table, out) in enumerate(((ta, ta_out), (tc, tc_out), (tb, tb_out), (tcf, tcf_out))):
        copy = pltpu.make_async_copy(table, out, local_sem.at[2 + n])
        copy.start()
        stores.append(copy)
    for copy in copies + stores:
        copy.wait()


def patch(es, hs, cs, x0, y0):
    first = rows_of((PB, CZ)) == 0
    final = rows_of((PB, CZ)) == PB - 1

    def e_at(k, i, j):
        return es[k, pl.ds((x0 + i) * CB + y0 + j, PB)]

    def h_at(k, i, j):
        return hs[k, pl.ds((x0 + i + 1) * CB + y0 + j, PB)]

    def up(v, edge):
        return jnp.where(final, edge, pltpu.roll(v, PB - 1, 0))

    def down(v, edge):
        return jnp.where(first, edge, pltpu.roll(v, 1, 0))

    class Cell:
        pass

    def averages(name, o, e, c, u1, u0, wu, v1, v0, wv, pa, pb):
        vm = 0.5 * (v0 + v1)
        um = 0.5 * (u0 + u1)
        qu = 0.25 * wu
        qv = 0.25 * wv
        base_a = e - c * (vm + qv)
        base_b = e + c * (um - qu)
        setattr(o, name + pa + "1", base_a + c * u1)
        setattr(o, name + pa + "0", base_a + c * (u0 - 0.5 * wu))
        setattr(o, name + pb + "1", base_b - c * v1)
        setattr(o, name + pb + "0", base_b - c * (v0 + 0.5 * wv))
        setattr(o, name + "s" + pa + "0", e + c * (u0 - wu - vm - 0.5 * wv))
        setattr(o, name + "s" + pb + "0", e + c * (um - 0.5 * wu - v0 - wv))

    def stage_one(i):
        o = Cell()
        ex, ey, ez = [e_at(k, i, 0) for k in range(3)]
        exu, ezu = e_at(0, i, 1), e_at(2, i, 1)
        exd, eyd, ezd = [e_at(k, i, -1) for k in range(3)]
        exf, eyf, ezf = [e_at(k, i + 1, 0) for k in range(3)]
        eyb, ezb = e_at(1, i - 1, 0), e_at(2, i - 1, 0)
        exbu, exb = e_at(0, i - 1, 1), e_at(0, i - 1, 0)
        eyfd = e_at(1, i + 1, -1)
        hx, hy, hz = [h_at(k, i, 0) for k in range(3)]
        hxd, hzd = h_at(0, i, -1), h_at(2, i, -1)
        hyb, hzb = h_at(1, i - 1, 0), h_at(2, i - 1, 0)
        c = cs[pl.ds((x0 + i) * CB + y0, PB)]
        dyex, dyez = exu - ex, ezu - ez
        dxey, dxez = eyf - ey, ezf - ez
        dzex, dzey = z_next(ex) - ex, z_next(ey) - ey
        dyexb = exbu - exb
        dxeyd = eyfd - eyd
        szex, szey = z_prev(dzex), z_prev(dzey)
        averages(
            "x", o, ex, c,
            0.5 * dyex, hz - hzd - 0.5 * (ex - exd), 0.5 * (dxey - dxeyd),
            -0.5 * dzex, hy - z_prev(hy) + 0.5 * szex, 0.5 * (dxez - z_prev(dxez)),
            "y", "z",
        )
        averages(
            "y", o, ey, c,
            0.5 * dzey, hx - z_prev(hx) - 0.5 * szey, 0.5 * (dyez - z_prev(dyez)),
            -0.5 * dxey, hz - hzb + 0.5 * (ey - eyb), 0.5 * (dyex - dyexb),
            "z", "x",
        )
        dzexb = z_next(exb) - exb
        dzeyd = z_next(eyd) - eyd
        averages(
            "z", o, ez, c,
            0.5 * dxez, hy - hyb - 0.5 * (ez - ezb), 0.5 * (dzex - dzexb),
            -0.5 * dyez, hx - hxd + 0.5 * (ez - ezd), 0.5 * (dzey - dzeyd),
            "x", "y",
        )
        o.c = c
        o.h = (hx, hy, hz)
        o.d = (dyez, dzey, dzex, dxez, dxey, dyex)
        o.down = (exd, eyd, ezd, eyfd, hxd, hzd, dzeyd)
        o.up = (exu, ezu, e_at(1, i, 1))
        return o

    def ring_ahead(i):
        o = Cell()
        ey, ez = e_at(1, i, 0), e_at(2, i, 0)
        o.yx0 = o.ysx0 = ey
        o.zx0 = o.zsx0 = ez
        return o

    def ring_behind(o):
        ex, ey, ez = [e_at(k, -1, 0) for k in range(3)]
        h2zx = h_at(2, -1, 0) - 0.5 * (o.yx0 - ey) + 0.25 * (e_at(0, -1, 1) - ex)
        h2yx = h_at(1, -1, 0) - 0.25 * (z_next(ex) - ex) + 0.5 * (o.zx0 - ez)
        return h2zx, h2yx

    def stage_two(o, n, behind):
        hx, hy, hz = o.h
        dyez, dzey, dzex, dxez, dxey, dyex = o.d
        exd, eyd, ezd, eyfd, hxd, hzd, dzeyd = o.down
        exu, ezu, eyu = o.up
        h2zx_b, h2yx_b = behind
        xy0u = up(o.xy0, exu)
        zy0u = up(o.zy0, ezu)
        h2zy = hz - 0.25 * dxey + 0.5 * dyex - 0.25 * (n.ysx0 - o.ysx0) + 0.5 * (xy0u - o.xy1)
        h2zx = hz - 0.5 * dxey + 0.25 * dyex - 0.5 * (n.yx0 - o.yx1) + 0.25 * (up(o.xsy0, exu) - o.xsy0)
        h2xz = hx - 0.25 * dyez + 0.5 * dzey - 0.25 * (up(o.zsy0, ezu) - o.zsy0) + 0.5 * (z_next(o.yz0) - o.yz1)
        h2xy = hx - 0.5 * dyez + 0.25 * dzey - 0.5 * (zy0u - o.zy1) + 0.25 * (z_next(o.ysz0) - o.ysz0)
        h2yx = hy - 0.25 * dzex + 0.5 * dxez - 0.25 * (z_next(o.xsz0) - o.xsz0) + 0.5 * (n.zx0 - o.zx1)
        h2yz = hy - 0.5 * dzex + 0.25 * dxez - 0.5 * (z_next(o.xz0) - o.xz1) + 0.25 * (n.zsx0 - o.zsx0)
        h2zy_d = down(h2zy, hzd - 0.25 * (eyfd - eyd) + 0.5 * (o.xy0 - exd))
        h2xy_d = down(h2xy, hxd - 0.5 * (o.zy0 - ezd) + 0.25 * dzeyd)
        half = 0.5 * o.c
        ex = 0.5 * (o.xy0 + o.xy1) + half * (h2zy - h2zy_d - h2yz + z_prev(h2yz))
        ey = 0.5 * (o.yz0 + o.yz1) + half * (h2xz - z_prev(h2xz) - h2zx + h2zx_b)
        ez = 0.5 * (o.zx0 + o.zx1) + half * (h2yx - h2yx_b - h2xy + h2xy_d)
        hx = hx - 0.25 * (dyez - dzey + zy0u - o.zy0 - z_next(o.yz0) + o.yz0)
        hy = hy - 0.25 * (dzex - dxez + z_next(o.xz0) - o.xz0 - n.zx0 + o.zx0)
        hz = hz - 0.25 * (dxey - dyex + n.yx0 - o.yx0 - xy0u + o.xy0)
        return (ex, ey, ez), (hx, hy, hz), (h2zx, h2yx)

    now = stage_one(0)
    behind = ring_behind(now)
    for i in range(PB):
        later = stage_one(i + 1) if i < PB - 1 else ring_ahead(i + 1)
        e_new, h_new, behind = stage_two(now, later, behind)
        pending = (i, e_new, h_new)
        if i > 0:
            write(es, hs, x0, y0, previous)
        previous = pending
        now = later
    write(es, hs, x0, y0, previous)


def write(es, hs, x0, y0, item):
    i, e_new, h_new = item
    for k in range(3):
        es[k, pl.ds((x0 + i) * CB + y0, PB)] = e_new[k]
        hs[k, pl.ds((x0 + i + 1) * CB + y0, PB)] = h_new[k]


def second_kernel(owner, corner, spots, place, halo, e_in, h_in, c_in, e_out, h_out, sampled, es, hs, cs, ye, yh, taken, slot_x, slot_y, count, sem):
    loads = [
        pltpu.make_async_copy(e_in, es.at[:, pl.ds(0, ROWS)], sem.at[0]),
        pltpu.make_async_copy(h_in, hs.at[:, pl.ds(CB, ROWS)], sem.at[1]),
        pltpu.make_async_copy(c_in, cs, sem.at[2]),
    ]
    for copy in loads:
        copy.start()
    me = lax.axis_index("gx") * GY + lax.axis_index("gy")

    def look(n, found):
        slot_x[found] = corner[2 * n]
        slot_y[found] = corner[2 * n + 1]
        return jnp.minimum(found + (owner[n] == me).astype(jnp.int32), SLOTS)

    count[0] = lax.fori_loop(0, GX * GY, look, 0, unroll=8)
    for copy in loads:
        copy.wait()
    lane = lanes_of((1, CZ))

    def patches():
        def one(n, carry):
            patch(es, hs, cs, slot_x[n], slot_y[n])
            return carry

        lax.fori_loop(0, count[0], one, 0)

    def sample():
        e_rows = es.reshape(3 * (ROWS + CB), CZ)
        h_rows = hs.reshape(3 * (ROWS + CB), CZ)

        def one(n, carry):
            mask = lane == spots[n]
            k1, k2 = spots[SPB + n], spots[2 * SPB + n]
            taken[pl.ds(n, 1)] = jnp.where(mask, h_rows[pl.ds(k1 + CB, 1)], 0.0)
            taken[pl.ds(n + SPB, 1)] = jnp.where(mask, h_rows[pl.ds(k2 + CB, 1)], 0.0)
            taken[pl.ds(n + 2 * SPB, 1)] = jnp.where(mask, e_rows[pl.ds(k1, 1)], 0.0)
            taken[pl.ds(n + 3 * SPB, 1)] = jnp.where(mask, e_rows[pl.ds(k2, 1)], 0.0)
            return carry

        lax.fori_loop(0, SPB, one, 0, unroll=16)
        high, low = split(taken[...])
        ones = jnp.ones((16, CZ), BF16)
        return dot_t(ones, high) + dot_t(ones, low)

    slots = place[0:1]
    face = place[1:2]
    sign = jnp.where(slots >= 0, (2 * (face % 2) - 1).astype(F32), 0.0)
    for moment in range(2):
        if moment:
            place_halo(es, hs, halo, ye, yh)
            advance(es, hs, cs, ye, yh)
        patches()
        if moment:
            stores = [
                pltpu.make_async_copy(es.at[:, pl.ds(0, ROWS)], e_out, sem.at[0]),
                pltpu.make_async_copy(hs.at[:, pl.ds(CB, ROWS)], h_out, sem.at[1]),
            ]
            for copy in stores:
                copy.start()
        got = sample()
        got = [got[0:1, j * SPB : (j + 1) * SPB] for j in range(4)]
        sampled[4 * moment : 4 * moment + 1] = -sign * got[1]
        sampled[4 * moment + 1 : 4 * moment + 2] = sign * got[0]
        sampled[4 * moment + 2 : 4 * moment + 3] = sign * got[3]
        sampled[4 * moment + 3 : 4 * moment + 4] = -sign * got[2]
    cell = jnp.maximum(slots, 0)
    sampled[8:9] = (cell // (CB * CZ)).astype(F32)
    sampled[9:10] = (cell // CZ % CB).astype(F32)
    sampled[10:11] = (cell % CZ).astype(F32)
    sampled[11:12] = jnp.where(slots >= 0, face, 6).astype(F32)
    sampled[12:16] = jnp.zeros((4, SPB), F32)
    for copy in stores:
        copy.wait()


def third_kernel(omega, sampled, ta_in, tc_in, tb_in, tcf_in, far, got, gathered, ta, tc, tb, tcf, hot, hotz, spread_hi, spread_lo, lhs1, lhs2, lhsz, acc, rows48, send_buf, recv_buf, load_sem, send1, recv1, send2, recv2):
    gx = lax.axis_index("gx")
    gy = lax.axis_index("gy")
    loads = [
        pltpu.make_async_copy(ta_in, ta, load_sem.at[0]),
        pltpu.make_async_copy(tc_in, tc.at[:, pl.ds(0, 2 * ZF)], load_sem.at[1]),
        pltpu.make_async_copy(tc_in.at[:, pl.ds(0, ZF)], tc.at[:, pl.ds(2 * ZF, ZF)], load_sem.at[2]),
        pltpu.make_async_copy(tb_in, tb, load_sem.at[3]),
        pltpu.make_async_copy(tcf_in, tcf, load_sem.at[4]),
    ]
    for copy in loads:
        copy.start()
    barrier = pltpu.get_barrier_semaphore()
    for d in range(1, GX):
        pl.semaphore_signal(barrier, inc=1, device_id=(lax.rem(gx + d, GX), gy), device_id_type=MESH)
    for d in range(1, GY):
        pl.semaphore_signal(barrier, inc=1, device_id=(gx, lax.rem(gy + d, GY)), device_id_type=MESH)
    tc[:, 3 * ZF : 4 * ZF] = jnp.zeros((2, ZF, QF), BF16)
    pl.semaphore_wait(barrier, GX + GY - 2)
    first = []
    for d in range(1, GX):
        copy = pltpu.make_async_remote_copy(
            src_ref=sampled,
            dst_ref=gathered.at[GX - d],
            send_sem=send1.at[d],
            recv_sem=recv1.at[GX - d],
            device_id=(lax.rem(gx + d, GX), gy),
            device_id_type=MESH,
        )
        copy.start()
        first.append(copy)
    gathered[0] = sampled[...]
    for copy in first:
        copy.wait()

    for b in range(GX):
        lanes = slice(b * SPB, (b + 1) * SPB)
        got[0:16, lanes] = gathered[b]
        block = lax.rem(gx + b, GX)
        x = gathered[b, 8:9] + (block * CB).astype(F32)
        z = gathered[b, 10:11]
        got[12:13, lanes] = jnp.where(x < 128.0, 127.0 - x, x - 128.0)
        got[13:14, lanes] = jnp.where(x < 128.0, -1.0, 1.0)
        got[14:15, lanes] = jnp.where(z < 64.0, 63.0 - z, z - 64.0)
        got[15:16, lanes] = jnp.where(z < 64.0, -1.0, 1.0)

    def one_hot(to, place_row, sign_row, count, blocks):
        for b, start in enumerate(blocks):
            lanes = pl.ds(start, SPB)
            there = slice(b * SPB, (b + 1) * SPB)
            where_at = jnp.broadcast_to(got[place_row : place_row + 1, lanes], (16, SPB))
            sign = jnp.broadcast_to(got[sign_row : sign_row + 1, lanes], (16, SPB))
            at = rows_of((16, SPB)).astype(F32)
            for j in range(0, count, 16):
                same = at + float(j) == where_at
                to[j : j + 16, there] = jnp.where(same, 1.0, 0.0).astype(BF16)
                to[count + j : count + j + 16, there] = jnp.where(same, sign, 0.0).astype(BF16)

    def halves(v):
        high = v.astype(BF16).astype(F32)
        return high, v - high

    def spread(v, key, start, step, first_row, there, count):
        high, low = halves(v)

        def one(n, carry):
            same = key == (start + step * n).astype(F32)
            at = pl.ds(pl.multiple_of(first_row + n * 16, 16), 16)
            spread_hi[at, there] = jnp.where(same, high, 0.0).astype(BF16)
            spread_lo[at, there] = jnp.where(same, low, 0.0).astype(BF16)
            return carry

        lax.fori_loop(0, count, one, 0, unroll=8)

    def row16(row, lanes):
        return jnp.broadcast_to(got[row : row + 1, lanes], (16, SPB))

    upper = rows_of((16, SPB)) // 8
    every = [b * SPB for b in range(GX)]
    ends = [pl.multiple_of(lax.rem(GX - gx, GX) * SPB, SPB), pl.multiple_of((GX - 1 - gx) * SPB, SPB)]

    def twice(lanes):
        v = got[0:8, lanes]
        return jnp.concatenate([v, v], axis=0)

    def spread_z(y_low, count):
        wanted = (4 + upper).astype(F32)
        for b in range(GX):
            lanes = slice(b * SPB, (b + 1) * SPB)
            v = jnp.where(row16(11, lanes) == wanted, twice(lanes), 0.0)
            spread(v, row16(9, lanes), y_low, 1, 0, lanes, count)

    def spread_x(y_low, count):
        for e, start in enumerate(ends):
            lanes = pl.ds(start, SPB)
            wanted = jnp.where(upper == e, float(e), -1.0)
            v = jnp.where(row16(11, lanes) == wanted, twice(lanes), 0.0)
            spread(v, row16(9, lanes), y_low, 1, 0, slice(e * SPB, (e + 1) * SPB), count)

    def spread_y():
        for b in range(GX):
            lanes = slice(b * SPB, (b + 1) * SPB)
            face = row16(11, lanes)
            v = jnp.where((face == 2.0) | (face == 3.0), twice(lanes), 0.0)
            spread(v, row16(10, lanes) - upper.astype(F32), 16, 2, 0, lanes, YF_ROWS // 2)

    def dense(to, rows):
        for m in range(0, rows, CHUNK):
            d = dot_t(spread_hi[m : m + CHUNK], hot[...]) + dot_t(spread_lo[m : m + CHUNK], hot[...])
            for k in range(2):
                high, low = split(d[:, k * XF : (k + 1) * XF])
                lhs1[k, to + m : to + m + CHUNK, 0:XF] = high
                lhs1[k, to + m : to + m + CHUNK, XF : 2 * XF] = high
                lhs2[k, to + m : to + m + CHUNK] = low

    def dense_x(rows):
        for m in range(0, rows, CHUNK):
            at = slice(m, m + CHUNK)
            d = dot_t(spread_hi[at, 0 : 2 * SPB], hotz[...]) + dot_t(spread_lo[at, 0 : 2 * SPB], hotz[...])
            for k in range(2):
                high, low = split(d[:, k * ZF : (k + 1) * ZF])
                lhsz[k, at] = jnp.concatenate([high, high, low, jnp.zeros_like(low)], axis=1)

    def times_x(to, lanes):
        out = []
        for k in range(2):
            table = ta[k, :, lanes]
            out.append(dot(lhs1[k, to : to + CHUNK], table) + dot(lhs2[k, to : to + CHUNK], table[0:XF]))
        return out

    def times_z(to, lanes):
        return [dot(lhsz[k, to : to + CHUNK], tc[k, :, lanes]) for k in range(2)]

    def outer_y(g, total, y_low, lanes):
        re, im = total
        for y in range(16):
            at = slice(y * 16, (y + 1) * 16)
            bc, bs = tb[0, pl.ds(y_low + y, 1), lanes], tb[1, pl.ds(y_low + y, 1), lanes]
            re = re + (bc * g[0][at] - bs * g[1][at])
            im = im + (bc * g[1][at] + bs * g[0][at])
        return re, im

    def outer_z(g, total, z_low, lanes):
        re, im = total
        for o in range(CHUNK // 8):
            z = z_low + o
            j, sign = (z - 64, 1.0) if z >= 64 else (63 - z, -1.0)
            at = slice(o * 8, (o + 1) * 8)
            cc, cs = tcf[0, j : j + 1, lanes], sign * tcf[1, j : j + 1, lanes]
            re = re + (cc * g[0][at] - cs * g[1][at])
            im = im + (cc * g[1][at] + cs * g[0][at])
        return re, im

    def keep(base, total, lanes):
        n = total[0].shape[0]
        acc[base, 0, 0:n, lanes] = total[0]
        acc[base, 1, 0:n, lanes] = total[1]

    edge = (gy == 0) | (gy == GY - 1)
    zero16 = jnp.zeros((16, CHUNK), F32)
    zero8 = jnp.zeros((8, CHUNK), F32)
    one_hot(hot, 12, 13, XF, every)
    one_hot(hotz, 14, 15, ZF, ends)
    for copy in loads:
        copy.wait()

    @pl.when(jnp.logical_not(edge))
    def _():
        spread_z(0, CB)
        dense(0, CB * 16)
        spread_x(0, CB)
        dense_x(CB * 16)
        acc[2] = jnp.zeros((2, 16, QF), F32)

        def chunk(n, carry):
            lanes = pl.ds(pl.multiple_of(n * CHUNK, CHUNK), CHUNK)
            total = (zero16, zero16)
            for y in range(2):
                total = outer_y(times_x(y * CHUNK, lanes), total, y * 16, lanes)
            keep(0, total, lanes)
            total = (zero16, zero16)
            for y in range(2):
                total = outer_y(times_z(y * CHUNK, lanes), total, y * 16, lanes)
            keep(1, total, lanes)
            return carry

        lax.fori_loop(0, QF // CHUNK, chunk, 0)

    @pl.when(edge)
    def _():
        y_low = jnp.where(gy == 0, 16, 0)
        spread_z(y_low, 16)
        dense(0, CHUNK)
        spread_x(y_low, 16)
        dense_x(CHUNK)
        spread_y()
        dense(CHUNK, YF_ROWS * 8)

        def chunk(n, carry):
            lanes = pl.ds(pl.multiple_of(n * CHUNK, CHUNK), CHUNK)
            keep(0, outer_y(times_x(0, lanes), (zero16, zero16), y_low, lanes), lanes)
            keep(1, outer_y(times_z(0, lanes), (zero16, zero16), y_low, lanes), lanes)
            total = (zero8, zero8)
            for z in range(0, YF_ROWS, CHUNK // 8):
                total = outer_z(times_x(CHUNK + z * 8, lanes), total, z + 16, lanes)
            keep(2, total, lanes)
            return carry

        lax.fori_loop(0, QF // CHUNK, chunk, 0)

    scale = 1.0 / math.sqrt(GX * GY * SPB)
    y_face = jnp.where(gy == 0, 16, 15)
    moment = 1.0 + (rows_of((8, 1)) // 4).astype(F32)
    for f in range(FREQ):
        lanes = slice(f * QN, (f + 1) * QN)
        mc, ms = turn(omega[f] * (1.0 / (2.0 * math.pi)) * moment)
        mc, ms = mc * scale, ms * scale

        def both(base, c, s):
            low_re, high_re = acc[base, 0, 0:8, lanes], acc[base, 0, 8:16, lanes]
            low_im, high_im = acc[base, 1, 0:8, lanes], acc[base, 1, 8:16, lanes]
            re = c * (low_re + high_re) + s * (low_im - high_im)
            im = c * (low_im + high_im) + s * (high_re - low_re)
            return re, im

        def late(re, im):
            a, b = mc * re + ms * im, mc * im - ms * re
            return a[0:4] + a[4:8], b[0:4] + b[4:8]

        zf = late(*both(0, tcf[0, Z_FACE : Z_FACE + 1, lanes], tcf[1, Z_FACE : Z_FACE + 1, lanes]))
        xf = late(*both(1, tb[0, CB : CB + 1, lanes], tb[1, CB : CB + 1, lanes]))
        c, s = tb[0, pl.ds(y_face, 1), lanes], tb[1, pl.ds(y_face, 1), lanes]
        re, im = acc[2, 0, 0:8, lanes], acc[2, 1, 0:8, lanes]
        yf = late(c * re - s * im, c * im + s * re)
        for k in range(2):
            z4, x4, y4 = zf[k], xf[k], yf[k]
            six = [
                z4[0:1] + y4[1:2], z4[1:2] + x4[0:1], x4[1:2] + y4[0:1],
                z4[2:3] + y4[3:4], z4[3:4] + x4[2:3], x4[3:4] + y4[2:3],
            ]
            for j, v in enumerate(six):
                rows48[12 * f + 6 * k + j : 12 * f + 6 * k + j + 1] = v
    rows48[48:128] = jnp.zeros((80, QN), F32)
    for t in range(0, QN, 128):
        send_buf[t : t + 128] = jnp.transpose(rows48[:, t : t + 128])

    second = []
    for d in range(1, GY):
        to = lax.rem(gy + d, GY)
        copy = pltpu.make_async_remote_copy(
            src_ref=send_buf.at[pl.ds(pl.multiple_of(to * OWN, OWN), OWN)],
            dst_ref=recv_buf.at[GY - d],
            send_sem=send2.at[d],
            recv_sem=recv2.at[GY - d],
            device_id=(gx, to),
            device_id_type=MESH,
        )
        copy.start()
        second.append(copy)
    total = send_buf[pl.ds(pl.multiple_of(gy * OWN, OWN), OWN)]
    for copy in second:
        copy.wait()
    for d in range(1, GY):
        total = total + recv_buf[d]
    far[...] = total[:, 0:48]


VMEM = pl.BlockSpec(memory_space=pltpu.VMEM)
SMEM = pl.BlockSpec(memory_space=pltpu.SMEM)
ANY = pl.BlockSpec(memory_space=pl.ANY)


def local(efield, hfield, e_coef, omega, patch_owner, patch_corner, surface_points, surface_faces, angle_index):
    field = jax.ShapeDtypeStruct((3, ROWS, CZ), F32)
    fields = [
        pltpu.VMEM((3, ROWS + CB, CZ), F32),
        pltpu.VMEM((3, ROWS + CB, CZ), F32),
        pltpu.VMEM((ROWS, CZ), F32),
        pltpu.VMEM((2, CB, CZ), F32),
        pltpu.VMEM((2, CB, CZ), F32),
    ]
    coef = e_coef.reshape(ROWS, CZ)
    mine = lax.dynamic_slice(angle_index, (lax.axis_index("gx") * QN, 0), (QN, 2)).T
    efield, hfield, halo, *tabled = pl.pallas_call(
        first_kernel,
        out_shape=(
            field,
            field,
            jax.ShapeDtypeStruct((9, CB, CZ), F32),
            jax.ShapeDtypeStruct((2, 2 * XF, QF), BF16),
            jax.ShapeDtypeStruct((2, 2 * ZF, QF), BF16),
            jax.ShapeDtypeStruct((2, CB + 8, QF), F32),
            jax.ShapeDtypeStruct((2, ZF, QF), F32),
        ),
        in_specs=[SMEM, VMEM, ANY, ANY, ANY],
        out_specs=(ANY, ANY, VMEM, ANY, ANY, ANY, ANY),
        scratch_shapes=[
            pltpu.VMEM((8, QF), F32),
            pltpu.VMEM((2, 2 * XF, QF), BF16),
            pltpu.VMEM((2, 2 * ZF, QF), BF16),
            pltpu.VMEM((2, CB + 8, QF), F32),
            pltpu.VMEM((2, ZF, QF), F32),
        ]
        + fields
        + [
            pltpu.VMEM((2, 9, CB, CZ), F32),
            pltpu.VMEM((9, CB, CZ), F32),
            pltpu.SemaphoreType.DMA((6,)),
            pltpu.SemaphoreType.DMA((2, 6)),
            pltpu.SemaphoreType.DMA((2, 6)),
        ],
        compiler_params=pltpu.CompilerParams(collective_id=0, has_side_effects=True, vmem_limit_bytes=56 * 2**20),
        name="first_step",
    )(omega, mine, efield.reshape(3, ROWS, CZ), hfield.reshape(3, ROWS, CZ), coef)
    points = surface_points.reshape(SPB)
    faces = surface_faces.reshape(SPB)
    place = jnp.stack([points, faces])
    cell = jnp.maximum(points, 0)
    normal = faces // 2
    span = ROWS + CB
    first_row = jnp.where(normal == 2, 0, normal + 1) * span + cell // CZ
    second_row = jnp.where(normal == 0, 2, normal - 1) * span + cell // CZ
    spots = jnp.concatenate([cell % CZ, first_row, second_row])
    efield, hfield, sampled = pl.pallas_call(
        second_kernel,
        out_shape=(field, field, jax.ShapeDtypeStruct((16, SPB), F32)),
        in_specs=[SMEM, SMEM, SMEM, VMEM, VMEM, ANY, ANY, ANY],
        out_specs=(ANY, ANY, VMEM),
        scratch_shapes=fields
        + [
            pltpu.VMEM((4 * SPB, CZ), F32),
            pltpu.SMEM((SLOTS + 1,), jnp.int32),
            pltpu.SMEM((SLOTS + 1,), jnp.int32),
            pltpu.SMEM((1,), jnp.int32),
            pltpu.SemaphoreType.DMA((3,)),
        ],
        compiler_params=pltpu.CompilerParams(vmem_limit_bytes=56 * 2**20),
        name="patches",
    )(patch_owner, patch_corner.reshape(-1), spots, place, halo, efield, hfield, coef)
    far = pl.pallas_call(
        third_kernel,
        out_shape=jax.ShapeDtypeStruct((OWN, 48), F32),
        in_specs=[SMEM, VMEM, ANY, ANY, ANY, ANY],
        out_specs=VMEM,
        scratch_shapes=[
            pltpu.VMEM((16, GX * SPB), F32),
            pltpu.VMEM((GX, 16, SPB), F32),
            pltpu.VMEM((2, 2 * XF, QF), BF16),
            pltpu.VMEM((2, 4 * ZF, QF), BF16),
            pltpu.VMEM((2, CB + 8, QF), F32),
            pltpu.VMEM((2, ZF, QF), F32),
            pltpu.VMEM((2 * XF, GX * SPB), BF16),
            pltpu.VMEM((2 * ZF, 2 * SPB), BF16),
            pltpu.VMEM((YF_ROWS * 8, GX * SPB), BF16),
            pltpu.VMEM((YF_ROWS * 8, GX * SPB), BF16),
            pltpu.VMEM((2, YF_ROWS * 8 + CHUNK, 2 * XF), BF16),
            pltpu.VMEM((2, YF_ROWS * 8 + CHUNK, XF), BF16),
            pltpu.VMEM((2, CB * 16, 4 * ZF), BF16),
            pltpu.VMEM((3, 2, 16, QF), F32),
            pltpu.VMEM((128, QN), F32),
            pltpu.VMEM((QN, 128), F32),
            pltpu.VMEM((GY, OWN, 128), F32),
            pltpu.SemaphoreType.DMA((5,)),
            pltpu.SemaphoreType.DMA((GX,)),
            pltpu.SemaphoreType.DMA((GX,)),
            pltpu.SemaphoreType.DMA((GY,)),
            pltpu.SemaphoreType.DMA((GY,)),
        ],
        compiler_params=pltpu.CompilerParams(collective_id=1, has_side_effects=True, vmem_limit_bytes=56 * 2**20),
        name="projection",
    )(omega, sampled, *tabled)
    shape = (3, CB, CB, CZ)
    return efield.reshape(shape), hfield.reshape(shape), far


def solution(mesh):
    placed = (
        P(None, "gx", "gy", None),
        P(None, "gx", "gy", None),
        P("gx", "gy", None),
        P(),
        P(),
        P(),
        P("gx", "gy", None),
        P("gx", "gy", None),
        P(),
    )
    return jax.shard_map(
        local,
        mesh=mesh,
        in_specs=placed,
        out_specs=(P(None, "gx", "gy", None), P(None, "gx", "gy", None), P(("gx", "gy"), None)),
        check_vma=False,
    )
```

```python
import math

import jax
import jax.numpy as jnp
import numpy as np
from jax import lax
from jax.experimental import pallas as pl
from jax.experimental.pallas import tpu as pltpu
from jax.sharding import PartitionSpec as P

PB = 8
SLOTS = 4
NTH = 128
NPH = 256
CB = 32
CZ = 128
ROWS = CB * CB
SPB = 256
FREQ = 4
GX = 8
GY = 16
ANG = 4096
QN = ANG // GX
QF = QN * FREQ
OWN = ANG // (GX * GY)
MESH = pl.DeviceIdType.MESH
F32 = jnp.float32
BF16 = jnp.bfloat16


def lanes_of(shape):
    return lax.broadcasted_iota(jnp.int32, shape, 1)


def rows_of(shape):
    return lax.broadcasted_iota(jnp.int32, shape, 0)


def z_next(v):
    return jnp.where(lanes_of(v.shape) == CZ - 1, 0.0, pltpu.roll(v, CZ - 1, 1))


def z_prev(v):
    return jnp.where(lanes_of(v.shape) == 0, 0.0, pltpu.roll(v, 1, 1))


def y_next(v, edge):
    n = v.shape[0]
    return jnp.where(rows_of(v.shape) == n - 1, edge, pltpu.roll(v, n - 1, 0))


def y_prev(v, edge):
    return jnp.where(rows_of(v.shape) == 0, edge, pltpu.roll(v, 1, 0))


def prepare(es, hs, out):
    out[0] = es[1, 0:CB]
    out[1] = es[2, 0:CB]
    last = (CB - 1) * CB
    ex, ey, ez = [es[k, last : last + CB] for k in range(3)]
    hy, hz = [hs[k, last + CB : last + 2 * CB] for k in (1, 2)]
    out[2] = hy - 0.5 * (z_next(ex) - ex + ez)
    out[3] = hz + 0.5 * (ey + y_next(ex, 0.0) - ex)
    out[8, 8:16] = ey[CB - 8 : CB] * 0.0 + es[1, CB - 1 : CB]
    out[8, 0:8] = ex[0:1] + jnp.zeros((8, CZ), F32)
    out[8, 16:32] = jnp.zeros((16, CZ), F32)
    out[4] = es[0, pl.ds(0, CB, stride=CB)]
    out[5] = es[2, pl.ds(0, CB, stride=CB)]
    ex, ey, ez = [es[k, pl.ds(CB - 1, CB, stride=CB)] for k in range(3)]
    hx, hz = [hs[k, pl.ds(2 * CB - 1, CB, stride=CB)] for k in (0, 2)]
    out[6] = hx + 0.5 * (ez + z_next(ey) - ey)
    out[7] = hz - 0.5 * (y_next(ey, 0.0) - ey + ex)


def place_halo(es, hs, halo, ye, yh):
    gx = lax.axis_index("gx")
    gy = lax.axis_index("gy")
    x_low = (gx > 0).astype(F32)
    x_high = (gx < GX - 1).astype(F32)
    y_low = (gy > 0).astype(F32)
    y_high = (gy < GY - 1).astype(F32)
    last_row = rows_of((CB, CZ)) == CB - 1
    es[1, ROWS : ROWS + CB] = halo[0] * x_high
    es[2, ROWS : ROWS + CB] = halo[1] * x_high
    ye[0] = halo[4] * y_high
    ye[1] = halo[5] * y_high
    corner = jnp.where(last_row, halo[8, 0:1] * (0.5 * y_high), 0.0)
    hs[1, 0:CB] = x_low * (halo[2] + 0.5 * es[2, 0:CB])
    hs[2, 0:CB] = x_low * (halo[3] - 0.5 * es[1, 0:CB] + corner)
    corner = jnp.where(last_row, halo[8, 8:9] * (0.5 * x_high), 0.0)
    yh[0] = y_low * (halo[6] - 0.5 * es[2, pl.ds(0, CB, stride=CB)])
    yh[1] = y_low * (halo[7] + 0.5 * es[0, pl.ds(0, CB, stride=CB)] - corner)


def advance(es, hs, cs, ye, yh):
    last = rows_of((CB, CZ)) == CB - 1
    for x in range(CB):
        r = x * CB
        here, after = slice(r, r + CB), slice(r + CB, r + 2 * CB)
        ex, ey, ez = [es[k, here] for k in range(3)]
        ey1, ez1 = es[1, after], es[2, after]
        hx, hy, hz = [hs[k, after] for k in range(3)]
        if x == 0:
            hy0, hz0 = hs[1, here], hs[2, here]
        exu = jnp.where(last, ye[0, x : x + 1], es[0, r + 1 : r + CB + 1])
        ezu = jnp.where(last, ye[1, x : x + 1], es[2, r + 1 : r + CB + 1])
        hx = hx - 0.5 * (ezu - ez - z_next(ey) + ey)
        hy = hy - 0.5 * (z_next(ex) - ex - ez1 + ez)
        hz = hz - 0.5 * (ey1 - ey - exu + ex)
        for k, v in enumerate((hx, hy, hz)):
            hs[k, after] = v
        c = cs[here]
        ex = ex + c * (hz - y_prev(hz, yh[1, x : x + 1]) - hy + z_prev(hy))
        ey = ey + c * (hx - z_prev(hx) - hz + hz0)
        ez = ez + c * (hy - hy0 - hx + y_prev(hx, yh[0, x : x + 1]))
        for k, v in enumerate((ex, ey, ez)):
            es[k, here] = v
        hy0, hz0 = hy, hz


def neighbours():
    gx = lax.axis_index("gx")
    gy = lax.axis_index("gy")
    xn, xp = lax.rem(gx + 1, GX), lax.rem(gx + GX - 1, GX)
    yn, yp = lax.rem(gy + 1, GY), lax.rem(gy + GY - 1, GY)
    return [(xp, gy), (xn, gy), (gx, yp), (gx, yn), (xn, yp), (xp, yn)]


def pieces(ref, n):
    if n < 4:
        return ref.at[pl.ds(2 * n, 2)]
    return ref.at[8, pl.ds(8 * (n - 4), 8)]


def fitted(function, degrees, points=4001):
    r = np.cos(np.linspace(0.0, np.pi, points)) * 0.5
    basis = np.stack([r**d for d in degrees], axis=1)
    return [float(v) for v in np.linalg.lstsq(basis, function(np.pi * r) * math.sqrt(2.0), rcond=None)[0]]


SIN = fitted(np.sin, (1, 3, 5, 7, 9))
COS = fitted(np.cos, (0, 2, 4, 6, 8))


def turn(t):
    r = t - jnp.round(t)
    r2 = r * r
    s = r * (SIN[0] + r2 * (SIN[1] + r2 * (SIN[2] + r2 * (SIN[3] + r2 * SIN[4]))))
    c = COS[0] + r2 * (COS[1] + r2 * (COS[2] + r2 * (COS[3] + r2 * COS[4])))
    return 1.0 - s * s, s * c


def split(v):
    high = v.astype(BF16)
    return high, (v - high.astype(F32)).astype(BF16)


def dot(a, b):
    return jnp.dot(a, b, preferred_element_type=F32)


def dot_t(a, b):
    return lax.dot_general(a, b, (((1,), (1,)), ((), ())), preferred_element_type=F32)


CUT1 = 2
CUT2 = 5
XF = 128
ZF = 64
YF_ROWS = 96
CHUNK = 256
X_FACE = 111
Z_FACE = 47


def directions(omega, angles, kdir):
    index = angles[:, pl.ds(pl.multiple_of(lax.axis_index("gx") * QN, QN), QN)].astype(F32)
    theta = math.pi * (index[0:1] + 0.5) / NTH
    phi = 2.0 * math.pi * (index[1:2] + 0.5) / NPH
    st, ct = jnp.sin(theta), jnp.cos(theta)
    sp, cp = jnp.sin(phi), jnp.cos(phi)
    for f in range(FREQ):
        w = omega[f] * (1.0 / (2.0 * math.pi))
        lanes = slice(f * QN, (f + 1) * QN)
        kdir[0:1, lanes] = st * cp * w
        kdir[1:2, lanes] = st * sp * w
        kdir[2:3, lanes] = ct * w


def tables(kdir, ta, tc, tb, tcf, n):
    y_start = (lax.axis_index("gy") * CB).astype(F32) + (0.5 - CB * GY / 2.0)
    lanes = pl.ds(pl.multiple_of(n * CHUNK, CHUNK), CHUNK)
    kx, ky, kz = kdir[0:1, lanes], kdir[1:2, lanes], kdir[2:3, lanes]
    count = rows_of((16, CHUNK)).astype(F32)
    for j in range(0, XF, 16):
        for k, v in enumerate(turn((count + (j + 0.5)) * kx)):
            high, low = split(v)
            ta[k, j : j + 16, lanes] = high
            ta[k, XF + j : XF + j + 16, lanes] = low
    for j in range(0, ZF, 16):
        for k, v in enumerate(turn((count + (j + 0.5)) * kz)):
            high, low = split(v)
            tc[k, j : j + 16, lanes] = high
            tc[k, ZF + j : ZF + j + 16, lanes] = low
            tcf[k, j : j + 16, lanes] = v
    for j in range(0, CB, 16):
        for k, v in enumerate(turn((count + (y_start + j)) * ky)):
            tb[k, j : j + 16, lanes] = v
    for k, v in enumerate(turn(jnp.full((8, CHUNK), X_FACE + 0.5, F32) * kx)):
        tb[k, CB : CB + 8, lanes] = v


def first_kernel(omega, angles, points, faces, e_in, h_in, c_in, e_out, h_out, halo2, ta_out, tc_out, tb_out, tcf_out, spots, kdir, ta, tc, tb, tcf, es, hs, cs, ye, yh, sent, halo1, local_sem, send_sem, recv_sem):
    loads = [
        pltpu.make_async_copy(e_in, es.at[:, pl.ds(0, ROWS)], local_sem.at[0]),
        pltpu.make_async_copy(h_in, hs.at[:, pl.ds(CB, ROWS)], local_sem.at[1]),
        pltpu.make_async_copy(c_in, cs, local_sem.at[2]),
    ]
    for copy in loads:
        copy.start()
    barrier = pltpu.get_barrier_semaphore()
    for device in neighbours():
        pl.semaphore_signal(barrier, inc=1, device_id=device, device_id_type=MESH)
    directions(omega, angles, kdir)
    cell = jnp.maximum(points[...], 0)
    normal = lax.shift_right_logical(faces[...], 1)
    row = lax.shift_right_logical(cell, 7)
    spots[0:1] = cell & (CZ - 1)
    spots[1:2] = jnp.where(normal == 2, 0, normal + 1) * (ROWS + CB) + row
    spots[2:3] = jnp.where(normal == 0, 2, normal - 1) * (ROWS + CB) + row
    spots[3:8] = jnp.zeros((5, SPB), jnp.int32)

    def some_tables(low, high):
        def one(n, carry):
            tables(kdir, ta, tc, tb, tcf, n)
            return carry

        lax.fori_loop(low, high, one, 0)

    some_tables(0, CUT1)
    loads[0].wait()
    loads[1].wait()

    def exchange(number, halo):
        copies = []
        for n, device in enumerate(neighbours()):
            copy = pltpu.make_async_remote_copy(
                src_ref=pieces(sent.at[number], n),
                dst_ref=pieces(halo, n),
                send_sem=send_sem.at[number, n],
                recv_sem=recv_sem.at[number, n],
                device_id=device,
                device_id_type=MESH,
            )
            copy.start()
            copies.append(copy)
        return copies

    prepare(es, hs, sent.at[0])
    pl.semaphore_wait(barrier, 6)
    copies = exchange(0, halo1)
    some_tables(CUT1, CUT2)
    loads[2].wait()
    for copy in copies:
        copy.wait()
    place_halo(es, hs, halo1, ye, yh)
    advance(es, hs, cs, ye, yh)
    prepare(es, hs, sent.at[1])
    copies = exchange(1, halo2)
    stores = [
        pltpu.make_async_copy(es.at[:, pl.ds(0, ROWS)], e_out, local_sem.at[0]),
        pltpu.make_async_copy(hs.at[:, pl.ds(CB, ROWS)], h_out, local_sem.at[1]),
    ]
    for copy in stores:
        copy.start()
    some_tables(CUT2, QF // CHUNK)
    for n, (table, out) in enumerate(((ta, ta_out), (tc, tc_out), (tb, tb_out), (tcf, tcf_out))):
        copy = pltpu.make_async_copy(table, out, local_sem.at[2 + n])
        copy.start()
        stores.append(copy)
    for copy in copies + stores:
        copy.wait()


def patch(es, hs, cs, x0, y0):
    first = rows_of((PB, CZ)) == 0
    final = rows_of((PB, CZ)) == PB - 1

    def e_at(k, i, j):
        return es[k, pl.ds((x0 + i) * CB + y0 + j, PB)]

    def h_at(k, i, j):
        return hs[k, pl.ds((x0 + i + 1) * CB + y0 + j, PB)]

    def up(v, edge):
        return jnp.where(final, edge, pltpu.roll(v, PB - 1, 0))

    def down(v, edge):
        return jnp.where(first, edge, pltpu.roll(v, 1, 0))

    class Cell:
        pass

    def averages(name, o, e, c, u1, u0, wu, v1, v0, wv, pa, pb):
        vm = 0.5 * (v0 + v1)
        um = 0.5 * (u0 + u1)
        qu = 0.25 * wu
        qv = 0.25 * wv
        base_a = e - c * (vm + qv)
        base_b = e + c * (um - qu)
        setattr(o, name + pa + "1", base_a + c * u1)
        setattr(o, name + pa + "0", base_a + c * (u0 - 0.5 * wu))
        setattr(o, name + pb + "1", base_b - c * v1)
        setattr(o, name + pb + "0", base_b - c * (v0 + 0.5 * wv))
        setattr(o, name + "s" + pa + "0", e + c * (u0 - wu - vm - 0.5 * wv))
        setattr(o, name + "s" + pb + "0", e + c * (um - 0.5 * wu - v0 - wv))

    def stage_one(i):
        o = Cell()
        ex, ey, ez = [e_at(k, i, 0) for k in range(3)]
        exu, ezu = e_at(0, i, 1), e_at(2, i, 1)
        exd, eyd, ezd = [e_at(k, i, -1) for k in range(3)]
        exf, eyf, ezf = [e_at(k, i + 1, 0) for k in range(3)]
        eyb, ezb = e_at(1, i - 1, 0), e_at(2, i - 1, 0)
        exbu, exb = e_at(0, i - 1, 1), e_at(0, i - 1, 0)
        eyfd = e_at(1, i + 1, -1)
        hx, hy, hz = [h_at(k, i, 0) for k in range(3)]
        hxd, hzd = h_at(0, i, -1), h_at(2, i, -1)
        hyb, hzb = h_at(1, i - 1, 0), h_at(2, i - 1, 0)
        c = cs[pl.ds((x0 + i) * CB + y0, PB)]
        dyex, dyez = exu - ex, ezu - ez
        dxey, dxez = eyf - ey, ezf - ez
        dzex, dzey = z_next(ex) - ex, z_next(ey) - ey
        dyexb = exbu - exb
        dxeyd = eyfd - eyd
        szex, szey = z_prev(dzex), z_prev(dzey)
        averages(
            "x", o, ex, c,
            0.5 * dyex, hz - hzd - 0.5 * (ex - exd), 0.5 * (dxey - dxeyd),
            -0.5 * dzex, hy - z_prev(hy) + 0.5 * szex, 0.5 * (dxez - z_prev(dxez)),
            "y", "z",
        )
        averages(
            "y", o, ey, c,
            0.5 * dzey, hx - z_prev(hx) - 0.5 * szey, 0.5 * (dyez - z_prev(dyez)),
            -0.5 * dxey, hz - hzb + 0.5 * (ey - eyb), 0.5 * (dyex - dyexb),
            "z", "x",
        )
        dzexb = z_next(exb) - exb
        dzeyd = z_next(eyd) - eyd
        averages(
            "z", o, ez, c,
            0.5 * dxez, hy - hyb - 0.5 * (ez - ezb), 0.5 * (dzex - dzexb),
            -0.5 * dyez, hx - hxd + 0.5 * (ez - ezd), 0.5 * (dzey - dzeyd),
            "x", "y",
        )
        o.c = c
        o.h = (hx, hy, hz)
        o.d = (dyez, dzey, dzex, dxez, dxey, dyex)
        o.down = (exd, eyd, ezd, eyfd, hxd, hzd, dzeyd)
        o.up = (exu, ezu, e_at(1, i, 1))
        return o

    def ring_ahead(i):
        o = Cell()
        ey, ez = e_at(1, i, 0), e_at(2, i, 0)
        o.yx0 = o.ysx0 = ey
        o.zx0 = o.zsx0 = ez
        return o

    def ring_behind(o):
        ex, ey, ez = [e_at(k, -1, 0) for k in range(3)]
        h2zx = h_at(2, -1, 0) - 0.5 * (o.yx0 - ey) + 0.25 * (e_at(0, -1, 1) - ex)
        h2yx = h_at(1, -1, 0) - 0.25 * (z_next(ex) - ex) + 0.5 * (o.zx0 - ez)
        return h2zx, h2yx

    def stage_two(o, n, behind):
        hx, hy, hz = o.h
        dyez, dzey, dzex, dxez, dxey, dyex = o.d
        exd, eyd, ezd, eyfd, hxd, hzd, dzeyd = o.down
        exu, ezu, eyu = o.up
        h2zx_b, h2yx_b = behind
        xy0u = up(o.xy0, exu)
        zy0u = up(o.zy0, ezu)
        h2zy = hz - 0.25 * dxey + 0.5 * dyex - 0.25 * (n.ysx0 - o.ysx0) + 0.5 * (xy0u - o.xy1)
        h2zx = hz - 0.5 * dxey + 0.25 * dyex - 0.5 * (n.yx0 - o.yx1) + 0.25 * (up(o.xsy0, exu) - o.xsy0)
        h2xz = hx - 0.25 * dyez + 0.5 * dzey - 0.25 * (up(o.zsy0, ezu) - o.zsy0) + 0.5 * (z_next(o.yz0) - o.yz1)
        h2xy = hx - 0.5 * dyez + 0.25 * dzey - 0.5 * (zy0u - o.zy1) + 0.25 * (z_next(o.ysz0) - o.ysz0)
        h2yx = hy - 0.25 * dzex + 0.5 * dxez - 0.25 * (z_next(o.xsz0) - o.xsz0) + 0.5 * (n.zx0 - o.zx1)
        h2yz = hy - 0.5 * dzex + 0.25 * dxez - 0.5 * (z_next(o.xz0) - o.xz1) + 0.25 * (n.zsx0 - o.zsx0)
        h2zy_d = down(h2zy, hzd - 0.25 * (eyfd - eyd) + 0.5 * (o.xy0 - exd))
        h2xy_d = down(h2xy, hxd - 0.5 * (o.zy0 - ezd) + 0.25 * dzeyd)
        half = 0.5 * o.c
        ex = 0.5 * (o.xy0 + o.xy1) + half * (h2zy - h2zy_d - h2yz + z_prev(h2yz))
        ey = 0.5 * (o.yz0 + o.yz1) + half * (h2xz - z_prev(h2xz) - h2zx + h2zx_b)
        ez = 0.5 * (o.zx0 + o.zx1) + half * (h2yx - h2yx_b - h2xy + h2xy_d)
        hx = hx - 0.25 * (dyez - dzey + zy0u - o.zy0 - z_next(o.yz0) + o.yz0)
        hy = hy - 0.25 * (dzex - dxez + z_next(o.xz0) - o.xz0 - n.zx0 + o.zx0)
        hz = hz - 0.25 * (dxey - dyex + n.yx0 - o.yx0 - xy0u + o.xy0)
        return (ex, ey, ez), (hx, hy, hz), (h2zx, h2yx)

    now = stage_one(0)
    behind = ring_behind(now)
    for i in range(PB):
        later = stage_one(i + 1) if i < PB - 1 else ring_ahead(i + 1)
        e_new, h_new, behind = stage_two(now, later, behind)
        pending = (i, e_new, h_new)
        if i > 0:
            write(es, hs, x0, y0, previous)
        previous = pending
        now = later
    write(es, hs, x0, y0, previous)


def write(es, hs, x0, y0, item):
    i, e_new, h_new = item
    for k in range(3):
        es[k, pl.ds((x0 + i) * CB + y0, PB)] = e_new[k]
        hs[k, pl.ds((x0 + i + 1) * CB + y0, PB)] = h_new[k]


def second_kernel(owner, corner, spots, points, faces, halo, e_in, h_in, c_in, e_out, h_out, sampled, es, hs, cs, ye, yh, taken, slot_x, slot_y, count, sem):
    loads = [
        pltpu.make_async_copy(e_in, es.at[:, pl.ds(0, ROWS)], sem.at[0]),
        pltpu.make_async_copy(h_in, hs.at[:, pl.ds(CB, ROWS)], sem.at[1]),
        pltpu.make_async_copy(c_in, cs, sem.at[2]),
    ]
    for copy in loads:
        copy.start()
    me = lax.axis_index("gx") * GY + lax.axis_index("gy")

    def look(n, found):
        slot_x[found] = corner[0, n]
        slot_y[found] = corner[1, n]
        return jnp.minimum(found + (owner[n] == me).astype(jnp.int32), SLOTS)

    count[0] = lax.fori_loop(0, GX * GY, look, 0, unroll=8)
    for copy in loads:
        copy.wait()
    lane = lanes_of((1, CZ))

    def patches():
        def one(n, carry):
            patch(es, hs, cs, slot_x[n], slot_y[n])
            return carry

        lax.fori_loop(0, count[0], one, 0)

    def sample():
        e_rows = es.reshape(3 * (ROWS + CB), CZ)
        h_rows = hs.reshape(3 * (ROWS + CB), CZ)

        def one(n, carry):
            mask = lane == spots[0, n]
            k1, k2 = spots[1, n], spots[2, n]
            taken[pl.ds(n, 1)] = jnp.where(mask, h_rows[pl.ds(k1 + CB, 1)], 0.0)
            taken[pl.ds(n + SPB, 1)] = jnp.where(mask, h_rows[pl.ds(k2 + CB, 1)], 0.0)
            taken[pl.ds(n + 2 * SPB, 1)] = jnp.where(mask, e_rows[pl.ds(k1, 1)], 0.0)
            taken[pl.ds(n + 3 * SPB, 1)] = jnp.where(mask, e_rows[pl.ds(k2, 1)], 0.0)
            return carry

        lax.fori_loop(0, SPB, one, 0, unroll=16)
        high, low = split(taken[...])
        ones = jnp.ones((16, CZ), BF16)
        return dot_t(ones, high) + dot_t(ones, low)

    slots = points[...]
    face = faces[...]
    sign = jnp.where(slots >= 0, (2 * (face % 2) - 1).astype(F32), 0.0)
    for moment in range(2):
        if moment:
            place_halo(es, hs, halo, ye, yh)
            advance(es, hs, cs, ye, yh)
        patches()
        if moment:
            stores = [
                pltpu.make_async_copy(es.at[:, pl.ds(0, ROWS)], e_out, sem.at[0]),
                pltpu.make_async_copy(hs.at[:, pl.ds(CB, ROWS)], h_out, sem.at[1]),
            ]
            for copy in stores:
                copy.start()
        got = sample()
        got = [got[0:1, j * SPB : (j + 1) * SPB] for j in range(4)]
        sampled[4 * moment : 4 * moment + 1] = -sign * got[1]
        sampled[4 * moment + 1 : 4 * moment + 2] = sign * got[0]
        sampled[4 * moment + 2 : 4 * moment + 3] = sign * got[3]
        sampled[4 * moment + 3 : 4 * moment + 4] = -sign * got[2]
    cell = jnp.maximum(slots, 0)
    sampled[8:9] = (cell // (CB * CZ)).astype(F32)
    sampled[9:10] = (cell // CZ % CB).astype(F32)
    sampled[10:11] = (cell % CZ).astype(F32)
    sampled[11:12] = jnp.where(slots >= 0, face, 6).astype(F32)
    sampled[12:16] = jnp.zeros((4, SPB), F32)
    for copy in stores:
        copy.wait()


def third_kernel(omega, sampled, ta_in, tc_in, tb_in, tcf_in, far, got, gathered, ta, tc, tb, tcf, hot, hotz, spread_hi, spread_lo, lhs1, lhs2, lhsz, acc, rows48, send_buf, recv_buf, load_sem, send1, recv1, send2, recv2):
    gx = lax.axis_index("gx")
    gy = lax.axis_index("gy")
    loads = [
        pltpu.make_async_copy(ta_in, ta, load_sem.at[0]),
        pltpu.make_async_copy(tc_in, tc.at[:, pl.ds(0, 2 * ZF)], load_sem.at[1]),
        pltpu.make_async_copy(tc_in.at[:, pl.ds(0, ZF)], tc.at[:, pl.ds(2 * ZF, ZF)], load_sem.at[2]),
        pltpu.make_async_copy(tb_in, tb, load_sem.at[3]),
        pltpu.make_async_copy(tcf_in, tcf, load_sem.at[4]),
    ]
    for copy in loads:
        copy.start()
    barrier = pltpu.get_barrier_semaphore()
    for d in range(1, GX):
        pl.semaphore_signal(barrier, inc=1, device_id=(lax.rem(gx + d, GX), gy), device_id_type=MESH)
    for d in range(1, GY):
        pl.semaphore_signal(barrier, inc=1, device_id=(gx, lax.rem(gy + d, GY)), device_id_type=MESH)
    tc[:, 3 * ZF : 4 * ZF] = jnp.zeros((2, ZF, QF), BF16)
    pl.semaphore_wait(barrier, GX + GY - 2)
    first = []
    for d in range(1, GX):
        copy = pltpu.make_async_remote_copy(
            src_ref=sampled,
            dst_ref=gathered.at[GX - d],
            send_sem=send1.at[d],
            recv_sem=recv1.at[GX - d],
            device_id=(lax.rem(gx + d, GX), gy),
            device_id_type=MESH,
        )
        copy.start()
        first.append(copy)
    gathered[0] = sampled[...]
    for copy in first:
        copy.wait()

    for b in range(GX):
        lanes = slice(b * SPB, (b + 1) * SPB)
        got[0:16, lanes] = gathered[b]
        block = lax.rem(gx + b, GX)
        x = gathered[b, 8:9] + (block * CB).astype(F32)
        z = gathered[b, 10:11]
        got[12:13, lanes] = jnp.where(x < 128.0, 127.0 - x, x - 128.0)
        got[13:14, lanes] = jnp.where(x < 128.0, -1.0, 1.0)
        got[14:15, lanes] = jnp.where(z < 64.0, 63.0 - z, z - 64.0)
        got[15:16, lanes] = jnp.where(z < 64.0, -1.0, 1.0)

    def one_hot(to, place_row, sign_row, count, blocks):
        for b, start in enumerate(blocks):
            lanes = pl.ds(start, SPB)
            there = slice(b * SPB, (b + 1) * SPB)
            where_at = jnp.broadcast_to(got[place_row : place_row + 1, lanes], (16, SPB))
            sign = jnp.broadcast_to(got[sign_row : sign_row + 1, lanes], (16, SPB))
            at = rows_of((16, SPB)).astype(F32)
            for j in range(0, count, 16):
                same = at + float(j) == where_at
                to[j : j + 16, there] = jnp.where(same, 1.0, 0.0).astype(BF16)
                to[count + j : count + j + 16, there] = jnp.where(same, sign, 0.0).astype(BF16)

    def halves(v):
        high = v.astype(BF16).astype(F32)
        return high, v - high

    def spread(v, key, start, step, first_row, there, count):
        high, low = halves(v)

        def one(n, carry):
            same = key == (start + step * n).astype(F32)
            at = pl.ds(pl.multiple_of(first_row + n * 16, 16), 16)
            spread_hi[at, there] = jnp.where(same, high, 0.0).astype(BF16)
            spread_lo[at, there] = jnp.where(same, low, 0.0).astype(BF16)
            return carry

        lax.fori_loop(0, count, one, 0, unroll=8)

    def row16(row, lanes):
        return jnp.broadcast_to(got[row : row + 1, lanes], (16, SPB))

    upper = rows_of((16, SPB)) // 8
    every = [b * SPB for b in range(GX)]
    ends = [pl.multiple_of(lax.rem(GX - gx, GX) * SPB, SPB), pl.multiple_of((GX - 1 - gx) * SPB, SPB)]

    def twice(lanes):
        v = got[0:8, lanes]
        return jnp.concatenate([v, v], axis=0)

    def spread_z(y_low, count):
        wanted = (4 + upper).astype(F32)
        for b in range(GX):
            lanes = slice(b * SPB, (b + 1) * SPB)
            v = jnp.where(row16(11, lanes) == wanted, twice(lanes), 0.0)
            spread(v, row16(9, lanes), y_low, 1, 0, lanes, count)

    def spread_x(y_low, count):
        for e, start in enumerate(ends):
            lanes = pl.ds(start, SPB)
            wanted = jnp.where(upper == e, float(e), -1.0)
            v = jnp.where(row16(11, lanes) == wanted, twice(lanes), 0.0)
            spread(v, row16(9, lanes), y_low, 1, 0, slice(e * SPB, (e + 1) * SPB), count)

    def spread_y():
        for b in range(GX):
            lanes = slice(b * SPB, (b + 1) * SPB)
            face = row16(11, lanes)
            v = jnp.where((face == 2.0) | (face == 3.0), twice(lanes), 0.0)
            spread(v, row16(10, lanes) - upper.astype(F32), 16, 2, 0, lanes, YF_ROWS // 2)

    def dense(to, rows):
        for m in range(0, rows, CHUNK):
            d = dot_t(spread_hi[m : m + CHUNK], hot[...]) + dot_t(spread_lo[m : m + CHUNK], hot[...])
            for k in range(2):
                high, low = split(d[:, k * XF : (k + 1) * XF])
                lhs1[k, to + m : to + m + CHUNK, 0:XF] = high
                lhs1[k, to + m : to + m + CHUNK, XF : 2 * XF] = high
                lhs2[k, to + m : to + m + CHUNK] = low

    def dense_x(rows):
        for m in range(0, rows, CHUNK):
            at = slice(m, m + CHUNK)
            d = dot_t(spread_hi[at, 0 : 2 * SPB], hotz[...]) + dot_t(spread_lo[at, 0 : 2 * SPB], hotz[...])
            for k in range(2):
                high, low = split(d[:, k * ZF : (k + 1) * ZF])
                lhsz[k, at] = jnp.concatenate([high, high, low, jnp.zeros_like(low)], axis=1)

    def times_x(to, lanes):
        out = []
        for k in range(2):
            table = ta[k, :, lanes]
            out.append(dot(lhs1[k, to : to + CHUNK], table) + dot(lhs2[k, to : to + CHUNK], table[0:XF]))
        return out

    def times_z(to, lanes):
        return [dot(lhsz[k, to : to + CHUNK], tc[k, :, lanes]) for k in range(2)]

    def outer_y(g, total, y_low, lanes):
        re, im = total
        for y in range(16):
            at = slice(y * 16, (y + 1) * 16)
            bc, bs = tb[0, pl.ds(y_low + y, 1), lanes], tb[1, pl.ds(y_low + y, 1), lanes]
            re = re + (bc * g[0][at] - bs * g[1][at])
            im = im + (bc * g[1][at] + bs * g[0][at])
        return re, im

    def outer_z(g, total, z_low, lanes):
        re, im = total
        for o in range(CHUNK // 8):
            z = z_low + o
            j, sign = (z - 64, 1.0) if z >= 64 else (63 - z, -1.0)
            at = slice(o * 8, (o + 1) * 8)
            cc, cs = tcf[0, j : j + 1, lanes], sign * tcf[1, j : j + 1, lanes]
            re = re + (cc * g[0][at] - cs * g[1][at])
            im = im + (cc * g[1][at] + cs * g[0][at])
        return re, im

    def keep(base, total, lanes):
        n = total[0].shape[0]
        acc[base, 0, 0:n, lanes] = total[0]
        acc[base, 1, 0:n, lanes] = total[1]

    edge = (gy == 0) | (gy == GY - 1)
    zero16 = jnp.zeros((16, CHUNK), F32)
    zero8 = jnp.zeros((8, CHUNK), F32)
    one_hot(hot, 12, 13, XF, every)
    one_hot(hotz, 14, 15, ZF, ends)
    for copy in loads:
        copy.wait()

    @pl.when(jnp.logical_not(edge))
    def _():
        spread_z(0, CB)
        dense(0, CB * 16)
        spread_x(0, CB)
        dense_x(CB * 16)
        acc[2] = jnp.zeros((2, 16, QF), F32)

        def chunk(n, carry):
            lanes = pl.ds(pl.multiple_of(n * CHUNK, CHUNK), CHUNK)
            total = (zero16, zero16)
            for y in range(2):
                total = outer_y(times_x(y * CHUNK, lanes), total, y * 16, lanes)
            keep(0, total, lanes)
            total = (zero16, zero16)
            for y in range(2):
                total = outer_y(times_z(y * CHUNK, lanes), total, y * 16, lanes)
            keep(1, total, lanes)
            return carry

        lax.fori_loop(0, QF // CHUNK, chunk, 0)

    @pl.when(edge)
    def _():
        y_low = jnp.where(gy == 0, 16, 0)
        spread_z(y_low, 16)
        dense(0, CHUNK)
        spread_x(y_low, 16)
        dense_x(CHUNK)
        spread_y()
        dense(CHUNK, YF_ROWS * 8)

        def chunk(n, carry):
            lanes = pl.ds(pl.multiple_of(n * CHUNK, CHUNK), CHUNK)
            keep(0, outer_y(times_x(0, lanes), (zero16, zero16), y_low, lanes), lanes)
            keep(1, outer_y(times_z(0, lanes), (zero16, zero16), y_low, lanes), lanes)
            total = (zero8, zero8)
            for z in range(0, YF_ROWS, CHUNK // 8):
                total = outer_z(times_x(CHUNK + z * 8, lanes), total, z + 16, lanes)
            keep(2, total, lanes)
            return carry

        lax.fori_loop(0, QF // CHUNK, chunk, 0)

    scale = 1.0 / math.sqrt(GX * GY * SPB)
    y_face = jnp.where(gy == 0, 16, 15)
    moment = 1.0 + (rows_of((8, 1)) // 4).astype(F32)
    for f in range(FREQ):
        lanes = slice(f * QN, (f + 1) * QN)
        mc, ms = turn(omega[f] * (1.0 / (2.0 * math.pi)) * moment)
        mc, ms = mc * scale, ms * scale

        def both(base, c, s):
            low_re, high_re = acc[base, 0, 0:8, lanes], acc[base, 0, 8:16, lanes]
            low_im, high_im = acc[base, 1, 0:8, lanes], acc[base, 1, 8:16, lanes]
            re = c * (low_re + high_re) + s * (low_im - high_im)
            im = c * (low_im + high_im) + s * (high_re - low_re)
            return re, im

        def late(re, im):
            a, b = mc * re + ms * im, mc * im - ms * re
            return a[0:4] + a[4:8], b[0:4] + b[4:8]

        zf = late(*both(0, tcf[0, Z_FACE : Z_FACE + 1, lanes], tcf[1, Z_FACE : Z_FACE + 1, lanes]))
        xf = late(*both(1, tb[0, CB : CB + 1, lanes], tb[1, CB : CB + 1, lanes]))
        c, s = tb[0, pl.ds(y_face, 1), lanes], tb[1, pl.ds(y_face, 1), lanes]
        re, im = acc[2, 0, 0:8, lanes], acc[2, 1, 0:8, lanes]
        yf = late(c * re - s * im, c * im + s * re)
        for k in range(2):
            z4, x4, y4 = zf[k], xf[k], yf[k]
            six = [
                z4[0:1] + y4[1:2], z4[1:2] + x4[0:1], x4[1:2] + y4[0:1],
                z4[2:3] + y4[3:4], z4[3:4] + x4[2:3], x4[3:4] + y4[2:3],
            ]
            for j, v in enumerate(six):
                rows48[12 * f + 6 * k + j : 12 * f + 6 * k + j + 1] = v
    rows48[48:128] = jnp.zeros((80, QN), F32)
    for t in range(0, QN, 128):
        send_buf[t : t + 128] = jnp.transpose(rows48[:, t : t + 128])

    second = []
    for d in range(1, GY):
        to = lax.rem(gy + d, GY)
        copy = pltpu.make_async_remote_copy(
            src_ref=send_buf.at[pl.ds(pl.multiple_of(to * OWN, OWN), OWN)],
            dst_ref=recv_buf.at[GY - d],
            send_sem=send2.at[d],
            recv_sem=recv2.at[GY - d],
            device_id=(gx, to),
            device_id_type=MESH,
        )
        copy.start()
        second.append(copy)
    total = send_buf[pl.ds(pl.multiple_of(gy * OWN, OWN), OWN)]
    for copy in second:
        copy.wait()
    for d in range(1, GY):
        total = total + recv_buf[d]
    far[...] = total[:, 0:48]


VMEM = pl.BlockSpec(memory_space=pltpu.VMEM)
SMEM = pl.BlockSpec(memory_space=pltpu.SMEM)
ANY = pl.BlockSpec(memory_space=pl.ANY)


def local(efield, hfield, e_coef, omega, patch_owner, patch_corner, surface_points, surface_faces, angle_index):
    field = jax.ShapeDtypeStruct((3, ROWS, CZ), F32)
    fields = [
        pltpu.VMEM((3, ROWS + CB, CZ), F32),
        pltpu.VMEM((3, ROWS + CB, CZ), F32),
        pltpu.VMEM((ROWS, CZ), F32),
        pltpu.VMEM((2, CB, CZ), F32),
        pltpu.VMEM((2, CB, CZ), F32),
    ]
    coef = e_coef.reshape(ROWS, CZ)
    points = surface_points.reshape(1, SPB)
    faces = surface_faces.reshape(1, SPB)
    efield, hfield, halo, *tabled, spots = pl.pallas_call(
        first_kernel,
        out_shape=(
            field,
            field,
            jax.ShapeDtypeStruct((9, CB, CZ), F32),
            jax.ShapeDtypeStruct((2, 2 * XF, QF), BF16),
            jax.ShapeDtypeStruct((2, 2 * ZF, QF), BF16),
            jax.ShapeDtypeStruct((2, CB + 8, QF), F32),
            jax.ShapeDtypeStruct((2, ZF, QF), F32),
            jax.ShapeDtypeStruct((8, SPB), jnp.int32),
        ),
        in_specs=[SMEM, VMEM, VMEM, VMEM, ANY, ANY, ANY],
        out_specs=(ANY, ANY, VMEM, ANY, ANY, ANY, ANY, VMEM),
        scratch_shapes=[
            pltpu.VMEM((8, QF), F32),
            pltpu.VMEM((2, 2 * XF, QF), BF16),
            pltpu.VMEM((2, 2 * ZF, QF), BF16),
            pltpu.VMEM((2, CB + 8, QF), F32),
            pltpu.VMEM((2, ZF, QF), F32),
        ]
        + fields
        + [
            pltpu.VMEM((2, 9, CB, CZ), F32),
            pltpu.VMEM((9, CB, CZ), F32),
            pltpu.SemaphoreType.DMA((6,)),
            pltpu.SemaphoreType.DMA((2, 6)),
            pltpu.SemaphoreType.DMA((2, 6)),
        ],
        compiler_params=pltpu.CompilerParams(collective_id=0, has_side_effects=True, vmem_limit_bytes=56 * 2**20),
        name="first_step",
    )(omega, angle_index.T, points, faces, efield.reshape(3, ROWS, CZ), hfield.reshape(3, ROWS, CZ), coef)
    efield, hfield, sampled = pl.pallas_call(
        second_kernel,
        out_shape=(field, field, jax.ShapeDtypeStruct((16, SPB), F32)),
        in_specs=[SMEM, SMEM, SMEM, VMEM, VMEM, VMEM, ANY, ANY, ANY],
        out_specs=(ANY, ANY, VMEM),
        scratch_shapes=fields
        + [
            pltpu.VMEM((4 * SPB, CZ), F32),
            pltpu.SMEM((SLOTS + 1,), jnp.int32),
            pltpu.SMEM((SLOTS + 1,), jnp.int32),
            pltpu.SMEM((1,), jnp.int32),
            pltpu.SemaphoreType.DMA((3,)),
        ],
        compiler_params=pltpu.CompilerParams(vmem_limit_bytes=56 * 2**20),
        name="patches",
    )(patch_owner, patch_corner.T, spots, points, faces, halo, efield, hfield, coef)
    far = pl.pallas_call(
        third_kernel,
        out_shape=jax.ShapeDtypeStruct((OWN, 48), F32),
        in_specs=[SMEM, VMEM, ANY, ANY, ANY, ANY],
        out_specs=VMEM,
        scratch_shapes=[
            pltpu.VMEM((16, GX * SPB), F32),
            pltpu.VMEM((GX, 16, SPB), F32),
            pltpu.VMEM((2, 2 * XF, QF), BF16),
            pltpu.VMEM((2, 4 * ZF, QF), BF16),
            pltpu.VMEM((2, CB + 8, QF), F32),
            pltpu.VMEM((2, ZF, QF), F32),
            pltpu.VMEM((2 * XF, GX * SPB), BF16),
            pltpu.VMEM((2 * ZF, 2 * SPB), BF16),
            pltpu.VMEM((YF_ROWS * 8, GX * SPB), BF16),
            pltpu.VMEM((YF_ROWS * 8, GX * SPB), BF16),
            pltpu.VMEM((2, YF_ROWS * 8 + CHUNK, 2 * XF), BF16),
            pltpu.VMEM((2, YF_ROWS * 8 + CHUNK, XF), BF16),
            pltpu.VMEM((2, CB * 16, 4 * ZF), BF16),
            pltpu.VMEM((3, 2, 16, QF), F32),
            pltpu.VMEM((128, QN), F32),
            pltpu.VMEM((QN, 128), F32),
            pltpu.VMEM((GY, OWN, 128), F32),
            pltpu.SemaphoreType.DMA((5,)),
            pltpu.SemaphoreType.DMA((GX,)),
            pltpu.SemaphoreType.DMA((GX,)),
            pltpu.SemaphoreType.DMA((GY,)),
            pltpu.SemaphoreType.DMA((GY,)),
        ],
        compiler_params=pltpu.CompilerParams(collective_id=1, has_side_effects=True, vmem_limit_bytes=56 * 2**20),
        name="projection",
    )(omega, sampled, *tabled)
    shape = (3, CB, CB, CZ)
    return efield.reshape(shape), hfield.reshape(shape), far


def solution(mesh):
    placed = (
        P(None, "gx", "gy", None),
        P(None, "gx", "gy", None),
        P("gx", "gy", None),
        P(),
        P(),
        P(),
        P("gx", "gy", None),
        P("gx", "gy", None),
        P(),
    )
    return jax.shard_map(
        local,
        mesh=mesh,
        in_specs=placed,
        out_specs=(P(None, "gx", "gy", None), P(None, "gx", "gy", None), P(("gx", "gy"), None)),
        check_vma=False,
    )
```

```python
import math

import jax
import jax.numpy as jnp
import numpy as np
from jax import lax
from jax.experimental import pallas as pl
from jax.experimental.pallas import tpu as pltpu
from jax.sharding import PartitionSpec as P

PB = 8
SLOTS = 4
NTH = 128
NPH = 256
CB = 32
CZ = 128
ROWS = CB * CB
SPB = 256
FREQ = 4
GX = 8
GY = 16
ANG = 4096
QN = ANG // GX
QF = QN * FREQ
OWN = ANG // (GX * GY)
HALF = OWN // 2
MESH = pl.DeviceIdType.MESH
F32 = jnp.float32
BF16 = jnp.bfloat16


def lanes_of(shape):
    return lax.broadcasted_iota(jnp.int32, shape, 1)


def rows_of(shape):
    return lax.broadcasted_iota(jnp.int32, shape, 0)


def z_next(v):
    return jnp.where(lanes_of(v.shape) == CZ - 1, 0.0, pltpu.roll(v, CZ - 1, 1))


def z_prev(v):
    return jnp.where(lanes_of(v.shape) == 0, 0.0, pltpu.roll(v, 1, 1))


def y_next(v, edge):
    n = v.shape[0]
    return jnp.where(rows_of(v.shape) == n - 1, edge, pltpu.roll(v, n - 1, 0))


def y_prev(v, edge):
    return jnp.where(rows_of(v.shape) == 0, edge, pltpu.roll(v, 1, 0))


def prepare(es, hs, out):
    out[0] = es[1, 0:CB]
    out[1] = es[2, 0:CB]
    last = (CB - 1) * CB
    ex, ey, ez = [es[k, last : last + CB] for k in range(3)]
    hy, hz = [hs[k, last + CB : last + 2 * CB] for k in (1, 2)]
    out[2] = hy - 0.5 * (z_next(ex) - ex + ez)
    out[3] = hz + 0.5 * (ey + y_next(ex, 0.0) - ex)
    out[8, 8:16] = ey[CB - 8 : CB] * 0.0 + es[1, CB - 1 : CB]
    out[8, 0:8] = ex[0:1] + jnp.zeros((8, CZ), F32)
    out[8, 16:32] = jnp.zeros((16, CZ), F32)
    out[4] = es[0, pl.ds(0, CB, stride=CB)]
    out[5] = es[2, pl.ds(0, CB, stride=CB)]
    ex, ey, ez = [es[k, pl.ds(CB - 1, CB, stride=CB)] for k in range(3)]
    hx, hz = [hs[k, pl.ds(2 * CB - 1, CB, stride=CB)] for k in (0, 2)]
    out[6] = hx + 0.5 * (ez + z_next(ey) - ey)
    out[7] = hz - 0.5 * (y_next(ey, 0.0) - ey + ex)


def place_halo(es, hs, halo, ye, yh):
    gx = lax.axis_index("gx")
    gy = lax.axis_index("gy")
    x_low = (gx > 0).astype(F32)
    x_high = (gx < GX - 1).astype(F32)
    y_low = (gy > 0).astype(F32)
    y_high = (gy < GY - 1).astype(F32)
    last_row = rows_of((CB, CZ)) == CB - 1
    es[1, ROWS : ROWS + CB] = halo[0] * x_high
    es[2, ROWS : ROWS + CB] = halo[1] * x_high
    ye[0] = halo[4] * y_high
    ye[1] = halo[5] * y_high
    corner = jnp.where(last_row, halo[8, 0:1] * (0.5 * y_high), 0.0)
    hs[1, 0:CB] = x_low * (halo[2] + 0.5 * es[2, 0:CB])
    hs[2, 0:CB] = x_low * (halo[3] - 0.5 * es[1, 0:CB] + corner)
    corner = jnp.where(last_row, halo[8, 8:9] * (0.5 * x_high), 0.0)
    yh[0] = y_low * (halo[6] - 0.5 * es[2, pl.ds(0, CB, stride=CB)])
    yh[1] = y_low * (halo[7] + 0.5 * es[0, pl.ds(0, CB, stride=CB)] - corner)


def add_halo(es, hs, cs, halo, own):
    gx = lax.axis_index("gx")
    gy = lax.axis_index("gy")
    x_low = (gx > 0).astype(F32)
    x_high = (gx < GX - 1).astype(F32)
    y_low = (gy > 0).astype(F32)
    y_high = (gy < GY - 1).astype(F32)
    last_row = rows_of((CB, CZ)) == CB - 1
    low_rows = pl.ds(0, CB, stride=CB)
    high_rows = pl.ds(CB - 1, CB, stride=CB)
    h_rows = pl.ds(2 * CB - 1, CB, stride=CB)
    plane = slice(ROWS - CB, ROWS)
    dy, dz = 0.5 * x_high * halo[1], -0.5 * x_high * halo[0]
    hs[1, ROWS : ROWS + CB] += dy
    hs[2, ROWS : ROWS + CB] += dz
    c = cs[plane]
    es[0, plane] += c * (dz - y_prev(dz, 0.0) - dy + z_prev(dy))
    es[1, plane] -= c * dz
    es[2, plane] += c * dy
    dx, dz = -0.5 * y_high * halo[5], 0.5 * y_high * halo[4]
    hs[0, h_rows] = hs[0, h_rows] + dx
    hs[2, h_rows] = hs[2, h_rows] + dz
    c = cs[high_rows]
    es[0, high_rows] = es[0, high_rows] + c * dz
    es[1, high_rows] = es[1, high_rows] + c * (dx - z_prev(dx) - dz + y_prev(dz, 0.0))
    es[2, high_rows] = es[2, high_rows] - c * dx
    corner = jnp.where(last_row, halo[8, 0:1] * (0.5 * y_high), 0.0)
    before_y = x_low * (halo[2] + 0.5 * own[1])
    before_z = x_low * (halo[3] - 0.5 * own[0] + corner)
    c = cs[0:CB]
    es[1, 0:CB] += c * before_z
    es[2, 0:CB] -= c * before_y
    corner = jnp.where(last_row, halo[8, 8:9] * (0.5 * x_high), 0.0)
    before_x = y_low * (halo[6] - 0.5 * own[5])
    before_z = y_low * (halo[7] + 0.5 * own[4] - corner)
    c = cs[low_rows]
    es[0, low_rows] = es[0, low_rows] - c * before_z
    es[2, low_rows] = es[2, low_rows] + c * before_x


def advance(es, hs, cs, ye, yh):
    last = rows_of((CB, CZ)) == CB - 1
    for x in range(CB):
        r = x * CB
        here, after = slice(r, r + CB), slice(r + CB, r + 2 * CB)
        ex, ey, ez = [es[k, here] for k in range(3)]
        ey1, ez1 = es[1, after], es[2, after]
        hx, hy, hz = [hs[k, after] for k in range(3)]
        if x == 0:
            hy0, hz0 = hs[1, here], hs[2, here]
        exu = jnp.where(last, ye[0, x : x + 1], es[0, r + 1 : r + CB + 1])
        ezu = jnp.where(last, ye[1, x : x + 1], es[2, r + 1 : r + CB + 1])
        hx = hx - 0.5 * (ezu - ez - z_next(ey) + ey)
        hy = hy - 0.5 * (z_next(ex) - ex - ez1 + ez)
        hz = hz - 0.5 * (ey1 - ey - exu + ex)
        for k, v in enumerate((hx, hy, hz)):
            hs[k, after] = v
        c = cs[here]
        ex = ex + c * (hz - y_prev(hz, yh[1, x : x + 1]) - hy + z_prev(hy))
        ey = ey + c * (hx - z_prev(hx) - hz + hz0)
        ez = ez + c * (hy - hy0 - hx + y_prev(hx, yh[0, x : x + 1]))
        for k, v in enumerate((ex, ey, ez)):
            es[k, here] = v
        hy0, hz0 = hy, hz


def neighbours():
    gx = lax.axis_index("gx")
    gy = lax.axis_index("gy")
    xn, xp = lax.rem(gx + 1, GX), lax.rem(gx + GX - 1, GX)
    yn, yp = lax.rem(gy + 1, GY), lax.rem(gy + GY - 1, GY)
    return [(xp, gy), (xn, gy), (gx, yp), (gx, yn), (xn, yp), (xp, yn)]


def pieces(ref, n):
    if n < 4:
        return ref.at[pl.ds(2 * n, 2)]
    return ref.at[8, pl.ds(8 * (n - 4), 8)]


def fitted(function, degrees, points=4001):
    r = np.cos(np.linspace(0.0, np.pi, points)) * 0.5
    basis = np.stack([r**d for d in degrees], axis=1)
    return [float(v) for v in np.linalg.lstsq(basis, function(np.pi * r) * math.sqrt(2.0), rcond=None)[0]]


SIN = fitted(np.sin, (1, 3, 5, 7, 9))
COS = fitted(np.cos, (0, 2, 4, 6, 8))


def turn(t):
    r = t - jnp.round(t)
    r2 = r * r
    s = r * (SIN[0] + r2 * (SIN[1] + r2 * (SIN[2] + r2 * (SIN[3] + r2 * SIN[4]))))
    c = COS[0] + r2 * (COS[1] + r2 * (COS[2] + r2 * (COS[3] + r2 * COS[4])))
    return 1.0 - s * s, s * c


def split(v):
    high = v.astype(BF16)
    return high, (v - high.astype(F32)).astype(BF16)


def dot(a, b):
    return jnp.dot(a, b, preferred_element_type=F32)


def dot_t(a, b):
    return lax.dot_general(a, b, (((1,), (1,)), ((), ())), preferred_element_type=F32)


CUT1 = 2
CUT2 = 5
XF = 128
ZF = 64
YF_ROWS = 96
CHUNK = 256
X_FACE = 111
Z_FACE = 47


def directions(omega, angles, kdir):
    index = angles[:, pl.ds(pl.multiple_of(lax.axis_index("gx") * QN, QN), QN)].astype(F32)
    theta = math.pi * (index[0:1] + 0.5) / NTH
    phi = 2.0 * math.pi * (index[1:2] + 0.5) / NPH
    st, ct = jnp.sin(theta), jnp.cos(theta)
    sp, cp = jnp.sin(phi), jnp.cos(phi)
    for f in range(FREQ):
        w = omega[f] * (1.0 / (2.0 * math.pi))
        lanes = slice(f * QN, (f + 1) * QN)
        kdir[0:1, lanes] = st * cp * w
        kdir[1:2, lanes] = st * sp * w
        kdir[2:3, lanes] = ct * w


def tables(kdir, ta, tc, tb, n):
    y_start = (lax.axis_index("gy") * CB).astype(F32) + (0.5 - CB * GY / 2.0)
    lanes = pl.ds(pl.multiple_of(n * CHUNK, CHUNK), CHUNK)
    kx, ky, kz = kdir[0:1, lanes], kdir[1:2, lanes], kdir[2:3, lanes]
    count = rows_of((16, CHUNK)).astype(F32)
    for j in range(0, XF, 16):
        for k, v in enumerate(turn((count + (j + 0.5)) * kx)):
            high, low = split(v)
            ta[k, j : j + 16, lanes] = high
            ta[k, XF + j : XF + j + 16, lanes] = low
    for j in range(0, ZF, 16):
        for k, v in enumerate(turn((count + (j + 0.5)) * kz)):
            high, low = split(v)
            tc[k, j : j + 16, lanes] = high
            tc[k, ZF + j : ZF + j + 16, lanes] = low
    for j in range(0, CB, 16):
        for k, v in enumerate(turn((count + (y_start + j)) * ky)):
            tb[k, j : j + 16, lanes] = v
    for k, v in enumerate(turn(jnp.full((8, CHUNK), X_FACE + 0.5, F32) * kx)):
        tb[k, CB : CB + 8, lanes] = v


def first_kernel(omega, angles, points, faces, e_in, h_in, c_in, e_out, h_out, halo2, ta_out, tc_out, tb_out, spots, kdir, ta, tc, tb, es, hs, cs, ye, yh, sent, halo1, local_sem, send_sem, recv_sem):
    loads = [
        pltpu.make_async_copy(e_in, es.at[:, pl.ds(0, ROWS)], local_sem.at[0]),
        pltpu.make_async_copy(h_in, hs.at[:, pl.ds(CB, ROWS)], local_sem.at[1]),
        pltpu.make_async_copy(c_in, cs, local_sem.at[2]),
    ]
    for copy in loads:
        copy.start()
    barrier = pltpu.get_barrier_semaphore()
    for device in neighbours():
        pl.semaphore_signal(barrier, inc=1, device_id=device, device_id_type=MESH)
    directions(omega, angles, kdir)
    cell = jnp.maximum(points[...], 0)
    normal = lax.shift_right_logical(faces[...], 1)
    row = lax.shift_right_logical(cell, 7)
    spots[0:1] = cell & (CZ - 1)
    spots[1:2] = jnp.where(normal == 2, 0, normal + 1) * (ROWS + CB) + row
    spots[2:3] = jnp.where(normal == 0, 2, normal - 1) * (ROWS + CB) + row
    spots[3:8] = jnp.zeros((5, SPB), jnp.int32)

    def some_tables(low, high):
        def one(n, carry):
            tables(kdir, ta, tc, tb, n)
            return carry

        lax.fori_loop(low, high, one, 0)

    some_tables(0, CUT1)
    loads[0].wait()
    loads[1].wait()

    def exchange(number, halo):
        copies = []
        for n, device in enumerate(neighbours()):
            copy = pltpu.make_async_remote_copy(
                src_ref=pieces(sent.at[number], n),
                dst_ref=pieces(halo, n),
                send_sem=send_sem.at[number, n],
                recv_sem=recv_sem.at[number, n],
                device_id=device,
                device_id_type=MESH,
            )
            copy.start()
            copies.append(copy)
        return copies

    prepare(es, hs, sent.at[0])
    pl.semaphore_wait(barrier, 6)
    copies = exchange(0, halo1)
    for k in (1, 2):
        es[k, ROWS : ROWS + CB] = jnp.zeros((CB, CZ), F32)
        hs[k, 0:CB] = jnp.zeros((CB, CZ), F32)
    ye[...] = jnp.zeros_like(ye)
    yh[...] = jnp.zeros_like(yh)
    loads[2].wait()
    advance(es, hs, cs, ye, yh)
    some_tables(CUT1, CUT2)
    for copy in copies:
        copy.wait()
    add_halo(es, hs, cs, halo1, sent.at[0])
    prepare(es, hs, sent.at[1])
    copies = exchange(1, halo2)
    stores = [
        pltpu.make_async_copy(es.at[:, pl.ds(0, ROWS)], e_out, local_sem.at[0]),
        pltpu.make_async_copy(hs.at[:, pl.ds(CB, ROWS)], h_out, local_sem.at[1]),
    ]
    for copy in stores:
        copy.start()
    some_tables(CUT2, QF // CHUNK)
    for n, (table, out) in enumerate(((ta, ta_out), (tc, tc_out), (tb, tb_out))):
        copy = pltpu.make_async_copy(table, out, local_sem.at[2 + n])
        copy.start()
        stores.append(copy)
    for copy in copies + stores:
        copy.wait()


def patch(es, hs, cs, x0, y0):
    first = rows_of((PB, CZ)) == 0
    final = rows_of((PB, CZ)) == PB - 1

    def e_at(k, i, j):
        return es[k, pl.ds((x0 + i) * CB + y0 + j, PB)]

    def h_at(k, i, j):
        return hs[k, pl.ds((x0 + i + 1) * CB + y0 + j, PB)]

    def up(v, edge):
        return jnp.where(final, edge, pltpu.roll(v, PB - 1, 0))

    def down(v, edge):
        return jnp.where(first, edge, pltpu.roll(v, 1, 0))

    class Cell:
        pass

    def averages(name, o, e, c, u1, u0, wu, v1, v0, wv, pa, pb):
        vm = 0.5 * (v0 + v1)
        um = 0.5 * (u0 + u1)
        qu = 0.25 * wu
        qv = 0.25 * wv
        base_a = e - c * (vm + qv)
        base_b = e + c * (um - qu)
        setattr(o, name + pa + "1", base_a + c * u1)
        setattr(o, name + pa + "0", base_a + c * (u0 - 0.5 * wu))
        setattr(o, name + pb + "1", base_b - c * v1)
        setattr(o, name + pb + "0", base_b - c * (v0 + 0.5 * wv))
        setattr(o, name + "s" + pa + "0", e + c * (u0 - wu - vm - 0.5 * wv))
        setattr(o, name + "s" + pb + "0", e + c * (um - 0.5 * wu - v0 - wv))

    def stage_one(i):
        o = Cell()
        ex, ey, ez = [e_at(k, i, 0) for k in range(3)]
        exu, ezu = e_at(0, i, 1), e_at(2, i, 1)
        exd, eyd, ezd = [e_at(k, i, -1) for k in range(3)]
        exf, eyf, ezf = [e_at(k, i + 1, 0) for k in range(3)]
        eyb, ezb = e_at(1, i - 1, 0), e_at(2, i - 1, 0)
        exbu, exb = e_at(0, i - 1, 1), e_at(0, i - 1, 0)
        eyfd = e_at(1, i + 1, -1)
        hx, hy, hz = [h_at(k, i, 0) for k in range(3)]
        hxd, hzd = h_at(0, i, -1), h_at(2, i, -1)
        hyb, hzb = h_at(1, i - 1, 0), h_at(2, i - 1, 0)
        c = cs[pl.ds((x0 + i) * CB + y0, PB)]
        dyex, dyez = exu - ex, ezu - ez
        dxey, dxez = eyf - ey, ezf - ez
        dzex, dzey = z_next(ex) - ex, z_next(ey) - ey
        dyexb = exbu - exb
        dxeyd = eyfd - eyd
        szex, szey = z_prev(dzex), z_prev(dzey)
        averages(
            "x", o, ex, c,
            0.5 * dyex, hz - hzd - 0.5 * (ex - exd), 0.5 * (dxey - dxeyd),
            -0.5 * dzex, hy - z_prev(hy) + 0.5 * szex, 0.5 * (dxez - z_prev(dxez)),
            "y", "z",
        )
        averages(
            "y", o, ey, c,
            0.5 * dzey, hx - z_prev(hx) - 0.5 * szey, 0.5 * (dyez - z_prev(dyez)),
            -0.5 * dxey, hz - hzb + 0.5 * (ey - eyb), 0.5 * (dyex - dyexb),
            "z", "x",
        )
        dzexb = z_next(exb) - exb
        dzeyd = z_next(eyd) - eyd
        averages(
            "z", o, ez, c,
            0.5 * dxez, hy - hyb - 0.5 * (ez - ezb), 0.5 * (dzex - dzexb),
            -0.5 * dyez, hx - hxd + 0.5 * (ez - ezd), 0.5 * (dzey - dzeyd),
            "x", "y",
        )
        o.c = c
        o.h = (hx, hy, hz)
        o.d = (dyez, dzey, dzex, dxez, dxey, dyex)
        o.down = (exd, eyd, ezd, eyfd, hxd, hzd, dzeyd)
        o.up = (exu, ezu, e_at(1, i, 1))
        return o

    def ring_ahead(i):
        o = Cell()
        ey, ez = e_at(1, i, 0), e_at(2, i, 0)
        o.yx0 = o.ysx0 = ey
        o.zx0 = o.zsx0 = ez
        return o

    def ring_behind(o):
        ex, ey, ez = [e_at(k, -1, 0) for k in range(3)]
        h2zx = h_at(2, -1, 0) - 0.5 * (o.yx0 - ey) + 0.25 * (e_at(0, -1, 1) - ex)
        h2yx = h_at(1, -1, 0) - 0.25 * (z_next(ex) - ex) + 0.5 * (o.zx0 - ez)
        return h2zx, h2yx

    def stage_two(o, n, behind):
        hx, hy, hz = o.h
        dyez, dzey, dzex, dxez, dxey, dyex = o.d
        exd, eyd, ezd, eyfd, hxd, hzd, dzeyd = o.down
        exu, ezu, eyu = o.up
        h2zx_b, h2yx_b = behind
        xy0u = up(o.xy0, exu)
        zy0u = up(o.zy0, ezu)
        h2zy = hz - 0.25 * dxey + 0.5 * dyex - 0.25 * (n.ysx0 - o.ysx0) + 0.5 * (xy0u - o.xy1)
        h2zx = hz - 0.5 * dxey + 0.25 * dyex - 0.5 * (n.yx0 - o.yx1) + 0.25 * (up(o.xsy0, exu) - o.xsy0)
        h2xz = hx - 0.25 * dyez + 0.5 * dzey - 0.25 * (up(o.zsy0, ezu) - o.zsy0) + 0.5 * (z_next(o.yz0) - o.yz1)
        h2xy = hx - 0.5 * dyez + 0.25 * dzey - 0.5 * (zy0u - o.zy1) + 0.25 * (z_next(o.ysz0) - o.ysz0)
        h2yx = hy - 0.25 * dzex + 0.5 * dxez - 0.25 * (z_next(o.xsz0) - o.xsz0) + 0.5 * (n.zx0 - o.zx1)
        h2yz = hy - 0.5 * dzex + 0.25 * dxez - 0.5 * (z_next(o.xz0) - o.xz1) + 0.25 * (n.zsx0 - o.zsx0)
        h2zy_d = down(h2zy, hzd - 0.25 * (eyfd - eyd) + 0.5 * (o.xy0 - exd))
        h2xy_d = down(h2xy, hxd - 0.5 * (o.zy0 - ezd) + 0.25 * dzeyd)
        half = 0.5 * o.c
        ex = 0.5 * (o.xy0 + o.xy1) + half * (h2zy - h2zy_d - h2yz + z_prev(h2yz))
        ey = 0.5 * (o.yz0 + o.yz1) + half * (h2xz - z_prev(h2xz) - h2zx + h2zx_b)
        ez = 0.5 * (o.zx0 + o.zx1) + half * (h2yx - h2yx_b - h2xy + h2xy_d)
        hx = hx - 0.25 * (dyez - dzey + zy0u - o.zy0 - z_next(o.yz0) + o.yz0)
        hy = hy - 0.25 * (dzex - dxez + z_next(o.xz0) - o.xz0 - n.zx0 + o.zx0)
        hz = hz - 0.25 * (dxey - dyex + n.yx0 - o.yx0 - xy0u + o.xy0)
        return (ex, ey, ez), (hx, hy, hz), (h2zx, h2yx)

    now = stage_one(0)
    behind = ring_behind(now)
    for i in range(PB):
        later = stage_one(i + 1) if i < PB - 1 else ring_ahead(i + 1)
        e_new, h_new, behind = stage_two(now, later, behind)
        pending = (i, e_new, h_new)
        if i > 0:
            write(es, hs, x0, y0, previous)
        previous = pending
        now = later
    write(es, hs, x0, y0, previous)


def write(es, hs, x0, y0, item):
    i, e_new, h_new = item
    for k in range(3):
        es[k, pl.ds((x0 + i) * CB + y0, PB)] = e_new[k]
        hs[k, pl.ds((x0 + i + 1) * CB + y0, PB)] = h_new[k]


def second_kernel(owner, corner, spots, points, faces, halo, e_in, h_in, c_in, e_out, h_out, sampled, es, hs, cs, ye, yh, taken, slot_x, slot_y, count, sem):
    loads = [
        pltpu.make_async_copy(e_in, es.at[:, pl.ds(0, ROWS)], sem.at[0]),
        pltpu.make_async_copy(h_in, hs.at[:, pl.ds(CB, ROWS)], sem.at[1]),
        pltpu.make_async_copy(c_in, cs, sem.at[2]),
    ]
    for copy in loads:
        copy.start()
    me = lax.axis_index("gx") * GY + lax.axis_index("gy")

    def look(n, found):
        slot_x[found] = corner[0, n]
        slot_y[found] = corner[1, n]
        return jnp.minimum(found + (owner[n] == me).astype(jnp.int32), SLOTS)

    count[0] = lax.fori_loop(0, GX * GY, look, 0, unroll=8)
    for copy in loads:
        copy.wait()
    lane = lanes_of((1, CZ))

    def patches():
        def one(n, carry):
            patch(es, hs, cs, slot_x[n], slot_y[n])
            return carry

        lax.fori_loop(0, count[0], one, 0)

    def sample():
        e_rows = es.reshape(3 * (ROWS + CB), CZ)
        h_rows = hs.reshape(3 * (ROWS + CB), CZ)

        def one(n, carry):
            mask = lane == spots[0, n]
            k1, k2 = spots[1, n], spots[2, n]
            taken[pl.ds(n, 1)] = jnp.where(mask, h_rows[pl.ds(k1 + CB, 1)], 0.0)
            taken[pl.ds(n + SPB, 1)] = jnp.where(mask, h_rows[pl.ds(k2 + CB, 1)], 0.0)
            taken[pl.ds(n + 2 * SPB, 1)] = jnp.where(mask, e_rows[pl.ds(k1, 1)], 0.0)
            taken[pl.ds(n + 3 * SPB, 1)] = jnp.where(mask, e_rows[pl.ds(k2, 1)], 0.0)
            return carry

        lax.fori_loop(0, SPB, one, 0, unroll=16)
        high, low = split(taken[...])
        ones = jnp.ones((16, CZ), BF16)
        return dot_t(ones, high) + dot_t(ones, low)

    slots = points[...]
    face = faces[...]
    sign = jnp.where(slots >= 0, (2 * (face % 2) - 1).astype(F32), 0.0)
    for moment in range(2):
        if moment:
            place_halo(es, hs, halo, ye, yh)
            advance(es, hs, cs, ye, yh)
        patches()
        if moment:
            stores = [
                pltpu.make_async_copy(es.at[:, pl.ds(0, ROWS)], e_out, sem.at[0]),
                pltpu.make_async_copy(hs.at[:, pl.ds(CB, ROWS)], h_out, sem.at[1]),
            ]
            for copy in stores:
                copy.start()
        got = sample()
        got = [got[0:1, j * SPB : (j + 1) * SPB] for j in range(4)]
        sampled[4 * moment : 4 * moment + 1] = -sign * got[1]
        sampled[4 * moment + 1 : 4 * moment + 2] = sign * got[0]
        sampled[4 * moment + 2 : 4 * moment + 3] = sign * got[3]
        sampled[4 * moment + 3 : 4 * moment + 4] = -sign * got[2]
    cell = jnp.maximum(slots, 0)
    sampled[8:9] = (cell // (CB * CZ)).astype(F32)
    sampled[9:10] = (cell // CZ % CB).astype(F32)
    sampled[10:11] = (cell % CZ).astype(F32)
    sampled[11:12] = jnp.where(slots >= 0, face, 6).astype(F32)
    sampled[12:16] = jnp.zeros((4, SPB), F32)
    for copy in stores:
        copy.wait()


def third_kernel(omega, sampled, ta_in, tc_in, tb_in, far, got, gathered, ta, tc, tb, tcf, hot, hotz, spread_hi, spread_lo, lhs1, lhs2, lhsz, acc, rows48, send_buf, recv_buf, load_sem, send1, recv1, send2, recv2):
    gx = lax.axis_index("gx")
    gy = lax.axis_index("gy")
    loads = [
        pltpu.make_async_copy(ta_in, ta, load_sem.at[0]),
        pltpu.make_async_copy(tc_in, tc.at[:, pl.ds(0, 2 * ZF)], load_sem.at[1]),
        pltpu.make_async_copy(tc_in.at[:, pl.ds(0, ZF)], tc.at[:, pl.ds(2 * ZF, ZF)], load_sem.at[2]),
        pltpu.make_async_copy(tb_in, tb, load_sem.at[3]),
    ]
    for copy in loads:
        copy.start()
    barrier = pltpu.get_barrier_semaphore()
    for d in range(1, GX):
        pl.semaphore_signal(barrier, inc=1, device_id=(lax.rem(gx + d, GX), gy), device_id_type=MESH)
    for d in range(1, GY):
        pl.semaphore_signal(barrier, inc=1, device_id=(gx, lax.rem(gy + d, GY)), device_id_type=MESH)
    tc[:, 3 * ZF : 4 * ZF] = jnp.zeros((2, ZF, QF), BF16)
    pl.semaphore_wait(barrier, GX + GY - 2)
    first = []
    for d in range(1, GX):
        copy = pltpu.make_async_remote_copy(
            src_ref=sampled,
            dst_ref=gathered.at[GX - d],
            send_sem=send1.at[d],
            recv_sem=recv1.at[GX - d],
            device_id=(lax.rem(gx + d, GX), gy),
            device_id_type=MESH,
        )
        copy.start()
        first.append(copy)
    gathered[0] = sampled[...]
    for copy in loads:
        copy.wait()
    tcf[...] = tc[:, 0:ZF].astype(F32) + tc[:, ZF : 2 * ZF].astype(F32)
    for copy in first:
        copy.wait()

    for b in range(GX):
        lanes = slice(b * SPB, (b + 1) * SPB)
        got[0:16, lanes] = gathered[b]
        block = lax.rem(gx + b, GX)
        x = gathered[b, 8:9] + (block * CB).astype(F32)
        z = gathered[b, 10:11]
        got[12:13, lanes] = jnp.where(x < 128.0, 127.0 - x, x - 128.0)
        got[13:14, lanes] = jnp.where(x < 128.0, -1.0, 1.0)
        got[14:15, lanes] = jnp.where(z < 64.0, 63.0 - z, z - 64.0)
        got[15:16, lanes] = jnp.where(z < 64.0, -1.0, 1.0)

    def one_hot(to, place_row, sign_row, count, blocks):
        for b, start in enumerate(blocks):
            lanes = pl.ds(start, SPB)
            there = slice(b * SPB, (b + 1) * SPB)
            where_at = jnp.broadcast_to(got[place_row : place_row + 1, lanes], (16, SPB))
            sign = jnp.broadcast_to(got[sign_row : sign_row + 1, lanes], (16, SPB))
            at = rows_of((16, SPB)).astype(F32)
            for j in range(0, count, 16):
                same = at + float(j) == where_at
                to[j : j + 16, there] = jnp.where(same, 1.0, 0.0).astype(BF16)
                to[count + j : count + j + 16, there] = jnp.where(same, sign, 0.0).astype(BF16)

    def spread(v, key, start, step, first_row, there, count):
        high, low = split(v)
        key = key.astype(BF16)
        zero = jnp.zeros_like(high)

        def one(n, carry):
            same = key == jnp.full((16, SPB), (start + step * n).astype(F32), F32).astype(BF16)
            at = pl.ds(pl.multiple_of(first_row + n * 16, 16), 16)
            spread_hi[at, there] = jnp.where(same, high, zero)
            spread_lo[at, there] = jnp.where(same, low, zero)
            return carry

        lax.fori_loop(0, count, one, 0, unroll=8)

    def row16(row, lanes):
        return jnp.broadcast_to(got[row : row + 1, lanes], (16, SPB))

    upper = rows_of((16, SPB)) // 8
    every = [b * SPB for b in range(GX)]
    ends = [pl.multiple_of(lax.rem(GX - gx, GX) * SPB, SPB), pl.multiple_of((GX - 1 - gx) * SPB, SPB)]

    def twice(lanes):
        v = got[0:8, lanes]
        return jnp.concatenate([v, v], axis=0)

    def spread_z(y_low, count):
        wanted = (4 + upper).astype(F32)
        for b in range(GX):
            lanes = slice(b * SPB, (b + 1) * SPB)
            v = jnp.where(row16(11, lanes) == wanted, twice(lanes), 0.0)
            spread(v, row16(9, lanes), y_low, 1, 0, lanes, count)

    def spread_x(y_low, count):
        for e, start in enumerate(ends):
            lanes = pl.ds(start, SPB)
            wanted = jnp.where(upper == e, float(e), -1.0)
            v = jnp.where(row16(11, lanes) == wanted, twice(lanes), 0.0)
            spread(v, row16(9, lanes), y_low, 1, 0, slice(e * SPB, (e + 1) * SPB), count)

    def spread_y():
        for b in range(GX):
            lanes = slice(b * SPB, (b + 1) * SPB)
            face = row16(11, lanes)
            v = jnp.where((face == 2.0) | (face == 3.0), twice(lanes), 0.0)
            spread(v, row16(10, lanes) - upper.astype(F32), 16, 2, 0, lanes, YF_ROWS // 2)

    def dense(to, rows):
        for m in range(0, rows, CHUNK):
            d = dot_t(spread_hi[m : m + CHUNK], hot[...]) + dot_t(spread_lo[m : m + CHUNK], hot[...])
            for k in range(2):
                high, low = split(d[:, k * XF : (k + 1) * XF])
                lhs1[k, to + m : to + m + CHUNK, 0:XF] = high
                lhs1[k, to + m : to + m + CHUNK, XF : 2 * XF] = high
                lhs2[k, to + m : to + m + CHUNK] = low

    def dense_x(rows):
        for m in range(0, rows, CHUNK):
            at = slice(m, m + CHUNK)
            d = dot_t(spread_hi[at, 0 : 2 * SPB], hotz[...]) + dot_t(spread_lo[at, 0 : 2 * SPB], hotz[...])
            for k in range(2):
                high, low = split(d[:, k * ZF : (k + 1) * ZF])
                lhsz[k, at] = jnp.concatenate([high, high, low, jnp.zeros_like(low)], axis=1)

    def times_x(to, lanes):
        out = []
        for k in range(2):
            table = ta[k, :, lanes]
            out.append(dot(lhs1[k, to : to + CHUNK], table) + dot(lhs2[k, to : to + CHUNK], table[0:XF]))
        return out

    def times_z(to, lanes):
        return [dot(lhsz[k, to : to + CHUNK], tc[k, :, lanes]) for k in range(2)]

    def outer_y(g, total, y_low, lanes):
        re, im = total
        for y in range(16):
            at = slice(y * 16, (y + 1) * 16)
            bc, bs = tb[0, pl.ds(y_low + y, 1), lanes], tb[1, pl.ds(y_low + y, 1), lanes]
            re = re + (bc * g[0][at] - bs * g[1][at])
            im = im + (bc * g[1][at] + bs * g[0][at])
        return re, im

    def outer_z(g, total, z_low, lanes):
        re, im = total
        for o in range(CHUNK // 8):
            z = z_low + o
            j, sign = (z - 64, 1.0) if z >= 64 else (63 - z, -1.0)
            at = slice(o * 8, (o + 1) * 8)
            cc, cs = tcf[0, j : j + 1, lanes], sign * tcf[1, j : j + 1, lanes]
            re = re + (cc * g[0][at] - cs * g[1][at])
            im = im + (cc * g[1][at] + cs * g[0][at])
        return re, im

    def keep(base, total, lanes):
        n = total[0].shape[0]
        acc[base, 0, 0:n, lanes] = total[0]
        acc[base, 1, 0:n, lanes] = total[1]

    edge = (gy == 0) | (gy == GY - 1)
    zero16 = jnp.zeros((16, CHUNK), F32)
    zero8 = jnp.zeros((8, CHUNK), F32)
    one_hot(hot, 12, 13, XF, every)
    one_hot(hotz, 14, 15, ZF, ends)
    @pl.when(jnp.logical_not(edge))
    def _():
        spread_z(0, CB)
        dense(0, CB * 16)
        spread_x(0, CB)
        dense_x(CB * 16)
        acc[2] = jnp.zeros((2, 16, QF), F32)

        def chunk(n, carry):
            lanes = pl.ds(pl.multiple_of(n * CHUNK, CHUNK), CHUNK)
            total = (zero16, zero16)
            for y in range(2):
                total = outer_y(times_x(y * CHUNK, lanes), total, y * 16, lanes)
            keep(0, total, lanes)
            total = (zero16, zero16)
            for y in range(2):
                total = outer_y(times_z(y * CHUNK, lanes), total, y * 16, lanes)
            keep(1, total, lanes)
            return carry

        lax.fori_loop(0, QF // CHUNK, chunk, 0)

    @pl.when(edge)
    def _():
        y_low = jnp.where(gy == 0, 16, 0)
        spread_z(y_low, 16)
        dense(0, CHUNK)
        spread_x(y_low, 16)
        dense_x(CHUNK)
        spread_y()
        dense(CHUNK, YF_ROWS * 8)

        def chunk(n, carry):
            lanes = pl.ds(pl.multiple_of(n * CHUNK, CHUNK), CHUNK)
            keep(0, outer_y(times_x(0, lanes), (zero16, zero16), y_low, lanes), lanes)
            keep(1, outer_y(times_z(0, lanes), (zero16, zero16), y_low, lanes), lanes)
            total = (zero8, zero8)
            for z in range(0, YF_ROWS, CHUNK // 8):
                total = outer_z(times_x(CHUNK + z * 8, lanes), total, z + 16, lanes)
            keep(2, total, lanes)
            return carry

        lax.fori_loop(0, QF // CHUNK, chunk, 0)

    scale = 1.0 / math.sqrt(GX * GY * SPB)
    y_face = jnp.where(gy == 0, 16, 15)
    moment = 1.0 + (rows_of((8, 1)) // 4).astype(F32)
    for f in range(FREQ):
        lanes = slice(f * QN, (f + 1) * QN)
        mc, ms = turn(omega[f] * (1.0 / (2.0 * math.pi)) * moment)
        mc, ms = mc * scale, ms * scale

        def both(base, c, s):
            low_re, high_re = acc[base, 0, 0:8, lanes], acc[base, 0, 8:16, lanes]
            low_im, high_im = acc[base, 1, 0:8, lanes], acc[base, 1, 8:16, lanes]
            re = c * (low_re + high_re) + s * (low_im - high_im)
            im = c * (low_im + high_im) + s * (high_re - low_re)
            return re, im

        def late(re, im):
            a, b = mc * re + ms * im, mc * im - ms * re
            return a[0:4] + a[4:8], b[0:4] + b[4:8]

        zf = late(*both(0, tcf[0, Z_FACE : Z_FACE + 1, lanes], tcf[1, Z_FACE : Z_FACE + 1, lanes]))
        xf = late(*both(1, tb[0, CB : CB + 1, lanes], tb[1, CB : CB + 1, lanes]))
        c, s = tb[0, pl.ds(y_face, 1), lanes], tb[1, pl.ds(y_face, 1), lanes]
        re, im = acc[2, 0, 0:8, lanes], acc[2, 1, 0:8, lanes]
        yf = late(c * re - s * im, c * im + s * re)
        for k in range(2):
            z4, x4, y4 = zf[k], xf[k], yf[k]
            six = [
                z4[0:1] + y4[1:2], z4[1:2] + x4[0:1], x4[1:2] + y4[0:1],
                z4[2:3] + y4[3:4], z4[3:4] + x4[2:3], x4[3:4] + y4[2:3],
            ]
            for j, v in enumerate(six):
                rows48[12 * f + 6 * k + j : 12 * f + 6 * k + j + 1] = v
    rows48[48:128] = jnp.zeros((80, QN), F32)
    for t in range(0, QN, 128):
        turned = jnp.transpose(rows48[:, t : t + 128])
        for q in range(0, 128, OWN):
            at = (t + q) // 2
            second_half = pltpu.roll(turned[q + HALF : q + OWN], 64, 1)
            send_buf[at : at + HALF] = turned[q : q + HALF] + second_half

    second = []
    for d in range(1, GY):
        to = lax.rem(gy + d, GY)
        copy = pltpu.make_async_remote_copy(
            src_ref=send_buf.at[pl.ds(pl.multiple_of(to * HALF, HALF), HALF)],
            dst_ref=recv_buf.at[GY - d],
            send_sem=send2.at[d],
            recv_sem=recv2.at[GY - d],
            device_id=(gx, to),
            device_id_type=MESH,
        )
        copy.start()
        second.append(copy)
    total = send_buf[pl.ds(pl.multiple_of(gy * HALF, HALF), HALF)]
    for copy in second:
        copy.wait()
    for d in range(1, GY):
        total = total + recv_buf[d]
    far[0:HALF] = total[:, 0:48]
    far[HALF:OWN] = pltpu.roll(total, 64, 1)[:, 0:48]


VMEM = pl.BlockSpec(memory_space=pltpu.VMEM)
SMEM = pl.BlockSpec(memory_space=pltpu.SMEM)
ANY = pl.BlockSpec(memory_space=pl.ANY)


def local(efield, hfield, e_coef, omega, patch_owner, patch_corner, surface_points, surface_faces, angle_index):
    field = jax.ShapeDtypeStruct((3, ROWS, CZ), F32)
    fields = [
        pltpu.VMEM((3, ROWS + CB, CZ), F32),
        pltpu.VMEM((3, ROWS + CB, CZ), F32),
        pltpu.VMEM((ROWS, CZ), F32),
        pltpu.VMEM((2, CB, CZ), F32),
        pltpu.VMEM((2, CB, CZ), F32),
    ]
    coef = e_coef.reshape(ROWS, CZ)
    points = surface_points.reshape(1, SPB)
    faces = surface_faces.reshape(1, SPB)
    efield, hfield, halo, *tabled, spots = pl.pallas_call(
        first_kernel,
        out_shape=(
            field,
            field,
            jax.ShapeDtypeStruct((9, CB, CZ), F32),
            jax.ShapeDtypeStruct((2, 2 * XF, QF), BF16),
            jax.ShapeDtypeStruct((2, 2 * ZF, QF), BF16),
            jax.ShapeDtypeStruct((2, CB + 8, QF), F32),
            jax.ShapeDtypeStruct((8, SPB), jnp.int32),
        ),
        in_specs=[SMEM, VMEM, VMEM, VMEM, ANY, ANY, ANY],
        out_specs=(ANY, ANY, VMEM, ANY, ANY, ANY, VMEM),
        scratch_shapes=[
            pltpu.VMEM((8, QF), F32),
            pltpu.VMEM((2, 2 * XF, QF), BF16),
            pltpu.VMEM((2, 2 * ZF, QF), BF16),
            pltpu.VMEM((2, CB + 8, QF), F32),
        ]
        + fields
        + [
            pltpu.VMEM((2, 9, CB, CZ), F32),
            pltpu.VMEM((9, CB, CZ), F32),
            pltpu.SemaphoreType.DMA((6,)),
            pltpu.SemaphoreType.DMA((2, 6)),
            pltpu.SemaphoreType.DMA((2, 6)),
        ],
        compiler_params=pltpu.CompilerParams(collective_id=0, has_side_effects=True, vmem_limit_bytes=56 * 2**20),
        name="first_step",
    )(omega, angle_index.T, points, faces, efield.reshape(3, ROWS, CZ), hfield.reshape(3, ROWS, CZ), coef)
    efield, hfield, sampled = pl.pallas_call(
        second_kernel,
        out_shape=(field, field, jax.ShapeDtypeStruct((16, SPB), F32)),
        in_specs=[SMEM, SMEM, SMEM, VMEM, VMEM, VMEM, ANY, ANY, ANY],
        out_specs=(ANY, ANY, VMEM),
        scratch_shapes=fields
        + [
            pltpu.VMEM((4 * SPB, CZ), F32),
            pltpu.SMEM((SLOTS + 1,), jnp.int32),
            pltpu.SMEM((SLOTS + 1,), jnp.int32),
            pltpu.SMEM((1,), jnp.int32),
            pltpu.SemaphoreType.DMA((3,)),
        ],
        compiler_params=pltpu.CompilerParams(vmem_limit_bytes=56 * 2**20),
        name="patches",
    )(patch_owner, patch_corner.T, spots, points, faces, halo, efield, hfield, coef)
    far = pl.pallas_call(
        third_kernel,
        out_shape=jax.ShapeDtypeStruct((OWN, 48), F32),
        in_specs=[SMEM, VMEM, ANY, ANY, ANY],
        out_specs=VMEM,
        scratch_shapes=[
            pltpu.VMEM((16, GX * SPB), F32),
            pltpu.VMEM((GX, 16, SPB), F32),
            pltpu.VMEM((2, 2 * XF, QF), BF16),
            pltpu.VMEM((2, 4 * ZF, QF), BF16),
            pltpu.VMEM((2, CB + 8, QF), F32),
            pltpu.VMEM((2, ZF, QF), F32),
            pltpu.VMEM((2 * XF, GX * SPB), BF16),
            pltpu.VMEM((2 * ZF, 2 * SPB), BF16),
            pltpu.VMEM((YF_ROWS * 8, GX * SPB), BF16),
            pltpu.VMEM((YF_ROWS * 8, GX * SPB), BF16),
            pltpu.VMEM((2, YF_ROWS * 8 + CHUNK, 2 * XF), BF16),
            pltpu.VMEM((2, YF_ROWS * 8 + CHUNK, XF), BF16),
            pltpu.VMEM((2, CB * 16, 4 * ZF), BF16),
            pltpu.VMEM((3, 2, 16, QF), F32),
            pltpu.VMEM((128, QN), F32),
            pltpu.VMEM((QN // 2, 128), F32),
            pltpu.VMEM((GY, HALF, 128), F32),
            pltpu.SemaphoreType.DMA((4,)),
            pltpu.SemaphoreType.DMA((GX,)),
            pltpu.SemaphoreType.DMA((GX,)),
            pltpu.SemaphoreType.DMA((GY,)),
            pltpu.SemaphoreType.DMA((GY,)),
        ],
        compiler_params=pltpu.CompilerParams(collective_id=1, has_side_effects=True, vmem_limit_bytes=44 * 2**20),
        name="projection",
    )(omega, sampled, *tabled)
    shape = (3, CB, CB, CZ)
    return efield.reshape(shape), hfield.reshape(shape), far


def solution(mesh):
    placed = (
        P(None, "gx", "gy", None),
        P(None, "gx", "gy", None),
        P("gx", "gy", None),
        P(),
        P(),
        P(),
        P("gx", "gy", None),
        P("gx", "gy", None),
        P(),
    )
    return jax.shard_map(
        local,
        mesh=mesh,
        in_specs=placed,
        out_specs=(P(None, "gx", "gy", None), P(None, "gx", "gy", None), P(("gx", "gy"), None)),
        check_vma=False,
    )
```

```python
import math

import jax
import jax.numpy as jnp
import numpy as np
from jax import lax
from jax.experimental import pallas as pl
from jax.experimental.pallas import tpu as pltpu
from jax.sharding import PartitionSpec as P

PB = 8
SLOTS = 4
NTH = 128
NPH = 256
CB = 32
CZ = 128
ROWS = CB * CB
SPB = 256
FREQ = 4
GX = 8
GY = 16
ANG = 4096
QN = ANG // GX
QF = QN * FREQ
OWN = ANG // (GX * GY)
HALF = OWN // 2
MESH = pl.DeviceIdType.MESH
F32 = jnp.float32
BF16 = jnp.bfloat16


def lanes_of(shape):
    return lax.broadcasted_iota(jnp.int32, shape, 1)


def rows_of(shape):
    return lax.broadcasted_iota(jnp.int32, shape, 0)


def z_next(v):
    return jnp.where(lanes_of(v.shape) == CZ - 1, 0.0, pltpu.roll(v, CZ - 1, 1))


def z_prev(v):
    return jnp.where(lanes_of(v.shape) == 0, 0.0, pltpu.roll(v, 1, 1))


def y_next(v, edge):
    n = v.shape[0]
    return jnp.where(rows_of(v.shape) == n - 1, edge, pltpu.roll(v, n - 1, 0))


def y_prev(v, edge):
    return jnp.where(rows_of(v.shape) == 0, edge, pltpu.roll(v, 1, 0))


def prepare(es, hs, out):
    out[0] = es[1, 0:CB]
    out[1] = es[2, 0:CB]
    last = (CB - 1) * CB
    ex, ey, ez = [es[k, last : last + CB] for k in range(3)]
    hy, hz = [hs[k, last + CB : last + 2 * CB] for k in (1, 2)]
    out[2] = hy - 0.5 * (z_next(ex) - ex + ez)
    out[3] = hz + 0.5 * (ey + y_next(ex, 0.0) - ex)
    out[8, 8:16] = ey[CB - 8 : CB] * 0.0 + es[1, CB - 1 : CB]
    out[8, 0:8] = ex[0:1] + jnp.zeros((8, CZ), F32)
    out[8, 16:32] = jnp.zeros((16, CZ), F32)
    out[4] = es[0, pl.ds(0, CB, stride=CB)]
    out[5] = es[2, pl.ds(0, CB, stride=CB)]
    ex, ey, ez = [es[k, pl.ds(CB - 1, CB, stride=CB)] for k in range(3)]
    hx, hz = [hs[k, pl.ds(2 * CB - 1, CB, stride=CB)] for k in (0, 2)]
    out[6] = hx + 0.5 * (ez + z_next(ey) - ey)
    out[7] = hz - 0.5 * (y_next(ey, 0.0) - ey + ex)


def place_halo(es, hs, halo, ye, yh):
    gx = lax.axis_index("gx")
    gy = lax.axis_index("gy")
    x_low = (gx > 0).astype(F32)
    x_high = (gx < GX - 1).astype(F32)
    y_low = (gy > 0).astype(F32)
    y_high = (gy < GY - 1).astype(F32)
    last_row = rows_of((CB, CZ)) == CB - 1
    es[1, ROWS : ROWS + CB] = halo[0] * x_high
    es[2, ROWS : ROWS + CB] = halo[1] * x_high
    ye[0] = halo[4] * y_high
    ye[1] = halo[5] * y_high
    corner = jnp.where(last_row, halo[8, 0:1] * (0.5 * y_high), 0.0)
    hs[1, 0:CB] = x_low * (halo[2] + 0.5 * es[2, 0:CB])
    hs[2, 0:CB] = x_low * (halo[3] - 0.5 * es[1, 0:CB] + corner)
    corner = jnp.where(last_row, halo[8, 8:9] * (0.5 * x_high), 0.0)
    yh[0] = y_low * (halo[6] - 0.5 * es[2, pl.ds(0, CB, stride=CB)])
    yh[1] = y_low * (halo[7] + 0.5 * es[0, pl.ds(0, CB, stride=CB)] - corner)


def add_halo(es, hs, cs, halo, own):
    gx = lax.axis_index("gx")
    gy = lax.axis_index("gy")
    x_low = (gx > 0).astype(F32)
    x_high = (gx < GX - 1).astype(F32)
    y_low = (gy > 0).astype(F32)
    y_high = (gy < GY - 1).astype(F32)
    last_row = rows_of((CB, CZ)) == CB - 1
    low_rows = pl.ds(0, CB, stride=CB)
    high_rows = pl.ds(CB - 1, CB, stride=CB)
    h_rows = pl.ds(2 * CB - 1, CB, stride=CB)
    plane = slice(ROWS - CB, ROWS)
    dy, dz = 0.5 * x_high * halo[1], -0.5 * x_high * halo[0]
    hs[1, ROWS : ROWS + CB] += dy
    hs[2, ROWS : ROWS + CB] += dz
    c = cs[plane]
    es[0, plane] += c * (dz - y_prev(dz, 0.0) - dy + z_prev(dy))
    es[1, plane] -= c * dz
    es[2, plane] += c * dy
    dx, dz = -0.5 * y_high * halo[5], 0.5 * y_high * halo[4]
    hs[0, h_rows] = hs[0, h_rows] + dx
    hs[2, h_rows] = hs[2, h_rows] + dz
    c = cs[high_rows]
    es[0, high_rows] = es[0, high_rows] + c * dz
    es[1, high_rows] = es[1, high_rows] + c * (dx - z_prev(dx) - dz + y_prev(dz, 0.0))
    es[2, high_rows] = es[2, high_rows] - c * dx
    corner = jnp.where(last_row, halo[8, 0:1] * (0.5 * y_high), 0.0)
    before_y = x_low * (halo[2] + 0.5 * own[1])
    before_z = x_low * (halo[3] - 0.5 * own[0] + corner)
    c = cs[0:CB]
    es[1, 0:CB] += c * before_z
    es[2, 0:CB] -= c * before_y
    corner = jnp.where(last_row, halo[8, 8:9] * (0.5 * x_high), 0.0)
    before_x = y_low * (halo[6] - 0.5 * own[5])
    before_z = y_low * (halo[7] + 0.5 * own[4] - corner)
    c = cs[low_rows]
    es[0, low_rows] = es[0, low_rows] - c * before_z
    es[2, low_rows] = es[2, low_rows] + c * before_x


def advance(es, hs, cs, ye, yh):
    last = rows_of((CB, CZ)) == CB - 1
    for x in range(CB):
        r = x * CB
        here, after = slice(r, r + CB), slice(r + CB, r + 2 * CB)
        ex, ey, ez = [es[k, here] for k in range(3)]
        ey1, ez1 = es[1, after], es[2, after]
        hx, hy, hz = [hs[k, after] for k in range(3)]
        if x == 0:
            hy0, hz0 = hs[1, here], hs[2, here]
        exu = jnp.where(last, ye[0, x : x + 1], es[0, r + 1 : r + CB + 1])
        ezu = jnp.where(last, ye[1, x : x + 1], es[2, r + 1 : r + CB + 1])
        hx = hx - 0.5 * (ezu - ez - z_next(ey) + ey)
        hy = hy - 0.5 * (z_next(ex) - ex - ez1 + ez)
        hz = hz - 0.5 * (ey1 - ey - exu + ex)
        for k, v in enumerate((hx, hy, hz)):
            hs[k, after] = v
        c = cs[here]
        ex = ex + c * (hz - y_prev(hz, yh[1, x : x + 1]) - hy + z_prev(hy))
        ey = ey + c * (hx - z_prev(hx) - hz + hz0)
        ez = ez + c * (hy - hy0 - hx + y_prev(hx, yh[0, x : x + 1]))
        for k, v in enumerate((ex, ey, ez)):
            es[k, here] = v
        hy0, hz0 = hy, hz


def neighbours():
    gx = lax.axis_index("gx")
    gy = lax.axis_index("gy")
    xn, xp = lax.rem(gx + 1, GX), lax.rem(gx + GX - 1, GX)
    yn, yp = lax.rem(gy + 1, GY), lax.rem(gy + GY - 1, GY)
    return [(xp, gy), (xn, gy), (gx, yp), (gx, yn), (xn, yp), (xp, yn)]


def pieces(ref, n):
    if n < 4:
        return ref.at[pl.ds(2 * n, 2)]
    return ref.at[8, pl.ds(8 * (n - 4), 8)]


def fitted(function, degrees, points=4001):
    r = np.cos(np.linspace(0.0, np.pi, points)) * 0.5
    basis = np.stack([r**d for d in degrees], axis=1)
    return [float(v) for v in np.linalg.lstsq(basis, function(np.pi * r) * math.sqrt(2.0), rcond=None)[0]]


SIN = fitted(np.sin, (1, 3, 5, 7, 9))
COS = fitted(np.cos, (0, 2, 4, 6, 8))


def turn(t):
    r = t - jnp.round(t)
    r2 = r * r
    s = r * (SIN[0] + r2 * (SIN[1] + r2 * (SIN[2] + r2 * (SIN[3] + r2 * SIN[4]))))
    c = COS[0] + r2 * (COS[1] + r2 * (COS[2] + r2 * (COS[3] + r2 * COS[4])))
    return 1.0 - s * s, s * c


def split(v):
    high = v.astype(BF16)
    return high, (v - high.astype(F32)).astype(BF16)


def dot(a, b):
    return jnp.dot(a, b, preferred_element_type=F32)


def dot_t(a, b):
    return lax.dot_general(a, b, (((1,), (1,)), ((), ())), preferred_element_type=F32)


CUT1 = 2
CUT2 = 5
XF = 128
ZF = 64
YF_ROWS = 96
CHUNK = 256
X_FACE = 111
Z_FACE = 47


def directions(omega, angles, kdir):
    index = angles[:, pl.ds(pl.multiple_of(lax.axis_index("gx") * QN, QN), QN)].astype(F32)
    theta = math.pi * (index[0:1] + 0.5) / NTH
    phi = 2.0 * math.pi * (index[1:2] + 0.5) / NPH
    st, ct = jnp.sin(theta), jnp.cos(theta)
    sp, cp = jnp.sin(phi), jnp.cos(phi)
    for f in range(FREQ):
        w = omega[f] * (1.0 / (2.0 * math.pi))
        lanes = slice(f * QN, (f + 1) * QN)
        kdir[0:1, lanes] = st * cp * w
        kdir[1:2, lanes] = st * sp * w
        kdir[2:3, lanes] = ct * w


def tables(kdir, ta, tc, tb, n):
    y_start = (lax.axis_index("gy") * CB).astype(F32) + (0.5 - CB * GY / 2.0)
    lanes = pl.ds(pl.multiple_of(n * CHUNK, CHUNK), CHUNK)
    kx, ky, kz = kdir[0:1, lanes], kdir[1:2, lanes], kdir[2:3, lanes]
    count = rows_of((16, CHUNK)).astype(F32)
    for j in range(0, XF, 16):
        for k, v in enumerate(turn((count + (j + 0.5)) * kx)):
            high, low = split(v)
            ta[k, j : j + 16, lanes] = high
            ta[k, XF + j : XF + j + 16, lanes] = low
    for j in range(0, ZF, 16):
        for k, v in enumerate(turn((count + (j + 0.5)) * kz)):
            high, low = split(v)
            tc[k, j : j + 16, lanes] = high
            tc[k, ZF + j : ZF + j + 16, lanes] = low
    for j in range(0, CB, 16):
        for k, v in enumerate(turn((count + (y_start + j)) * ky)):
            tb[k, j : j + 16, lanes] = v
    for k, v in enumerate(turn(jnp.full((8, CHUNK), X_FACE + 0.5, F32) * kx)):
        tb[k, CB : CB + 8, lanes] = v


def first_kernel(omega, angles, points, faces, e_in, h_in, c_in, e_out, h_out, halo2, ta_out, tc_out, tb_out, spots, kdir, ta, tc, tb, es, hs, cs, ye, yh, sent, halo1, local_sem, send_sem, recv_sem):
    loads = [
        pltpu.make_async_copy(e_in, es.at[:, pl.ds(0, ROWS)], local_sem.at[0]),
        pltpu.make_async_copy(h_in, hs.at[:, pl.ds(CB, ROWS)], local_sem.at[1]),
        pltpu.make_async_copy(c_in, cs, local_sem.at[2]),
    ]
    for copy in loads:
        copy.start()
    barrier = pltpu.get_barrier_semaphore()
    for device in neighbours():
        pl.semaphore_signal(barrier, inc=1, device_id=device, device_id_type=MESH)
    directions(omega, angles, kdir)
    cell = jnp.maximum(points[...], 0)
    normal = lax.shift_right_logical(faces[...], 1)
    row = lax.shift_right_logical(cell, 7)
    spots[0:1] = cell & (CZ - 1)
    spots[1:2] = jnp.where(normal == 2, 0, normal + 1) * (ROWS + CB) + row
    spots[2:3] = jnp.where(normal == 0, 2, normal - 1) * (ROWS + CB) + row
    spots[3:8] = jnp.zeros((5, SPB), jnp.int32)

    def some_tables(low, high):
        def one(n, carry):
            tables(kdir, ta, tc, tb, n)
            return carry

        lax.fori_loop(low, high, one, 0)

    some_tables(0, CUT1)
    loads[0].wait()
    loads[1].wait()

    def exchange(number, halo):
        copies = []
        for n, device in enumerate(neighbours()):
            copy = pltpu.make_async_remote_copy(
                src_ref=pieces(sent.at[number], n),
                dst_ref=pieces(halo, n),
                send_sem=send_sem.at[number, n],
                recv_sem=recv_sem.at[number, n],
                device_id=device,
                device_id_type=MESH,
            )
            copy.start()
            copies.append(copy)
        return copies

    prepare(es, hs, sent.at[0])
    pl.semaphore_wait(barrier, 6)
    copies = exchange(0, halo1)
    for k in (1, 2):
        es[k, ROWS : ROWS + CB] = jnp.zeros((CB, CZ), F32)
        hs[k, 0:CB] = jnp.zeros((CB, CZ), F32)
    ye[...] = jnp.zeros_like(ye)
    yh[...] = jnp.zeros_like(yh)
    loads[2].wait()
    advance(es, hs, cs, ye, yh)
    some_tables(CUT1, CUT2)
    for copy in copies:
        copy.wait()
    add_halo(es, hs, cs, halo1, sent.at[0])
    prepare(es, hs, sent.at[1])
    copies = exchange(1, halo2)
    stores = [
        pltpu.make_async_copy(es.at[:, pl.ds(0, ROWS)], e_out, local_sem.at[0]),
        pltpu.make_async_copy(hs.at[:, pl.ds(CB, ROWS)], h_out, local_sem.at[1]),
    ]
    for copy in stores:
        copy.start()
    some_tables(CUT2, QF // CHUNK)
    for n, (table, out) in enumerate(((ta, ta_out), (tc, tc_out), (tb, tb_out))):
        copy = pltpu.make_async_copy(table, out, local_sem.at[2 + n])
        copy.start()
        stores.append(copy)
    for copy in copies + stores:
        copy.wait()


def patch(es, hs, cs, x0, y0):
    first = rows_of((PB, CZ)) == 0
    final = rows_of((PB, CZ)) == PB - 1

    def e_at(k, i, j):
        return es[k, pl.ds((x0 + i) * CB + y0 + j, PB)]

    def h_at(k, i, j):
        return hs[k, pl.ds((x0 + i + 1) * CB + y0 + j, PB)]

    def up(v, edge):
        return jnp.where(final, edge, pltpu.roll(v, PB - 1, 0))

    def down(v, edge):
        return jnp.where(first, edge, pltpu.roll(v, 1, 0))

    class Cell:
        pass

    def averages(name, o, e, c, u1, u0, wu, v1, v0, wv, pa, pb):
        vm = 0.5 * (v0 + v1)
        um = 0.5 * (u0 + u1)
        qu = 0.25 * wu
        qv = 0.25 * wv
        base_a = e - c * (vm + qv)
        base_b = e + c * (um - qu)
        setattr(o, name + pa + "1", base_a + c * u1)
        setattr(o, name + pa + "0", base_a + c * (u0 - 0.5 * wu))
        setattr(o, name + pb + "1", base_b - c * v1)
        setattr(o, name + pb + "0", base_b - c * (v0 + 0.5 * wv))
        setattr(o, name + "s" + pa + "0", e + c * (u0 - wu - vm - 0.5 * wv))
        setattr(o, name + "s" + pb + "0", e + c * (um - 0.5 * wu - v0 - wv))

    def stage_one(i):
        o = Cell()
        ex, ey, ez = [e_at(k, i, 0) for k in range(3)]
        exu, ezu = e_at(0, i, 1), e_at(2, i, 1)
        exd, eyd, ezd = [e_at(k, i, -1) for k in range(3)]
        exf, eyf, ezf = [e_at(k, i + 1, 0) for k in range(3)]
        eyb, ezb = e_at(1, i - 1, 0), e_at(2, i - 1, 0)
        exbu, exb = e_at(0, i - 1, 1), e_at(0, i - 1, 0)
        eyfd = e_at(1, i + 1, -1)
        hx, hy, hz = [h_at(k, i, 0) for k in range(3)]
        hxd, hzd = h_at(0, i, -1), h_at(2, i, -1)
        hyb, hzb = h_at(1, i - 1, 0), h_at(2, i - 1, 0)
        c = cs[pl.ds((x0 + i) * CB + y0, PB)]
        dyex, dyez = exu - ex, ezu - ez
        dxey, dxez = eyf - ey, ezf - ez
        dzex, dzey = z_next(ex) - ex, z_next(ey) - ey
        dyexb = exbu - exb
        dxeyd = eyfd - eyd
        szex, szey = z_prev(dzex), z_prev(dzey)
        averages(
            "x", o, ex, c,
            0.5 * dyex, hz - hzd - 0.5 * (ex - exd), 0.5 * (dxey - dxeyd),
            -0.5 * dzex, hy - z_prev(hy) + 0.5 * szex, 0.5 * (dxez - z_prev(dxez)),
            "y", "z",
        )
        averages(
            "y", o, ey, c,
            0.5 * dzey, hx - z_prev(hx) - 0.5 * szey, 0.5 * (dyez - z_prev(dyez)),
            -0.5 * dxey, hz - hzb + 0.5 * (ey - eyb), 0.5 * (dyex - dyexb),
            "z", "x",
        )
        dzexb = z_next(exb) - exb
        dzeyd = z_next(eyd) - eyd
        averages(
            "z", o, ez, c,
            0.5 * dxez, hy - hyb - 0.5 * (ez - ezb), 0.5 * (dzex - dzexb),
            -0.5 * dyez, hx - hxd + 0.5 * (ez - ezd), 0.5 * (dzey - dzeyd),
            "x", "y",
        )
        o.c = c
        o.h = (hx, hy, hz)
        o.d = (dyez, dzey, dzex, dxez, dxey, dyex)
        o.down = (exd, eyd, ezd, eyfd, hxd, hzd, dzeyd)
        o.up = (exu, ezu, e_at(1, i, 1))
        return o

    def ring_ahead(i):
        o = Cell()
        ey, ez = e_at(1, i, 0), e_at(2, i, 0)
        o.yx0 = o.ysx0 = ey
        o.zx0 = o.zsx0 = ez
        return o

    def ring_behind(o):
        ex, ey, ez = [e_at(k, -1, 0) for k in range(3)]
        h2zx = h_at(2, -1, 0) - 0.5 * (o.yx0 - ey) + 0.25 * (e_at(0, -1, 1) - ex)
        h2yx = h_at(1, -1, 0) - 0.25 * (z_next(ex) - ex) + 0.5 * (o.zx0 - ez)
        return h2zx, h2yx

    def stage_two(o, n, behind):
        hx, hy, hz = o.h
        dyez, dzey, dzex, dxez, dxey, dyex = o.d
        exd, eyd, ezd, eyfd, hxd, hzd, dzeyd = o.down
        exu, ezu, eyu = o.up
        h2zx_b, h2yx_b = behind
        xy0u = up(o.xy0, exu)
        zy0u = up(o.zy0, ezu)
        h2zy = hz - 0.25 * dxey + 0.5 * dyex - 0.25 * (n.ysx0 - o.ysx0) + 0.5 * (xy0u - o.xy1)
        h2zx = hz - 0.5 * dxey + 0.25 * dyex - 0.5 * (n.yx0 - o.yx1) + 0.25 * (up(o.xsy0, exu) - o.xsy0)
        h2xz = hx - 0.25 * dyez + 0.5 * dzey - 0.25 * (up(o.zsy0, ezu) - o.zsy0) + 0.5 * (z_next(o.yz0) - o.yz1)
        h2xy = hx - 0.5 * dyez + 0.25 * dzey - 0.5 * (zy0u - o.zy1) + 0.25 * (z_next(o.ysz0) - o.ysz0)
        h2yx = hy - 0.25 * dzex + 0.5 * dxez - 0.25 * (z_next(o.xsz0) - o.xsz0) + 0.5 * (n.zx0 - o.zx1)
        h2yz = hy - 0.5 * dzex + 0.25 * dxez - 0.5 * (z_next(o.xz0) - o.xz1) + 0.25 * (n.zsx0 - o.zsx0)
        h2zy_d = down(h2zy, hzd - 0.25 * (eyfd - eyd) + 0.5 * (o.xy0 - exd))
        h2xy_d = down(h2xy, hxd - 0.5 * (o.zy0 - ezd) + 0.25 * dzeyd)
        half = 0.5 * o.c
        ex = 0.5 * (o.xy0 + o.xy1) + half * (h2zy - h2zy_d - h2yz + z_prev(h2yz))
        ey = 0.5 * (o.yz0 + o.yz1) + half * (h2xz - z_prev(h2xz) - h2zx + h2zx_b)
        ez = 0.5 * (o.zx0 + o.zx1) + half * (h2yx - h2yx_b - h2xy + h2xy_d)
        hx = hx - 0.25 * (dyez - dzey + zy0u - o.zy0 - z_next(o.yz0) + o.yz0)
        hy = hy - 0.25 * (dzex - dxez + z_next(o.xz0) - o.xz0 - n.zx0 + o.zx0)
        hz = hz - 0.25 * (dxey - dyex + n.yx0 - o.yx0 - xy0u + o.xy0)
        return (ex, ey, ez), (hx, hy, hz), (h2zx, h2yx)

    now = stage_one(0)
    behind = ring_behind(now)
    for i in range(PB):
        later = stage_one(i + 1) if i < PB - 1 else ring_ahead(i + 1)
        e_new, h_new, behind = stage_two(now, later, behind)
        pending = (i, e_new, h_new)
        if i > 0:
            write(es, hs, x0, y0, previous)
        previous = pending
        now = later
    write(es, hs, x0, y0, previous)


def write(es, hs, x0, y0, item):
    i, e_new, h_new = item
    for k in range(3):
        es[k, pl.ds((x0 + i) * CB + y0, PB)] = e_new[k]
        hs[k, pl.ds((x0 + i + 1) * CB + y0, PB)] = h_new[k]


def second_kernel(owner, corner, spots, points, faces, halo, e_in, h_in, c_in, e_out, h_out, sampled, es, hs, cs, ye, yh, taken, slot_x, slot_y, count, sem):
    loads = [
        pltpu.make_async_copy(e_in, es.at[:, pl.ds(0, ROWS)], sem.at[0]),
        pltpu.make_async_copy(h_in, hs.at[:, pl.ds(CB, ROWS)], sem.at[1]),
        pltpu.make_async_copy(c_in, cs, sem.at[2]),
    ]
    for copy in loads:
        copy.start()
    me = lax.axis_index("gx") * GY + lax.axis_index("gy")

    def look(n, found):
        slot_x[found] = corner[0, n]
        slot_y[found] = corner[1, n]
        return jnp.minimum(found + (owner[n] == me).astype(jnp.int32), SLOTS)

    count[0] = lax.fori_loop(0, GX * GY, look, 0, unroll=8)
    for copy in loads:
        copy.wait()
    lane = lanes_of((1, CZ))

    def patches():
        def one(n, carry):
            patch(es, hs, cs, slot_x[n], slot_y[n])
            return carry

        lax.fori_loop(0, count[0], one, 0)

    def sample():
        e_rows = es.reshape(3 * (ROWS + CB), CZ)
        h_rows = hs.reshape(3 * (ROWS + CB), CZ)

        def one(n, carry):
            mask = lane == spots[0, n]
            k1, k2 = spots[1, n], spots[2, n]
            taken[pl.ds(n, 1)] = jnp.where(mask, h_rows[pl.ds(k1 + CB, 1)], 0.0)
            taken[pl.ds(n + SPB, 1)] = jnp.where(mask, h_rows[pl.ds(k2 + CB, 1)], 0.0)
            taken[pl.ds(n + 2 * SPB, 1)] = jnp.where(mask, e_rows[pl.ds(k1, 1)], 0.0)
            taken[pl.ds(n + 3 * SPB, 1)] = jnp.where(mask, e_rows[pl.ds(k2, 1)], 0.0)
            return carry

        lax.fori_loop(0, SPB, one, 0, unroll=16)
        high, low = split(taken[...])
        ones = jnp.ones((16, CZ), BF16)
        return dot_t(ones, high) + dot_t(ones, low)

    slots = points[...]
    face = faces[...]
    sign = jnp.where(slots >= 0, (2 * (face % 2) - 1).astype(F32), 0.0)
    for moment in range(2):
        if moment:
            place_halo(es, hs, halo, ye, yh)
            advance(es, hs, cs, ye, yh)
        patches()
        if moment:
            stores = [
                pltpu.make_async_copy(es.at[:, pl.ds(0, ROWS)], e_out, sem.at[0]),
                pltpu.make_async_copy(hs.at[:, pl.ds(CB, ROWS)], h_out, sem.at[1]),
            ]
            for copy in stores:
                copy.start()
        got = sample()
        got = [got[0:1, j * SPB : (j + 1) * SPB] for j in range(4)]
        sampled[4 * moment : 4 * moment + 1] = -sign * got[1]
        sampled[4 * moment + 1 : 4 * moment + 2] = sign * got[0]
        sampled[4 * moment + 2 : 4 * moment + 3] = sign * got[3]
        sampled[4 * moment + 3 : 4 * moment + 4] = -sign * got[2]
    cell = jnp.maximum(slots, 0)
    sampled[8:9] = (cell // (CB * CZ)).astype(F32)
    sampled[9:10] = (cell // CZ % CB).astype(F32)
    sampled[10:11] = (cell % CZ).astype(F32)
    sampled[11:12] = jnp.where(slots >= 0, face, 6).astype(F32)
    sampled[12:16] = jnp.zeros((4, SPB), F32)
    for copy in stores:
        copy.wait()


def third_kernel(omega, sampled, ta_in, tc_in, tb_in, far, got, gathered, ta, tc, tb, tcf, hot, hotz, spread_hi, spread_lo, lhs1, lhs2, lhsz, acc, rows48, send_buf, recv_buf, load_sem, send1, recv1, send2, recv2):
    gx = lax.axis_index("gx")
    gy = lax.axis_index("gy")
    loads = [
        pltpu.make_async_copy(ta_in, ta, load_sem.at[0]),
        pltpu.make_async_copy(tc_in, tc.at[:, pl.ds(0, 2 * ZF)], load_sem.at[1]),
        pltpu.make_async_copy(tc_in.at[:, pl.ds(0, ZF)], tc.at[:, pl.ds(2 * ZF, ZF)], load_sem.at[2]),
        pltpu.make_async_copy(tb_in, tb, load_sem.at[3]),
    ]
    for copy in loads:
        copy.start()
    barrier = pltpu.get_barrier_semaphore()
    for d in range(1, GX):
        pl.semaphore_signal(barrier, inc=1, device_id=(lax.rem(gx + d, GX), gy), device_id_type=MESH)
    for d in range(1, GY):
        pl.semaphore_signal(barrier, inc=1, device_id=(gx, lax.rem(gy + d, GY)), device_id_type=MESH)
    tc[:, 3 * ZF : 4 * ZF] = jnp.zeros((2, ZF, QF), BF16)
    pl.semaphore_wait(barrier, GX + GY - 2)
    first = []
    for d in range(1, GX):
        copy = pltpu.make_async_remote_copy(
            src_ref=sampled,
            dst_ref=gathered.at[GX - d],
            send_sem=send1.at[d],
            recv_sem=recv1.at[GX - d],
            device_id=(lax.rem(gx + d, GX), gy),
            device_id_type=MESH,
        )
        copy.start()
        first.append(copy)
    gathered[0] = sampled[...]
    for copy in loads:
        copy.wait()
    tcf[...] = tc[:, 0:ZF].astype(F32) + tc[:, ZF : 2 * ZF].astype(F32)
    for copy in first:
        copy.wait()

    for b in range(GX):
        lanes = slice(b * SPB, (b + 1) * SPB)
        got[0:16, lanes] = gathered[b]
        block = lax.rem(gx + b, GX)
        x = gathered[b, 8:9] + (block * CB).astype(F32)
        z = gathered[b, 10:11]
        got[12:13, lanes] = jnp.where(x < 128.0, 127.0 - x, x - 128.0)
        got[13:14, lanes] = jnp.where(x < 128.0, -1.0, 1.0)
        got[14:15, lanes] = jnp.where(z < 64.0, 63.0 - z, z - 64.0)
        got[15:16, lanes] = jnp.where(z < 64.0, -1.0, 1.0)

    def one_hot(to, place_row, sign_row, count, blocks):
        for b, start in enumerate(blocks):
            lanes = pl.ds(start, SPB)
            there = slice(b * SPB, (b + 1) * SPB)
            where_at = jnp.broadcast_to(got[place_row : place_row + 1, lanes], (16, SPB))
            sign = jnp.broadcast_to(got[sign_row : sign_row + 1, lanes], (16, SPB))
            at = rows_of((16, SPB)).astype(F32)
            for j in range(0, count, 16):
                same = at + float(j) == where_at
                to[j : j + 16, there] = jnp.where(same, 1.0, 0.0).astype(BF16)
                to[count + j : count + j + 16, there] = jnp.where(same, sign, 0.0).astype(BF16)

    def spread(v, key, start, step, first_row, there, count):
        high, low = split(v)
        key = key.astype(BF16)
        zero = jnp.zeros_like(high)

        def one(n, carry):
            same = key == jnp.full((16, SPB), (start + step * n).astype(F32), F32).astype(BF16)
            at = pl.ds(pl.multiple_of(first_row + n * 16, 16), 16)
            spread_hi[at, there] = jnp.where(same, high, zero)
            spread_lo[at, there] = jnp.where(same, low, zero)
            return carry

        lax.fori_loop(0, count, one, 0, unroll=8)

    def row16(row, lanes):
        return jnp.broadcast_to(got[row : row + 1, lanes], (16, SPB))

    upper = rows_of((16, SPB)) // 8
    every = [b * SPB for b in range(GX)]
    ends = [pl.multiple_of(lax.rem(GX - gx, GX) * SPB, SPB), pl.multiple_of((GX - 1 - gx) * SPB, SPB)]

    def twice(lanes):
        v = got[0:8, lanes]
        return jnp.concatenate([v, v], axis=0)

    def spread_z(y_low, count):
        wanted = (4 + upper).astype(F32)
        for b in range(GX):
            lanes = slice(b * SPB, (b + 1) * SPB)
            v = jnp.where(row16(11, lanes) == wanted, twice(lanes), 0.0)
            spread(v, row16(9, lanes), y_low, 1, 0, lanes, count)

    def spread_x(y_low, count):
        for e, start in enumerate(ends):
            lanes = pl.ds(start, SPB)
            wanted = jnp.where(upper == e, float(e), -1.0)
            v = jnp.where(row16(11, lanes) == wanted, twice(lanes), 0.0)
            spread(v, row16(9, lanes), y_low, 1, 0, slice(e * SPB, (e + 1) * SPB), count)

    def spread_y():
        for b in range(GX):
            lanes = slice(b * SPB, (b + 1) * SPB)
            face = row16(11, lanes)
            v = jnp.where((face == 2.0) | (face == 3.0), twice(lanes), 0.0)
            spread(v, row16(10, lanes) - upper.astype(F32), 16, 2, 0, lanes, YF_ROWS // 2)

    def dense(to, rows):
        for m in range(0, rows, CHUNK):
            d = dot_t(spread_hi[m : m + CHUNK], hot[...]) + dot_t(spread_lo[m : m + CHUNK], hot[...])
            for k in range(2):
                high, low = split(d[:, k * XF : (k + 1) * XF])
                lhs1[k, to + m : to + m + CHUNK, 0:XF] = high
                lhs1[k, to + m : to + m + CHUNK, XF : 2 * XF] = high
                lhs2[k, to + m : to + m + CHUNK] = low

    def dense_x(rows):
        for m in range(0, rows, CHUNK):
            at = slice(m, m + CHUNK)
            d = dot_t(spread_hi[at, 0 : 2 * SPB], hotz[...]) + dot_t(spread_lo[at, 0 : 2 * SPB], hotz[...])
            for k in range(2):
                high, low = split(d[:, k * ZF : (k + 1) * ZF])
                lhsz[k, at] = jnp.concatenate([high, high, low, jnp.zeros_like(low)], axis=1)

    def times_x(to, lanes):
        out = []
        for k in range(2):
            table = ta[k, :, lanes]
            out.append(dot(lhs1[k, to : to + CHUNK], table) + dot(lhs2[k, to : to + CHUNK], table[0:XF]))
        return out

    def times_z(to, lanes):
        return [dot(lhsz[k, to : to + CHUNK], tc[k, :, lanes]) for k in range(2)]

    def outer_y(g, total, y_low, lanes):
        re, im = total
        for y in range(16):
            at = slice(y * 16, (y + 1) * 16)
            bc, bs = tb[0, pl.ds(y_low + y, 1), lanes], tb[1, pl.ds(y_low + y, 1), lanes]
            re = re + (bc * g[0][at] - bs * g[1][at])
            im = im + (bc * g[1][at] + bs * g[0][at])
        return re, im

    def outer_z(g, total, z_low, lanes):
        re, im = total
        for o in range(CHUNK // 8):
            z = z_low + o
            j, sign = (z - 64, 1.0) if z >= 64 else (63 - z, -1.0)
            at = slice(o * 8, (o + 1) * 8)
            cc, cs = tcf[0, j : j + 1, lanes], sign * tcf[1, j : j + 1, lanes]
            re = re + (cc * g[0][at] - cs * g[1][at])
            im = im + (cc * g[1][at] + cs * g[0][at])
        return re, im

    def keep(base, total, lanes):
        n = total[0].shape[0]
        acc[base, 0, 0:n, lanes] = total[0]
        acc[base, 1, 0:n, lanes] = total[1]

    edge = (gy == 0) | (gy == GY - 1)
    zero16 = jnp.zeros((16, CHUNK), F32)
    zero8 = jnp.zeros((8, CHUNK), F32)
    one_hot(hot, 12, 13, XF, every)
    one_hot(hotz, 14, 15, ZF, ends)
    @pl.when(jnp.logical_not(edge))
    def _():
        spread_z(0, CB)
        dense(0, CB * 16)
        spread_x(0, CB)
        dense_x(CB * 16)
        acc[2] = jnp.zeros((2, 16, QF), F32)

        def chunk(n, carry):
            lanes = pl.ds(pl.multiple_of(n * CHUNK, CHUNK), CHUNK)
            total = (zero16, zero16)
            for y in range(2):
                total = outer_y(times_x(y * CHUNK, lanes), total, y * 16, lanes)
            keep(0, total, lanes)
            total = (zero16, zero16)
            for y in range(2):
                total = outer_y(times_z(y * CHUNK, lanes), total, y * 16, lanes)
            keep(1, total, lanes)
            return carry

        lax.fori_loop(0, QF // CHUNK, chunk, 0)

    @pl.when(edge)
    def _():
        y_low = jnp.where(gy == 0, 16, 0)
        spread_z(y_low, 16)
        dense(0, CHUNK)
        spread_x(y_low, 16)
        dense_x(CHUNK)
        spread_y()
        dense(CHUNK, YF_ROWS * 8)

        def chunk(n, carry):
            lanes = pl.ds(pl.multiple_of(n * CHUNK, CHUNK), CHUNK)
            keep(0, outer_y(times_x(0, lanes), (zero16, zero16), y_low, lanes), lanes)
            keep(1, outer_y(times_z(0, lanes), (zero16, zero16), y_low, lanes), lanes)
            total = (zero8, zero8)
            for z in range(0, YF_ROWS, CHUNK // 8):
                total = outer_z(times_x(CHUNK + z * 8, lanes), total, z + 16, lanes)
            keep(2, total, lanes)
            return carry

        lax.fori_loop(0, QF // CHUNK, chunk, 0)

    scale = 1.0 / math.sqrt(GX * GY * SPB)
    y_face = jnp.where(gy == 0, 16, 15)
    moment = 1.0 + (rows_of((8, 1)) // 4).astype(F32)
    for f in range(FREQ):
        lanes = slice(f * QN, (f + 1) * QN)
        mc, ms = turn(omega[f] * (1.0 / (2.0 * math.pi)) * moment)
        mc, ms = mc * scale, ms * scale

        def both(base, c, s):
            low_re, high_re = acc[base, 0, 0:8, lanes], acc[base, 0, 8:16, lanes]
            low_im, high_im = acc[base, 1, 0:8, lanes], acc[base, 1, 8:16, lanes]
            re = c * (low_re + high_re) + s * (low_im - high_im)
            im = c * (low_im + high_im) + s * (high_re - low_re)
            return re, im

        def late(re, im):
            a, b = mc * re + ms * im, mc * im - ms * re
            return a[0:4] + a[4:8], b[0:4] + b[4:8]

        zf = late(*both(0, tcf[0, Z_FACE : Z_FACE + 1, lanes], tcf[1, Z_FACE : Z_FACE + 1, lanes]))
        xf = late(*both(1, tb[0, CB : CB + 1, lanes], tb[1, CB : CB + 1, lanes]))
        c, s = tb[0, pl.ds(y_face, 1), lanes], tb[1, pl.ds(y_face, 1), lanes]
        re, im = acc[2, 0, 0:8, lanes], acc[2, 1, 0:8, lanes]
        yf = late(c * re - s * im, c * im + s * re)
        for k in range(2):
            z4, x4, y4 = zf[k], xf[k], yf[k]
            six = [
                z4[0:1] + y4[1:2], z4[1:2] + x4[0:1], x4[1:2] + y4[0:1],
                z4[2:3] + y4[3:4], z4[3:4] + x4[2:3], x4[3:4] + y4[2:3],
            ]
            for j, v in enumerate(six):
                rows48[12 * f + 6 * k + j : 12 * f + 6 * k + j + 1] = v
    rows48[48:128] = jnp.zeros((80, QN), F32)
    for t in range(0, QN, 128):
        turned = jnp.transpose(rows48[:, t : t + 128])
        for q in range(0, 128, OWN):
            at = (t + q) // 2
            second_half = pltpu.roll(turned[q + HALF : q + OWN], 64, 1)
            send_buf[at : at + HALF] = turned[q : q + HALF] + second_half

    second = []
    for d in range(1, GY):
        to = lax.rem(gy + d, GY)
        copy = pltpu.make_async_remote_copy(
            src_ref=send_buf.at[pl.ds(pl.multiple_of(to * HALF, HALF), HALF)],
            dst_ref=recv_buf.at[GY - d],
            send_sem=send2.at[d],
            recv_sem=recv2.at[GY - d],
            device_id=(gx, to),
            device_id_type=MESH,
        )
        copy.start()
        second.append(copy)
    total = send_buf[pl.ds(pl.multiple_of(gy * HALF, HALF), HALF)]
    for copy in second:
        copy.wait()
    for d in range(1, GY):
        total = total + recv_buf[d]
    far[0:HALF] = total[:, 0:48]
    far[HALF:OWN] = pltpu.roll(total, 64, 1)[:, 0:48]


VMEM = pl.BlockSpec(memory_space=pltpu.VMEM)
SMEM = pl.BlockSpec(memory_space=pltpu.SMEM)
ANY = pl.BlockSpec(memory_space=pl.ANY)
HBM = pl.BlockSpec(memory_space=pltpu.HBM)


def local(efield, hfield, e_coef, omega, patch_owner, patch_corner, surface_points, surface_faces, angle_index):
    field = jax.ShapeDtypeStruct((3, ROWS, CZ), F32)
    fields = [
        pltpu.VMEM((3, ROWS + CB, CZ), F32),
        pltpu.VMEM((3, ROWS + CB, CZ), F32),
        pltpu.VMEM((ROWS, CZ), F32),
        pltpu.VMEM((2, CB, CZ), F32),
        pltpu.VMEM((2, CB, CZ), F32),
    ]
    coef = pltpu.with_memory_space_constraint(e_coef.reshape(ROWS, CZ), pltpu.HBM)
    omega = pltpu.with_memory_space_constraint(omega, pltpu.HBM)
    points = pltpu.with_memory_space_constraint(surface_points.reshape(1, SPB), pltpu.HBM)
    faces = pltpu.with_memory_space_constraint(surface_faces.reshape(1, SPB), pltpu.HBM)
    efield, hfield, halo, *tabled, spots = pl.pallas_call(
        first_kernel,
        out_shape=(
            field,
            field,
            jax.ShapeDtypeStruct((9, CB, CZ), F32),
            jax.ShapeDtypeStruct((2, 2 * XF, QF), BF16),
            jax.ShapeDtypeStruct((2, 2 * ZF, QF), BF16),
            jax.ShapeDtypeStruct((2, CB + 8, QF), F32),
            jax.ShapeDtypeStruct((8, SPB), jnp.int32),
        ),
        in_specs=[SMEM, VMEM, VMEM, VMEM, HBM, HBM, HBM],
        out_specs=(ANY, ANY, VMEM, ANY, ANY, ANY, VMEM),
        scratch_shapes=[
            pltpu.VMEM((8, QF), F32),
            pltpu.VMEM((2, 2 * XF, QF), BF16),
            pltpu.VMEM((2, 2 * ZF, QF), BF16),
            pltpu.VMEM((2, CB + 8, QF), F32),
        ]
        + fields
        + [
            pltpu.VMEM((2, 9, CB, CZ), F32),
            pltpu.VMEM((9, CB, CZ), F32),
            pltpu.SemaphoreType.DMA((6,)),
            pltpu.SemaphoreType.DMA((2, 6)),
            pltpu.SemaphoreType.DMA((2, 6)),
        ],
        compiler_params=pltpu.CompilerParams(collective_id=0, has_side_effects=True, vmem_limit_bytes=24 * 2**20),
        name="first_step",
    )(
        omega,
        pltpu.with_memory_space_constraint(angle_index.T, pltpu.HBM),
        points,
        faces,
        pltpu.with_memory_space_constraint(efield.reshape(3, ROWS, CZ), pltpu.HBM),
        pltpu.with_memory_space_constraint(hfield.reshape(3, ROWS, CZ), pltpu.HBM),
        coef,
    )
    efield, hfield, sampled = pl.pallas_call(
        second_kernel,
        out_shape=(field, field, jax.ShapeDtypeStruct((16, SPB), F32)),
        in_specs=[SMEM, SMEM, SMEM, VMEM, VMEM, VMEM, ANY, ANY, HBM],
        out_specs=(HBM, HBM, VMEM),
        scratch_shapes=fields
        + [
            pltpu.VMEM((4 * SPB, CZ), F32),
            pltpu.SMEM((SLOTS + 1,), jnp.int32),
            pltpu.SMEM((SLOTS + 1,), jnp.int32),
            pltpu.SMEM((1,), jnp.int32),
            pltpu.SemaphoreType.DMA((3,)),
        ],
        compiler_params=pltpu.CompilerParams(vmem_limit_bytes=24 * 2**20),
        name="patches",
    )(patch_owner, patch_corner.T, spots, points, faces, halo, efield, hfield, coef)
    far = pl.pallas_call(
        third_kernel,
        out_shape=jax.ShapeDtypeStruct((OWN, 48), F32),
        in_specs=[SMEM, VMEM, ANY, ANY, ANY],
        out_specs=VMEM,
        scratch_shapes=[
            pltpu.VMEM((16, GX * SPB), F32),
            pltpu.VMEM((GX, 16, SPB), F32),
            pltpu.VMEM((2, 2 * XF, QF), BF16),
            pltpu.VMEM((2, 4 * ZF, QF), BF16),
            pltpu.VMEM((2, CB + 8, QF), F32),
            pltpu.VMEM((2, ZF, QF), F32),
            pltpu.VMEM((2 * XF, GX * SPB), BF16),
            pltpu.VMEM((2 * ZF, 2 * SPB), BF16),
            pltpu.VMEM((YF_ROWS * 8, GX * SPB), BF16),
            pltpu.VMEM((YF_ROWS * 8, GX * SPB), BF16),
            pltpu.VMEM((2, YF_ROWS * 8 + CHUNK, 2 * XF), BF16),
            pltpu.VMEM((2, YF_ROWS * 8 + CHUNK, XF), BF16),
            pltpu.VMEM((2, CB * 16, 4 * ZF), BF16),
            pltpu.VMEM((3, 2, 16, QF), F32),
            pltpu.VMEM((128, QN), F32),
            pltpu.VMEM((QN // 2, 128), F32),
            pltpu.VMEM((GY, HALF, 128), F32),
            pltpu.SemaphoreType.DMA((4,)),
            pltpu.SemaphoreType.DMA((GX,)),
            pltpu.SemaphoreType.DMA((GX,)),
            pltpu.SemaphoreType.DMA((GY,)),
            pltpu.SemaphoreType.DMA((GY,)),
        ],
        compiler_params=pltpu.CompilerParams(collective_id=1, has_side_effects=True, vmem_limit_bytes=32 * 2**20),
        name="projection",
    )(omega, sampled, *tabled)
    shape = (3, CB, CB, CZ)
    return efield.reshape(shape), hfield.reshape(shape), far


def solution(mesh):
    placed = (
        P(None, "gx", "gy", None),
        P(None, "gx", "gy", None),
        P("gx", "gy", None),
        P(),
        P(),
        P(),
        P("gx", "gy", None),
        P("gx", "gy", None),
        P(),
    )
    return jax.shard_map(
        local,
        mesh=mesh,
        in_specs=placed,
        out_specs=(P(None, "gx", "gy", None), P(None, "gx", "gy", None), P(("gx", "gy"), None)),
        check_vma=False,
    )
```

```python
import math

import jax
import jax.numpy as jnp
import numpy as np
from jax import lax
from jax.experimental import pallas as pl
from jax.experimental.pallas import tpu as pltpu
from jax.sharding import PartitionSpec as P

PB = 8
SLOTS = 4
NTH = 128
NPH = 256
CB = 32
CZ = 128
ROWS = CB * CB
SPB = 256
FREQ = 4
GX = 8
GY = 16
ANG = 4096
QN = ANG // GX
QF = QN * FREQ
OWN = ANG // (GX * GY)
HALF = OWN // 2
MESH = pl.DeviceIdType.MESH
F32 = jnp.float32
BF16 = jnp.bfloat16


def lanes_of(shape):
    return lax.broadcasted_iota(jnp.int32, shape, 1)


def rows_of(shape):
    return lax.broadcasted_iota(jnp.int32, shape, 0)


def z_next(v):
    return jnp.where(lanes_of(v.shape) == CZ - 1, 0.0, pltpu.roll(v, CZ - 1, 1))


def z_prev(v):
    return jnp.where(lanes_of(v.shape) == 0, 0.0, pltpu.roll(v, 1, 1))


def y_next(v, edge):
    n = v.shape[0]
    return jnp.where(rows_of(v.shape) == n - 1, edge, pltpu.roll(v, n - 1, 0))


def y_prev(v, edge):
    return jnp.where(rows_of(v.shape) == 0, edge, pltpu.roll(v, 1, 0))


def prepare(es, hs, out):
    out[0] = es[1, 0:CB]
    out[1] = es[2, 0:CB]
    last = (CB - 1) * CB
    ex, ey, ez = [es[k, last : last + CB] for k in range(3)]
    hy, hz = [hs[k, last + CB : last + 2 * CB] for k in (1, 2)]
    out[2] = hy - 0.5 * (z_next(ex) - ex + ez)
    out[3] = hz + 0.5 * (ey + y_next(ex, 0.0) - ex)
    out[8, 8:16] = ey[CB - 8 : CB] * 0.0 + es[1, CB - 1 : CB]
    out[8, 0:8] = ex[0:1] + jnp.zeros((8, CZ), F32)
    out[8, 16:32] = jnp.zeros((16, CZ), F32)
    out[4] = es[0, pl.ds(0, CB, stride=CB)]
    out[5] = es[2, pl.ds(0, CB, stride=CB)]
    ex, ey, ez = [es[k, pl.ds(CB - 1, CB, stride=CB)] for k in range(3)]
    hx, hz = [hs[k, pl.ds(2 * CB - 1, CB, stride=CB)] for k in (0, 2)]
    out[6] = hx + 0.5 * (ez + z_next(ey) - ey)
    out[7] = hz - 0.5 * (y_next(ey, 0.0) - ey + ex)


def place_halo(es, hs, halo, ye, yh):
    gx = lax.axis_index("gx")
    gy = lax.axis_index("gy")
    x_low = (gx > 0).astype(F32)
    x_high = (gx < GX - 1).astype(F32)
    y_low = (gy > 0).astype(F32)
    y_high = (gy < GY - 1).astype(F32)
    last_row = rows_of((CB, CZ)) == CB - 1
    es[1, ROWS : ROWS + CB] = halo[0] * x_high
    es[2, ROWS : ROWS + CB] = halo[1] * x_high
    ye[0] = halo[4] * y_high
    ye[1] = halo[5] * y_high
    corner = jnp.where(last_row, halo[8, 0:1] * (0.5 * y_high), 0.0)
    hs[1, 0:CB] = x_low * (halo[2] + 0.5 * es[2, 0:CB])
    hs[2, 0:CB] = x_low * (halo[3] - 0.5 * es[1, 0:CB] + corner)
    corner = jnp.where(last_row, halo[8, 8:9] * (0.5 * x_high), 0.0)
    yh[0] = y_low * (halo[6] - 0.5 * es[2, pl.ds(0, CB, stride=CB)])
    yh[1] = y_low * (halo[7] + 0.5 * es[0, pl.ds(0, CB, stride=CB)] - corner)


def add_halo(es, hs, cs, halo, own):
    gx = lax.axis_index("gx")
    gy = lax.axis_index("gy")
    x_low = (gx > 0).astype(F32)
    x_high = (gx < GX - 1).astype(F32)
    y_low = (gy > 0).astype(F32)
    y_high = (gy < GY - 1).astype(F32)
    last_row = rows_of((CB, CZ)) == CB - 1
    low_rows = pl.ds(0, CB, stride=CB)
    high_rows = pl.ds(CB - 1, CB, stride=CB)
    h_rows = pl.ds(2 * CB - 1, CB, stride=CB)
    plane = slice(ROWS - CB, ROWS)
    dy, dz = 0.5 * x_high * halo[1], -0.5 * x_high * halo[0]
    hs[1, ROWS : ROWS + CB] += dy
    hs[2, ROWS : ROWS + CB] += dz
    c = cs[plane]
    es[0, plane] += c * (dz - y_prev(dz, 0.0) - dy + z_prev(dy))
    es[1, plane] -= c * dz
    es[2, plane] += c * dy
    dx, dz = -0.5 * y_high * halo[5], 0.5 * y_high * halo[4]
    hs[0, h_rows] = hs[0, h_rows] + dx
    hs[2, h_rows] = hs[2, h_rows] + dz
    c = cs[high_rows]
    es[0, high_rows] = es[0, high_rows] + c * dz
    es[1, high_rows] = es[1, high_rows] + c * (dx - z_prev(dx) - dz + y_prev(dz, 0.0))
    es[2, high_rows] = es[2, high_rows] - c * dx
    corner = jnp.where(last_row, halo[8, 0:1] * (0.5 * y_high), 0.0)
    before_y = x_low * (halo[2] + 0.5 * own[1])
    before_z = x_low * (halo[3] - 0.5 * own[0] + corner)
    c = cs[0:CB]
    es[1, 0:CB] += c * before_z
    es[2, 0:CB] -= c * before_y
    corner = jnp.where(last_row, halo[8, 8:9] * (0.5 * x_high), 0.0)
    before_x = y_low * (halo[6] - 0.5 * own[5])
    before_z = y_low * (halo[7] + 0.5 * own[4] - corner)
    c = cs[low_rows]
    es[0, low_rows] = es[0, low_rows] - c * before_z
    es[2, low_rows] = es[2, low_rows] + c * before_x


def advance(es, hs, cs, ye, yh):
    last = rows_of((CB, CZ)) == CB - 1
    for x in range(CB):
        r = x * CB
        here, after = slice(r, r + CB), slice(r + CB, r + 2 * CB)
        ex, ey, ez = [es[k, here] for k in range(3)]
        ey1, ez1 = es[1, after], es[2, after]
        hx, hy, hz = [hs[k, after] for k in range(3)]
        if x == 0:
            hy0, hz0 = hs[1, here], hs[2, here]
        exu = jnp.where(last, ye[0, x : x + 1], es[0, r + 1 : r + CB + 1])
        ezu = jnp.where(last, ye[1, x : x + 1], es[2, r + 1 : r + CB + 1])
        hx = hx - 0.5 * (ezu - ez - z_next(ey) + ey)
        hy = hy - 0.5 * (z_next(ex) - ex - ez1 + ez)
        hz = hz - 0.5 * (ey1 - ey - exu + ex)
        for k, v in enumerate((hx, hy, hz)):
            hs[k, after] = v
        c = cs[here]
        ex = ex + c * (hz - y_prev(hz, yh[1, x : x + 1]) - hy + z_prev(hy))
        ey = ey + c * (hx - z_prev(hx) - hz + hz0)
        ez = ez + c * (hy - hy0 - hx + y_prev(hx, yh[0, x : x + 1]))
        for k, v in enumerate((ex, ey, ez)):
            es[k, here] = v
        hy0, hz0 = hy, hz


def neighbours():
    gx = lax.axis_index("gx")
    gy = lax.axis_index("gy")
    xn, xp = lax.rem(gx + 1, GX), lax.rem(gx + GX - 1, GX)
    yn, yp = lax.rem(gy + 1, GY), lax.rem(gy + GY - 1, GY)
    return [(xp, gy), (xn, gy), (gx, yp), (gx, yn), (xn, yp), (xp, yn)]


def pieces(ref, n):
    if n < 4:
        return ref.at[pl.ds(2 * n, 2)]
    return ref.at[8, pl.ds(8 * (n - 4), 8)]


def fitted(function, degrees, points=4001):
    r = np.cos(np.linspace(0.0, np.pi, points)) * 0.5
    basis = np.stack([r**d for d in degrees], axis=1)
    return [float(v) for v in np.linalg.lstsq(basis, function(np.pi * r) * math.sqrt(2.0), rcond=None)[0]]


SIN = fitted(np.sin, (1, 3, 5, 7, 9))
COS = fitted(np.cos, (0, 2, 4, 6, 8))


def turn(t):
    r = t - jnp.round(t)
    r2 = r * r
    s = r * (SIN[0] + r2 * (SIN[1] + r2 * (SIN[2] + r2 * (SIN[3] + r2 * SIN[4]))))
    c = COS[0] + r2 * (COS[1] + r2 * (COS[2] + r2 * (COS[3] + r2 * COS[4])))
    return 1.0 - s * s, s * c


def split(v):
    high = v.astype(BF16)
    return high, (v - high.astype(F32)).astype(BF16)


def dot(a, b):
    return jnp.dot(a, b, preferred_element_type=F32)


def dot_t(a, b):
    return lax.dot_general(a, b, (((1,), (1,)), ((), ())), preferred_element_type=F32)


CUT2 = 2
XF = 128
ZF = 64
YF_ROWS = 96
CHUNK = 256
X_FACE = 111
Z_FACE = 47


def directions(omega, angles, kdir):
    index = angles[:, pl.ds(pl.multiple_of(lax.axis_index("gx") * QN, QN), QN)].astype(F32)
    theta = math.pi * (index[0:1] + 0.5) / NTH
    phi = 2.0 * math.pi * (index[1:2] + 0.5) / NPH
    st, ct = jnp.sin(theta), jnp.cos(theta)
    sp, cp = jnp.sin(phi), jnp.cos(phi)
    for f in range(FREQ):
        w = omega[f] * (1.0 / (2.0 * math.pi))
        lanes = slice(f * QN, (f + 1) * QN)
        kdir[0:1, lanes] = st * cp * w
        kdir[1:2, lanes] = st * sp * w
        kdir[2:3, lanes] = ct * w


def tables(kdir, ta, tc, tb, n):
    y_start = (lax.axis_index("gy") * CB).astype(F32) + (0.5 - CB * GY / 2.0)
    lanes = pl.ds(pl.multiple_of(n * CHUNK, CHUNK), CHUNK)
    kx, ky, kz = kdir[0:1, lanes], kdir[1:2, lanes], kdir[2:3, lanes]
    count = rows_of((16, CHUNK)).astype(F32)
    for j in range(0, XF, 16):
        for k, v in enumerate(turn((count + (j + 0.5)) * kx)):
            high, low = split(v)
            ta[k, j : j + 16, lanes] = high
            ta[k, XF + j : XF + j + 16, lanes] = low
    for j in range(0, ZF, 16):
        for k, v in enumerate(turn((count + (j + 0.5)) * kz)):
            high, low = split(v)
            tc[k, j : j + 16, lanes] = high
            tc[k, ZF + j : ZF + j + 16, lanes] = low
    for j in range(0, CB, 16):
        for k, v in enumerate(turn((count + (y_start + j)) * ky)):
            tb[k, j : j + 16, lanes] = v
    for k, v in enumerate(turn(jnp.full((8, CHUNK), X_FACE + 0.5, F32) * kx)):
        tb[k, CB : CB + 8, lanes] = v


def first_kernel(omega, angles, points, faces, e_in, h_in, c_in, e_out, h_out, halo2, ta_out, tc_out, tb_out, spots, kdir, ta, tc, tb, es, hs, cs, ye, yh, sent, halo1, local_sem, send_sem, recv_sem):
    loads = [
        pltpu.make_async_copy(e_in, es.at[:, pl.ds(0, ROWS)], local_sem.at[0]),
        pltpu.make_async_copy(h_in, hs.at[:, pl.ds(CB, ROWS)], local_sem.at[1]),
        pltpu.make_async_copy(c_in, cs, local_sem.at[2]),
    ]
    for copy in loads:
        copy.start()
    barrier = pltpu.get_barrier_semaphore()
    for device in neighbours():
        pl.semaphore_signal(barrier, inc=1, device_id=device, device_id_type=MESH)
    def some_tables(low, high):
        def one(n, carry):
            tables(kdir, ta, tc, tb, n)
            return carry

        lax.fori_loop(low, high, one, 0)

    loads[0].wait()
    loads[1].wait()

    def exchange(number, halo):
        copies = []
        for n, device in enumerate(neighbours()):
            copy = pltpu.make_async_remote_copy(
                src_ref=pieces(sent.at[number], n),
                dst_ref=pieces(halo, n),
                send_sem=send_sem.at[number, n],
                recv_sem=recv_sem.at[number, n],
                device_id=device,
                device_id_type=MESH,
            )
            copy.start()
            copies.append(copy)
        return copies

    prepare(es, hs, sent.at[0])
    pl.semaphore_wait(barrier, 6)
    copies = exchange(0, halo1)
    for k in (1, 2):
        es[k, ROWS : ROWS + CB] = jnp.zeros((CB, CZ), F32)
        hs[k, 0:CB] = jnp.zeros((CB, CZ), F32)
    ye[...] = jnp.zeros_like(ye)
    yh[...] = jnp.zeros_like(yh)
    loads[2].wait()
    advance(es, hs, cs, ye, yh)
    directions(omega, angles, kdir)
    cell = jnp.maximum(points[...], 0)
    normal = lax.shift_right_logical(faces[...], 1)
    row = lax.shift_right_logical(cell, 7)
    spots[0:1] = cell & (CZ - 1)
    spots[1:2] = jnp.where(normal == 2, 0, normal + 1) * (ROWS + CB) + row
    spots[2:3] = jnp.where(normal == 0, 2, normal - 1) * (ROWS + CB) + row
    spots[3:8] = jnp.zeros((5, SPB), jnp.int32)
    some_tables(0, CUT2)
    for copy in copies:
        copy.wait()
    add_halo(es, hs, cs, halo1, sent.at[0])
    prepare(es, hs, sent.at[1])
    copies = exchange(1, halo2)
    stores = [
        pltpu.make_async_copy(es.at[:, pl.ds(0, ROWS)], e_out, local_sem.at[0]),
        pltpu.make_async_copy(hs.at[:, pl.ds(CB, ROWS)], h_out, local_sem.at[1]),
    ]
    for copy in stores:
        copy.start()
    some_tables(CUT2, QF // CHUNK)
    for n, (table, out) in enumerate(((ta, ta_out), (tc, tc_out), (tb, tb_out))):
        copy = pltpu.make_async_copy(table, out, local_sem.at[2 + n])
        copy.start()
        stores.append(copy)
    for copy in copies + stores:
        copy.wait()


def patch(es, hs, cs, x0, y0):
    first = rows_of((PB, CZ)) == 0
    final = rows_of((PB, CZ)) == PB - 1

    def e_at(k, i, j):
        return es[k, pl.ds((x0 + i) * CB + y0 + j, PB)]

    def h_at(k, i, j):
        return hs[k, pl.ds((x0 + i + 1) * CB + y0 + j, PB)]

    def up(v, edge):
        return jnp.where(final, edge, pltpu.roll(v, PB - 1, 0))

    def down(v, edge):
        return jnp.where(first, edge, pltpu.roll(v, 1, 0))

    class Cell:
        pass

    def averages(name, o, e, c, u1, u0, wu, v1, v0, wv, pa, pb):
        vm = 0.5 * (v0 + v1)
        um = 0.5 * (u0 + u1)
        qu = 0.25 * wu
        qv = 0.25 * wv
        base_a = e - c * (vm + qv)
        base_b = e + c * (um - qu)
        setattr(o, name + pa + "1", base_a + c * u1)
        setattr(o, name + pa + "0", base_a + c * (u0 - 0.5 * wu))
        setattr(o, name + pb + "1", base_b - c * v1)
        setattr(o, name + pb + "0", base_b - c * (v0 + 0.5 * wv))
        setattr(o, name + "s" + pa + "0", e + c * (u0 - wu - vm - 0.5 * wv))
        setattr(o, name + "s" + pb + "0", e + c * (um - 0.5 * wu - v0 - wv))

    def stage_one(i):
        o = Cell()
        ex, ey, ez = [e_at(k, i, 0) for k in range(3)]
        exu, ezu = e_at(0, i, 1), e_at(2, i, 1)
        exd, eyd, ezd = [e_at(k, i, -1) for k in range(3)]
        exf, eyf, ezf = [e_at(k, i + 1, 0) for k in range(3)]
        eyb, ezb = e_at(1, i - 1, 0), e_at(2, i - 1, 0)
        exbu, exb = e_at(0, i - 1, 1), e_at(0, i - 1, 0)
        eyfd = e_at(1, i + 1, -1)
        hx, hy, hz = [h_at(k, i, 0) for k in range(3)]
        hxd, hzd = h_at(0, i, -1), h_at(2, i, -1)
        hyb, hzb = h_at(1, i - 1, 0), h_at(2, i - 1, 0)
        c = cs[pl.ds((x0 + i) * CB + y0, PB)]
        dyex, dyez = exu - ex, ezu - ez
        dxey, dxez = eyf - ey, ezf - ez
        dzex, dzey = z_next(ex) - ex, z_next(ey) - ey
        dyexb = exbu - exb
        dxeyd = eyfd - eyd
        szex, szey = z_prev(dzex), z_prev(dzey)
        averages(
            "x", o, ex, c,
            0.5 * dyex, hz - hzd - 0.5 * (ex - exd), 0.5 * (dxey - dxeyd),
            -0.5 * dzex, hy - z_prev(hy) + 0.5 * szex, 0.5 * (dxez - z_prev(dxez)),
            "y", "z",
        )
        averages(
            "y", o, ey, c,
            0.5 * dzey, hx - z_prev(hx) - 0.5 * szey, 0.5 * (dyez - z_prev(dyez)),
            -0.5 * dxey, hz - hzb + 0.5 * (ey - eyb), 0.5 * (dyex - dyexb),
            "z", "x",
        )
        dzexb = z_next(exb) - exb
        dzeyd = z_next(eyd) - eyd
        averages(
            "z", o, ez, c,
            0.5 * dxez, hy - hyb - 0.5 * (ez - ezb), 0.5 * (dzex - dzexb),
            -0.5 * dyez, hx - hxd + 0.5 * (ez - ezd), 0.5 * (dzey - dzeyd),
            "x", "y",
        )
        o.c = c
        o.h = (hx, hy, hz)
        o.d = (dyez, dzey, dzex, dxez, dxey, dyex)
        o.down = (exd, eyd, ezd, eyfd, hxd, hzd, dzeyd)
        o.up = (exu, ezu, e_at(1, i, 1))
        return o

    def ring_ahead(i):
        o = Cell()
        ey, ez = e_at(1, i, 0), e_at(2, i, 0)
        o.yx0 = o.ysx0 = ey
        o.zx0 = o.zsx0 = ez
        return o

    def ring_behind(o):
        ex, ey, ez = [e_at(k, -1, 0) for k in range(3)]
        h2zx = h_at(2, -1, 0) - 0.5 * (o.yx0 - ey) + 0.25 * (e_at(0, -1, 1) - ex)
        h2yx = h_at(1, -1, 0) - 0.25 * (z_next(ex) - ex) + 0.5 * (o.zx0 - ez)
        return h2zx, h2yx

    def stage_two(o, n, behind):
        hx, hy, hz = o.h
        dyez, dzey, dzex, dxez, dxey, dyex = o.d
        exd, eyd, ezd, eyfd, hxd, hzd, dzeyd = o.down
        exu, ezu, eyu = o.up
        h2zx_b, h2yx_b = behind
        xy0u = up(o.xy0, exu)
        zy0u = up(o.zy0, ezu)
        h2zy = hz - 0.25 * dxey + 0.5 * dyex - 0.25 * (n.ysx0 - o.ysx0) + 0.5 * (xy0u - o.xy1)
        h2zx = hz - 0.5 * dxey + 0.25 * dyex - 0.5 * (n.yx0 - o.yx1) + 0.25 * (up(o.xsy0, exu) - o.xsy0)
        h2xz = hx - 0.25 * dyez + 0.5 * dzey - 0.25 * (up(o.zsy0, ezu) - o.zsy0) + 0.5 * (z_next(o.yz0) - o.yz1)
        h2xy = hx - 0.5 * dyez + 0.25 * dzey - 0.5 * (zy0u - o.zy1) + 0.25 * (z_next(o.ysz0) - o.ysz0)
        h2yx = hy - 0.25 * dzex + 0.5 * dxez - 0.25 * (z_next(o.xsz0) - o.xsz0) + 0.5 * (n.zx0 - o.zx1)
        h2yz = hy - 0.5 * dzex + 0.25 * dxez - 0.5 * (z_next(o.xz0) - o.xz1) + 0.25 * (n.zsx0 - o.zsx0)
        h2zy_d = down(h2zy, hzd - 0.25 * (eyfd - eyd) + 0.5 * (o.xy0 - exd))
        h2xy_d = down(h2xy, hxd - 0.5 * (o.zy0 - ezd) + 0.25 * dzeyd)
        half = 0.5 * o.c
        ex = 0.5 * (o.xy0 + o.xy1) + half * (h2zy - h2zy_d - h2yz + z_prev(h2yz))
        ey = 0.5 * (o.yz0 + o.yz1) + half * (h2xz - z_prev(h2xz) - h2zx + h2zx_b)
        ez = 0.5 * (o.zx0 + o.zx1) + half * (h2yx - h2yx_b - h2xy + h2xy_d)
        hx = hx - 0.25 * (dyez - dzey + zy0u - o.zy0 - z_next(o.yz0) + o.yz0)
        hy = hy - 0.25 * (dzex - dxez + z_next(o.xz0) - o.xz0 - n.zx0 + o.zx0)
        hz = hz - 0.25 * (dxey - dyex + n.yx0 - o.yx0 - xy0u + o.xy0)
        return (ex, ey, ez), (hx, hy, hz), (h2zx, h2yx)

    now = stage_one(0)
    behind = ring_behind(now)
    for i in range(PB):
        later = stage_one(i + 1) if i < PB - 1 else ring_ahead(i + 1)
        e_new, h_new, behind = stage_two(now, later, behind)
        pending = (i, e_new, h_new)
        if i > 0:
            write(es, hs, x0, y0, previous)
        previous = pending
        now = later
    write(es, hs, x0, y0, previous)


def write(es, hs, x0, y0, item):
    i, e_new, h_new = item
    for k in range(3):
        es[k, pl.ds((x0 + i) * CB + y0, PB)] = e_new[k]
        hs[k, pl.ds((x0 + i + 1) * CB + y0, PB)] = h_new[k]


def second_kernel(owner, corner, spots, points, faces, halo, e_in, h_in, c_in, e_out, h_out, sampled, es, hs, cs, ye, yh, taken, slot_x, slot_y, count, sem):
    loads = [
        pltpu.make_async_copy(e_in, es.at[:, pl.ds(0, ROWS)], sem.at[0]),
        pltpu.make_async_copy(h_in, hs.at[:, pl.ds(CB, ROWS)], sem.at[1]),
        pltpu.make_async_copy(c_in, cs, sem.at[2]),
    ]
    for copy in loads:
        copy.start()
    me = lax.axis_index("gx") * GY + lax.axis_index("gy")

    def look(n, found):
        slot_x[found] = corner[0, n]
        slot_y[found] = corner[1, n]
        return jnp.minimum(found + (owner[n] == me).astype(jnp.int32), SLOTS)

    count[0] = lax.fori_loop(0, GX * GY, look, 0, unroll=8)
    for copy in loads:
        copy.wait()
    lane = lanes_of((1, CZ))

    def patches():
        def one(n, carry):
            patch(es, hs, cs, slot_x[n], slot_y[n])
            return carry

        lax.fori_loop(0, count[0], one, 0)

    def sample():
        e_rows = es.reshape(3 * (ROWS + CB), CZ)
        h_rows = hs.reshape(3 * (ROWS + CB), CZ)

        def one(n, carry):
            mask = lane == spots[0, n]
            k1, k2 = spots[1, n], spots[2, n]
            taken[pl.ds(n, 1)] = jnp.where(mask, h_rows[pl.ds(k1 + CB, 1)], 0.0)
            taken[pl.ds(n + SPB, 1)] = jnp.where(mask, h_rows[pl.ds(k2 + CB, 1)], 0.0)
            taken[pl.ds(n + 2 * SPB, 1)] = jnp.where(mask, e_rows[pl.ds(k1, 1)], 0.0)
            taken[pl.ds(n + 3 * SPB, 1)] = jnp.where(mask, e_rows[pl.ds(k2, 1)], 0.0)
            return carry

        lax.fori_loop(0, SPB, one, 0, unroll=16)
        high, low = split(taken[...])
        ones = jnp.ones((16, CZ), BF16)
        return dot_t(ones, high) + dot_t(ones, low)

    slots = points[...]
    face = faces[...]
    sign = jnp.where(slots >= 0, (2 * (face % 2) - 1).astype(F32), 0.0)
    for moment in range(2):
        if moment:
            place_halo(es, hs, halo, ye, yh)
            advance(es, hs, cs, ye, yh)
        patches()
        if moment:
            stores = [
                pltpu.make_async_copy(es.at[:, pl.ds(0, ROWS)], e_out, sem.at[0]),
                pltpu.make_async_copy(hs.at[:, pl.ds(CB, ROWS)], h_out, sem.at[1]),
            ]
            for copy in stores:
                copy.start()
        got = sample()
        got = [got[0:1, j * SPB : (j + 1) * SPB] for j in range(4)]
        sampled[4 * moment : 4 * moment + 1] = -sign * got[1]
        sampled[4 * moment + 1 : 4 * moment + 2] = sign * got[0]
        sampled[4 * moment + 2 : 4 * moment + 3] = sign * got[3]
        sampled[4 * moment + 3 : 4 * moment + 4] = -sign * got[2]
    cell = jnp.maximum(slots, 0)
    sampled[8:9] = (cell // (CB * CZ)).astype(F32)
    sampled[9:10] = (cell // CZ % CB).astype(F32)
    sampled[10:11] = (cell % CZ).astype(F32)
    sampled[11:12] = jnp.where(slots >= 0, face, 6).astype(F32)
    sampled[12:16] = jnp.zeros((4, SPB), F32)
    for copy in stores:
        copy.wait()


def third_kernel(omega, sampled, ta_in, tc_in, tb_in, far, got, gathered, ta, tc, tb, tcf, hot, hotz, spread_hi, spread_lo, lhs1, lhs2, lhsz, acc, rows48, send_buf, recv_buf, load_sem, send1, recv1, send2, recv2):
    gx = lax.axis_index("gx")
    gy = lax.axis_index("gy")
    loads = [
        pltpu.make_async_copy(ta_in, ta, load_sem.at[0]),
        pltpu.make_async_copy(tc_in, tc.at[:, pl.ds(0, 2 * ZF)], load_sem.at[1]),
        pltpu.make_async_copy(tc_in.at[:, pl.ds(0, ZF)], tc.at[:, pl.ds(2 * ZF, ZF)], load_sem.at[2]),
        pltpu.make_async_copy(tb_in, tb, load_sem.at[3]),
    ]
    for copy in loads:
        copy.start()
    barrier = pltpu.get_barrier_semaphore()
    for d in range(1, GX):
        pl.semaphore_signal(barrier, inc=1, device_id=(lax.rem(gx + d, GX), gy), device_id_type=MESH)
    for d in range(1, GY):
        pl.semaphore_signal(barrier, inc=1, device_id=(gx, lax.rem(gy + d, GY)), device_id_type=MESH)
    pl.semaphore_wait(barrier, GX + GY - 2)
    first = []
    for d in range(1, GX):
        copy = pltpu.make_async_remote_copy(
            src_ref=sampled,
            dst_ref=gathered.at[GX - d],
            send_sem=send1.at[d],
            recv_sem=recv1.at[GX - d],
            device_id=(lax.rem(gx + d, GX), gy),
            device_id_type=MESH,
        )
        copy.start()
        first.append(copy)
    gathered[0] = sampled[...]
    tc[:, 3 * ZF : 4 * ZF] = jnp.zeros((2, ZF, QF), BF16)
    for copy in loads:
        copy.wait()
    tcf[...] = tc[:, 0:ZF].astype(F32) + tc[:, ZF : 2 * ZF].astype(F32)
    for copy in first:
        copy.wait()

    for b in range(GX):
        lanes = slice(b * SPB, (b + 1) * SPB)
        got[0:16, lanes] = gathered[b]
        block = lax.rem(gx + b, GX)
        x = gathered[b, 8:9] + (block * CB).astype(F32)
        z = gathered[b, 10:11]
        got[12:13, lanes] = jnp.where(x < 128.0, 127.0 - x, x - 128.0)
        got[13:14, lanes] = jnp.where(x < 128.0, -1.0, 1.0)
        got[14:15, lanes] = jnp.where(z < 64.0, 63.0 - z, z - 64.0)
        got[15:16, lanes] = jnp.where(z < 64.0, -1.0, 1.0)

    def one_hot(to, place_row, sign_row, count, blocks):
        for b, start in enumerate(blocks):
            lanes = pl.ds(start, SPB)
            there = slice(b * SPB, (b + 1) * SPB)
            where_at = jnp.broadcast_to(got[place_row : place_row + 1, lanes], (16, SPB))
            sign = jnp.broadcast_to(got[sign_row : sign_row + 1, lanes], (16, SPB))
            at = rows_of((16, SPB)).astype(F32)
            for j in range(0, count, 16):
                same = at + float(j) == where_at
                to[j : j + 16, there] = jnp.where(same, 1.0, 0.0).astype(BF16)
                to[count + j : count + j + 16, there] = jnp.where(same, sign, 0.0).astype(BF16)

    def spread(v, key, start, step, first_row, there, count):
        high, low = split(v)
        key = key.astype(BF16)
        zero = jnp.zeros_like(high)

        def one(n, carry):
            same = key == jnp.full((16, SPB), (start + step * n).astype(F32), F32).astype(BF16)
            at = pl.ds(pl.multiple_of(first_row + n * 16, 16), 16)
            spread_hi[at, there] = jnp.where(same, high, zero)
            spread_lo[at, there] = jnp.where(same, low, zero)
            return carry

        lax.fori_loop(0, count, one, 0, unroll=True)

    def row16(row, lanes):
        return jnp.broadcast_to(got[row : row + 1, lanes], (16, SPB))

    upper = rows_of((16, SPB)) // 8
    every = [b * SPB for b in range(GX)]
    ends = [pl.multiple_of(lax.rem(GX - gx, GX) * SPB, SPB), pl.multiple_of((GX - 1 - gx) * SPB, SPB)]

    def twice(lanes):
        v = got[0:8, lanes]
        return jnp.concatenate([v, v], axis=0)

    def spread_z(y_low, count):
        wanted = (4 + upper).astype(F32)
        for b in range(GX):
            lanes = slice(b * SPB, (b + 1) * SPB)
            v = jnp.where(row16(11, lanes) == wanted, twice(lanes), 0.0)
            spread(v, row16(9, lanes), y_low, 1, 0, lanes, count)

    def spread_x(y_low, count):
        for e, start in enumerate(ends):
            lanes = pl.ds(start, SPB)
            wanted = jnp.where(upper == e, float(e), -1.0)
            v = jnp.where(row16(11, lanes) == wanted, twice(lanes), 0.0)
            spread(v, row16(9, lanes), y_low, 1, 0, slice(e * SPB, (e + 1) * SPB), count)

    def spread_y():
        for b in range(GX):
            lanes = slice(b * SPB, (b + 1) * SPB)
            face = row16(11, lanes)
            v = jnp.where((face == 2.0) | (face == 3.0), twice(lanes), 0.0)
            spread(v, row16(10, lanes) - upper.astype(F32), 16, 2, 0, lanes, YF_ROWS // 2)

    def dense(to, rows):
        for m in range(0, rows, CHUNK):
            d = dot_t(spread_hi[m : m + CHUNK], hot[...]) + dot_t(spread_lo[m : m + CHUNK], hot[...])
            for k in range(2):
                high, low = split(d[:, k * XF : (k + 1) * XF])
                lhs1[k, to + m : to + m + CHUNK, 0:XF] = high
                lhs1[k, to + m : to + m + CHUNK, XF : 2 * XF] = high
                lhs2[k, to + m : to + m + CHUNK] = low

    def dense_x(rows):
        for m in range(0, rows, CHUNK):
            at = slice(m, m + CHUNK)
            d = dot_t(spread_hi[at, 0 : 2 * SPB], hotz[...]) + dot_t(spread_lo[at, 0 : 2 * SPB], hotz[...])
            for k in range(2):
                high, low = split(d[:, k * ZF : (k + 1) * ZF])
                lhsz[k, at] = jnp.concatenate([high, high, low, jnp.zeros_like(low)], axis=1)

    def times_x(to, lanes):
        out = []
        for k in range(2):
            table = ta[k, :, lanes]
            out.append(dot(lhs1[k, to : to + CHUNK], table) + dot(lhs2[k, to : to + CHUNK], table[0:XF]))
        return out

    def times_z(to, lanes):
        return [dot(lhsz[k, to : to + CHUNK], tc[k, :, lanes]) for k in range(2)]

    def outer_y(g, total, y_low, lanes):
        re, im = total
        for y in range(16):
            at = slice(y * 16, (y + 1) * 16)
            bc, bs = tb[0, pl.ds(y_low + y, 1), lanes], tb[1, pl.ds(y_low + y, 1), lanes]
            re = re + (bc * g[0][at] - bs * g[1][at])
            im = im + (bc * g[1][at] + bs * g[0][at])
        return re, im

    def outer_z(g, total, z_low, lanes):
        re, im = total
        for o in range(CHUNK // 8):
            z = z_low + o
            j, sign = (z - 64, 1.0) if z >= 64 else (63 - z, -1.0)
            at = slice(o * 8, (o + 1) * 8)
            cc, cs = tcf[0, j : j + 1, lanes], sign * tcf[1, j : j + 1, lanes]
            re = re + (cc * g[0][at] - cs * g[1][at])
            im = im + (cc * g[1][at] + cs * g[0][at])
        return re, im

    def keep(base, total, lanes):
        n = total[0].shape[0]
        acc[base, 0, 0:n, lanes] = total[0]
        acc[base, 1, 0:n, lanes] = total[1]

    edge = (gy == 0) | (gy == GY - 1)
    zero16 = jnp.zeros((16, CHUNK), F32)
    zero8 = jnp.zeros((8, CHUNK), F32)
    one_hot(hot, 12, 13, XF, every)
    one_hot(hotz, 14, 15, ZF, ends)
    @pl.when(jnp.logical_not(edge))
    def _():
        spread_z(0, CB)
        dense(0, CB * 16)
        spread_x(0, CB)
        dense_x(CB * 16)
        acc[2] = jnp.zeros((2, 16, QF), F32)

        def chunk(n, carry):
            lanes = pl.ds(pl.multiple_of(n * CHUNK, CHUNK), CHUNK)
            total = (zero16, zero16)
            for y in range(2):
                total = outer_y(times_x(y * CHUNK, lanes), total, y * 16, lanes)
            keep(0, total, lanes)
            total = (zero16, zero16)
            for y in range(2):
                total = outer_y(times_z(y * CHUNK, lanes), total, y * 16, lanes)
            keep(1, total, lanes)
            return carry

        lax.fori_loop(0, QF // CHUNK, chunk, 0, unroll=2)

    @pl.when(edge)
    def _():
        y_low = jnp.where(gy == 0, 16, 0)
        spread_z(y_low, 16)
        dense(0, CHUNK)
        spread_x(y_low, 16)
        dense_x(CHUNK)
        spread_y()
        dense(CHUNK, YF_ROWS * 8)

        def chunk(n, carry):
            lanes = pl.ds(pl.multiple_of(n * CHUNK, CHUNK), CHUNK)
            keep(0, outer_y(times_x(0, lanes), (zero16, zero16), y_low, lanes), lanes)
            keep(1, outer_y(times_z(0, lanes), (zero16, zero16), y_low, lanes), lanes)
            total = (zero8, zero8)
            for z in range(0, YF_ROWS, CHUNK // 8):
                total = outer_z(times_x(CHUNK + z * 8, lanes), total, z + 16, lanes)
            keep(2, total, lanes)
            return carry

        lax.fori_loop(0, QF // CHUNK, chunk, 0, unroll=2)

    scale = 1.0 / math.sqrt(GX * GY * SPB)
    y_face = jnp.where(gy == 0, 16, 15)
    moment = 1.0 + (rows_of((8, 1)) // 4).astype(F32)
    for f in range(FREQ):
        lanes = slice(f * QN, (f + 1) * QN)
        mc, ms = turn(omega[f] * (1.0 / (2.0 * math.pi)) * moment)
        mc, ms = mc * scale, ms * scale

        def both(base, c, s):
            low_re, high_re = acc[base, 0, 0:8, lanes], acc[base, 0, 8:16, lanes]
            low_im, high_im = acc[base, 1, 0:8, lanes], acc[base, 1, 8:16, lanes]
            re = c * (low_re + high_re) + s * (low_im - high_im)
            im = c * (low_im + high_im) + s * (high_re - low_re)
            return re, im

        def late(re, im):
            a, b = mc * re + ms * im, mc * im - ms * re
            return a[0:4] + a[4:8], b[0:4] + b[4:8]

        zf = late(*both(0, tcf[0, Z_FACE : Z_FACE + 1, lanes], tcf[1, Z_FACE : Z_FACE + 1, lanes]))
        xf = late(*both(1, tb[0, CB : CB + 1, lanes], tb[1, CB : CB + 1, lanes]))
        c, s = tb[0, pl.ds(y_face, 1), lanes], tb[1, pl.ds(y_face, 1), lanes]
        re, im = acc[2, 0, 0:8, lanes], acc[2, 1, 0:8, lanes]
        yf = late(c * re - s * im, c * im + s * re)
        for k in range(2):
            z4, x4, y4 = zf[k], xf[k], yf[k]
            six = [
                z4[0:1] + y4[1:2], z4[1:2] + x4[0:1], x4[1:2] + y4[0:1],
                z4[2:3] + y4[3:4], z4[3:4] + x4[2:3], x4[3:4] + y4[2:3],
            ]
            for j, v in enumerate(six):
                rows48[12 * f + 6 * k + j : 12 * f + 6 * k + j + 1] = v
    rows48[48:128] = jnp.zeros((80, QN), F32)
    for t in range(0, QN, 128):
        turned = jnp.transpose(rows48[:, t : t + 128])
        for q in range(0, 128, OWN):
            at = (t + q) // 2
            second_half = pltpu.roll(turned[q + HALF : q + OWN], 64, 1)
            send_buf[at : at + HALF] = turned[q : q + HALF] + second_half

    second = []
    for d in range(1, GY):
        to = lax.rem(gy + d, GY)
        copy = pltpu.make_async_remote_copy(
            src_ref=send_buf.at[pl.ds(pl.multiple_of(to * HALF, HALF), HALF)],
            dst_ref=recv_buf.at[GY - d],
            send_sem=send2.at[d],
            recv_sem=recv2.at[GY - d],
            device_id=(gx, to),
            device_id_type=MESH,
        )
        copy.start()
        second.append(copy)
    total = send_buf[pl.ds(pl.multiple_of(gy * HALF, HALF), HALF)]
    for copy in second:
        copy.wait()
    for d in range(1, GY):
        total = total + recv_buf[d]
    far[0:HALF] = total[:, 0:48]
    far[HALF:OWN] = pltpu.roll(total, 64, 1)[:, 0:48]


VMEM = pl.BlockSpec(memory_space=pltpu.VMEM)
SMEM = pl.BlockSpec(memory_space=pltpu.SMEM)
ANY = pl.BlockSpec(memory_space=pl.ANY)
HBM = pl.BlockSpec(memory_space=pltpu.HBM)


def local(efield, hfield, e_coef, omega, patch_owner, patch_corner, surface_points, surface_faces, angle_index):
    field = jax.ShapeDtypeStruct((3, ROWS, CZ), F32)
    fields = [
        pltpu.VMEM((3, ROWS + CB, CZ), F32),
        pltpu.VMEM((3, ROWS + CB, CZ), F32),
        pltpu.VMEM((ROWS, CZ), F32),
        pltpu.VMEM((2, CB, CZ), F32),
        pltpu.VMEM((2, CB, CZ), F32),
    ]
    coef = pltpu.with_memory_space_constraint(e_coef.reshape(ROWS, CZ), pltpu.HBM)
    omega = pltpu.with_memory_space_constraint(omega, pltpu.HBM)
    points = pltpu.with_memory_space_constraint(surface_points.reshape(1, SPB), pltpu.HBM)
    faces = pltpu.with_memory_space_constraint(surface_faces.reshape(1, SPB), pltpu.HBM)
    efield, hfield, halo, *tabled, spots = pl.pallas_call(
        first_kernel,
        out_shape=(
            field,
            field,
            jax.ShapeDtypeStruct((9, CB, CZ), F32),
            jax.ShapeDtypeStruct((2, 2 * XF, QF), BF16),
            jax.ShapeDtypeStruct((2, 2 * ZF, QF), BF16),
            jax.ShapeDtypeStruct((2, CB + 8, QF), F32),
            jax.ShapeDtypeStruct((8, SPB), jnp.int32),
        ),
        in_specs=[SMEM, VMEM, VMEM, VMEM, HBM, HBM, HBM],
        out_specs=(ANY, ANY, VMEM, ANY, ANY, ANY, VMEM),
        scratch_shapes=[
            pltpu.VMEM((8, QF), F32),
            pltpu.VMEM((2, 2 * XF, QF), BF16),
            pltpu.VMEM((2, 2 * ZF, QF), BF16),
            pltpu.VMEM((2, CB + 8, QF), F32),
        ]
        + fields
        + [
            pltpu.VMEM((2, 9, CB, CZ), F32),
            pltpu.VMEM((9, CB, CZ), F32),
            pltpu.SemaphoreType.DMA((6,)),
            pltpu.SemaphoreType.DMA((2, 6)),
            pltpu.SemaphoreType.DMA((2, 6)),
        ],
        compiler_params=pltpu.CompilerParams(collective_id=0, has_side_effects=True, vmem_limit_bytes=24 * 2**20),
        name="first_step",
    )(
        omega,
        pltpu.with_memory_space_constraint(angle_index.T, pltpu.HBM),
        points,
        faces,
        pltpu.with_memory_space_constraint(efield.reshape(3, ROWS, CZ), pltpu.HBM),
        pltpu.with_memory_space_constraint(hfield.reshape(3, ROWS, CZ), pltpu.HBM),
        coef,
    )
    efield, hfield, sampled = pl.pallas_call(
        second_kernel,
        out_shape=(field, field, jax.ShapeDtypeStruct((16, SPB), F32)),
        in_specs=[SMEM, SMEM, SMEM, VMEM, VMEM, VMEM, ANY, ANY, HBM],
        out_specs=(HBM, HBM, VMEM),
        scratch_shapes=fields
        + [
            pltpu.VMEM((4 * SPB, CZ), F32),
            pltpu.SMEM((SLOTS + 1,), jnp.int32),
            pltpu.SMEM((SLOTS + 1,), jnp.int32),
            pltpu.SMEM((1,), jnp.int32),
            pltpu.SemaphoreType.DMA((3,)),
        ],
        compiler_params=pltpu.CompilerParams(vmem_limit_bytes=24 * 2**20),
        name="patches",
    )(patch_owner, patch_corner.T, spots, points, faces, halo, efield, hfield, coef)
    far = pl.pallas_call(
        third_kernel,
        out_shape=jax.ShapeDtypeStruct((OWN, 48), F32),
        in_specs=[SMEM, VMEM, ANY, ANY, ANY],
        out_specs=VMEM,
        scratch_shapes=[
            pltpu.VMEM((16, GX * SPB), F32),
            pltpu.VMEM((GX, 16, SPB), F32),
            pltpu.VMEM((2, 2 * XF, QF), BF16),
            pltpu.VMEM((2, 4 * ZF, QF), BF16),
            pltpu.VMEM((2, CB + 8, QF), F32),
            pltpu.VMEM((2, ZF, QF), F32),
            pltpu.VMEM((2 * XF, GX * SPB), BF16),
            pltpu.VMEM((2 * ZF, 2 * SPB), BF16),
            pltpu.VMEM((YF_ROWS * 8, GX * SPB), BF16),
            pltpu.VMEM((YF_ROWS * 8, GX * SPB), BF16),
            pltpu.VMEM((2, YF_ROWS * 8 + CHUNK, 2 * XF), BF16),
            pltpu.VMEM((2, YF_ROWS * 8 + CHUNK, XF), BF16),
            pltpu.VMEM((2, CB * 16, 4 * ZF), BF16),
            pltpu.VMEM((3, 2, 16, QF), F32),
            pltpu.VMEM((128, QN), F32),
            pltpu.VMEM((QN // 2, 128), F32),
            pltpu.VMEM((GY, HALF, 128), F32),
            pltpu.SemaphoreType.DMA((4,)),
            pltpu.SemaphoreType.DMA((GX,)),
            pltpu.SemaphoreType.DMA((GX,)),
            pltpu.SemaphoreType.DMA((GY,)),
            pltpu.SemaphoreType.DMA((GY,)),
        ],
        compiler_params=pltpu.CompilerParams(collective_id=1, has_side_effects=True, vmem_limit_bytes=32 * 2**20),
        name="projection",
    )(omega, sampled, *tabled)
    shape = (3, CB, CB, CZ)
    return efield.reshape(shape), hfield.reshape(shape), far


def solution(mesh):
    placed = (
        P(None, "gx", "gy", None),
        P(None, "gx", "gy", None),
        P("gx", "gy", None),
        P(),
        P(),
        P(),
        P("gx", "gy", None),
        P("gx", "gy", None),
        P(),
    )
    return jax.shard_map(
        local,
        mesh=mesh,
        in_specs=placed,
        out_specs=(P(None, "gx", "gy", None), P(None, "gx", "gy", None), P(("gx", "gy"), None)),
        check_vma=False,
    )
```
